32 devices in a mesh: lon: 4 (over y, x), sec: 8 (over z, core).
Axes of the slice: x: 2, y: 2, z: 4, core: 2. Of those that a mesh axis runs over, the one named last changes fastest.
Arguments:
- moisture: float32 [16, 128, 1024], P(None, 'sec', 'lon'), may hold values from 0 to 2
- heat: float32 [16, 128, 1024], P(None, 'sec', 'lon'), may hold values from -6 to 6
- moist_cond: float32 [16, 128, 1024], P(None, 'sec', 'lon'), may hold values from 0.05 to 2
- heat_cond: float32 [16, 128, 1024], P(None, 'sec', 'lon'), may hold values from 0.1 to 3
- rain: float32 [128, 1024], P('sec', 'lon'), may hold values from 0.01 to 1
- surface_flux: float32 [128, 1024], P('sec', 'lon'), may hold values from -6 to 6
- cell_reach: int32 [128, 1024], P('sec', 'lon'), may hold values from 0 to 16383
- records: bfloat16 [4, 16384, 256], P('lon', 'sec'), may hold values from 0 to 2
- unit_hydro: bfloat16 [4, 16384, 256], P('lon', 'sec'), may hold values from 0.049804688 to 1
- down_basin: int32 [4, 16384], P('lon', 'sec'), may hold values from 0 to 4095
- basin_home: int32 [4, 4096], P('lon'), may hold values from 0 to 4095, as said below
- send_index: int32 [4, 8, 8, 512], P('lon', 'sec'), may hold values from 0 to 2047, as said below
- send_count: int32 [4, 8, 8], P('lon', 'sec'), may hold values from 0 to 512, as said below
Outputs:
- moist_out: float32 [16, 128, 1024], P(None, 'sec', 'lon')
- heat_out: float32 [16, 128, 1024], P(None, 'sec', 'lon')
- record_out: bfloat16 [4, 16384, 256], P('lon', 'sec')
- basin_inflow: float32 [4, 4096, 256], P('lon', 'sec')
The draws below stay inside these ranges and needn't reach their ends.
Inputs may be any that keep to these rules, and one draw needn't show every extreme that they name: `send_index`: within a longitude group, device s lists each of its 2048 reaches in exactly one used slot; a reach listed in block d drains into a basin whose basin_home lies in d * 512 to (d+1) * 512 - 1. Unused slots hold 0. `send_count`: in every group one owner receives 512 reaches from every device of sec; counts of owners 2 m and 2 m + 1 from one device add up to 512. `basin_home`: each group's row is a permutation.
All inputs are finite; a program needn't handle non-finite values.
Results may differ from the reference program's by a relative error of at most 0.009.
Values may be sent and summed in bfloat16 or wider, within the bound.
No kernel may reach another device: no remote copies, remote signals or barrier semaphores. Data moves between devices by JAX's collectives and lax.ppermute only.
A program may use at most 64 MiB of HBM per device.

```python
import math
import jax
import jax.numpy as jnp
from jax import lax

NL = 16
LON_DEV = 256
H = 256
R_DEV = 2048
B_DEV = 512
CAP = 512
REACHES = 16384
BASINS = 4096
NLAT = 128
NLON = 1024
N_LON = 4
N_SEC = 8


def build_group(key):
    k_home, k_star, k_pairs, k_order, k_basin = jax.random.split(key, 5)
    inverse = jax.random.permutation(k_home, BASINS).astype(jnp.int32)
    homes = jnp.argsort(inverse, stable=True).astype(jnp.int32)
    star = jax.random.randint(k_star, (), 0, N_SEC, dtype=jnp.int32)
    pairs = jax.random.randint(k_pairs, (N_SEC, N_SEC // 2), 0, CAP + 1, dtype=jnp.int32)
    pair_ids = jnp.arange(N_SEC // 2, dtype=jnp.int32)
    forced = jnp.where(star % 2 == 0, CAP, 0).astype(jnp.int32)
    pairs = jnp.where(pair_ids[None, :] == star // 2, forced, pairs)
    counts = jnp.stack([pairs, CAP - pairs], axis=-1).reshape(N_SEC, N_SEC).astype(jnp.int32)
    ends = jnp.cumsum(counts, axis=1).astype(jnp.int32)
    starts = ends - counts
    order = jax.vmap(lambda k: jax.random.permutation(k, R_DEV).astype(jnp.int32))(jax.random.split(k_order, N_SEC))
    position = jnp.minimum(starts[:, :, None] + jnp.arange(CAP, dtype=jnp.int32)[None, None, :], R_DEV - 1)
    picked = jax.vmap(lambda line, place: line[place])(order, position)
    usable = jnp.arange(CAP, dtype=jnp.int32)[None, None, :] < counts[:, :, None]
    blocks = jnp.where(usable, picked, 0).astype(jnp.int32)
    owner = jnp.sum((ends[:, None, :] <= jnp.arange(R_DEV, dtype=jnp.int32)[None, :, None]).astype(jnp.int32), axis=-1)
    local_place = jax.random.randint(k_basin, (N_SEC, R_DEV), 0, B_DEV, dtype=jnp.int32)
    basin_at = inverse[owner * B_DEV + local_place]
    back = jnp.argsort(order, axis=1, stable=True)
    basins = jnp.take_along_axis(basin_at, back, axis=1).reshape(N_SEC * R_DEV).astype(jnp.int32)
    return (blocks, counts, basins, homes)


def build_all(key):
    base = jax.random.fold_in(key, 7)
    keys = jax.vmap(lambda g: jax.random.fold_in(base, g))(jnp.arange(N_LON))
    return jax.vmap(build_group)(keys)


def draw_send_index(key, part):
    return build_all(key)[0]


def draw_send_count(key, part):
    return build_all(key)[1]


def draw_down_basin(key, part):
    return build_all(key)[2]


def draw_basin_home(key, part):
    return build_all(key)[3]


def set_ends(entries, rng, low, high):
    shape = entries.shape
    index_at = [jax.random.randint(jax.random.fold_in(rng, axis), (), 0, shape[axis]) for axis in range(len(shape))]
    entries = entries.at[tuple(index_at)].set(low)
    longest = shape.index(max(shape))
    index_at[longest] = (index_at[longest] + 1) % shape[longest]
    return entries.at[tuple(index_at)].set(high)


def shard_levels(key, dims, pieces, least, top_value):
    gain = 1.0
    for axis_at, shards_of in pieces:
        heights = jax.random.uniform(jax.random.fold_in(jax.random.fold_in(key, 6), axis_at), (shards_of,), jnp.float32, least / len(pieces), top_value / len(pieces))
        gain = gain * jnp.repeat(jnp.exp(heights), dims[axis_at] // shards_of).reshape((-1,) + (1,) * (len(dims) - 1 - axis_at))
    return gain


def centred(stream_key, dims, width, bound, pieces=(), kind=jnp.bfloat16):
    gain = shard_levels(stream_key, dims, pieces, -0.22, 0.18) if pieces else 1.0
    array = jax.random.normal(stream_key, dims, jnp.float32) * width * gain
    return jnp.minimum(jnp.maximum(array, -bound), bound).astype(kind)


def setup_inputs(seed: int = 0) -> dict:
    splits = jax.random.split(jax.random.key(seed), 14)
    moisture = jnp.clip(2.0 * jax.random.uniform(splits[0], (NL, NLAT, NLON), jnp.float32) ** shard_levels(splits[0], (NL, NLAT, NLON), ((1, 8), (2, 4)), -0.2, 0.2), 0.0, 2.0)
    heat = centred(splits[1], (NL, NLAT, NLON), 1.0, 6.0, ((1, 8), (2, 4)), jnp.float32)
    moist_cond = jnp.clip(jnp.exp(math.log(2.0) - 3.6888794 * jax.random.uniform(splits[2], (NL, NLAT, NLON), jnp.float32) ** shard_levels(splits[2], (NL, NLAT, NLON), ((1, 8), (2, 4)), -0.2, 0.2)), 0.05, 2.0)
    heat_cond = jnp.clip(jnp.exp(math.log(3.0) - 3.4011974 * jax.random.uniform(splits[3], (NL, NLAT, NLON), jnp.float32) ** shard_levels(splits[3], (NL, NLAT, NLON), ((1, 8), (2, 4)), -0.2, 0.2)), 0.1, 3.0)
    rain = jnp.clip(jnp.exp(math.log(1.0) - 4.6051702 * jax.random.uniform(splits[4], (NLAT, NLON), jnp.float32) ** shard_levels(splits[4], (NLAT, NLON), ((0, 8), (1, 4)), -0.2, 0.2)), 0.01, 1.0)
    surface_flux = centred(splits[5], (NLAT, NLON), 1.0, 6.0, ((0, 8), (1, 4)), jnp.float32)
    cell_reach = set_ends(jax.random.randint(splits[6], (NLAT, NLON), 0, REACHES), jax.random.fold_in(splits[6], 1), 0, REACHES - 1).astype(jnp.int32)
    records = jnp.clip(2.0 * jax.random.uniform(splits[7], (N_LON, REACHES, H), jnp.float32) ** shard_levels(splits[7], (N_LON, REACHES, H), ((0, 4), (1, 8)), -0.2, 0.2), 0.0, 2.0).astype(jnp.bfloat16)
    unit_hydro = jnp.clip(jnp.exp(math.log(1.0) - 2.9996462 * jax.random.uniform(splits[8], (N_LON, REACHES, H), jnp.float32) ** shard_levels(splits[8], (N_LON, REACHES, H), ((0, 4), (1, 8)), -0.2, 0.2)), 0.049804688, 1.0).astype(jnp.bfloat16)
    down_basin = draw_down_basin(jax.random.fold_in(splits[13], 71), 0)
    basin_home = draw_basin_home(jax.random.fold_in(splits[13], 71), 0)
    send_index = draw_send_index(jax.random.fold_in(splits[13], 71), 0)
    send_count = draw_send_count(jax.random.fold_in(splits[13], 71), 0)
    return dict(moisture=moisture, heat=heat, moist_cond=moist_cond, heat_cond=heat_cond, rain=rain, surface_flux=surface_flux, cell_reach=cell_reach, records=records, unit_hydro=unit_hydro, down_basin=down_basin, basin_home=basin_home, send_index=send_index, send_count=send_count)


LATERAL = 0.2


def lateral(field):
    padded = jnp.pad(field, ((0, 0), (1, 1), (1, 1)))
    beside_all = padded[:, 2:, 1:-1] + padded[:, :-2, 1:-1] + padded[:, 1:-1, 2:] + padded[:, 1:-1, :-2]
    return field + LATERAL * (beside_all - 4.0 * field)


def column_solve(conduct, source):
    layer_count = conduct.shape[0]
    flat_zero = jnp.zeros_like(conduct[0])
    links = [0.5 * (conduct[layer] + conduct[layer + 1]) for layer in range(layer_count - 1)]
    above_link = links + [flat_zero]
    below_link = [flat_zero] + links
    prev_ratio = flat_zero
    prev_value = flat_zero
    ratio_list = []
    value_list = []
    for layer in range(layer_count):
        pivot_value = 1.0 + below_link[layer] + above_link[layer] + below_link[layer] * prev_ratio
        prev_ratio = -above_link[layer] / pivot_value
        prev_value = (source[layer] + below_link[layer] * prev_value) / pivot_value
        ratio_list.append(prev_ratio)
        value_list.append(prev_value)
    result = [None] * layer_count
    result[layer_count - 1] = value_list[layer_count - 1]
    for layer in range(layer_count - 2, -1, -1):
        result[layer] = value_list[layer] - ratio_list[layer] * result[layer + 1]
    return jnp.stack(result)


def reference(moisture, heat, moist_cond, heat_cond, rain, surface_flux, cell_reach, records, unit_hydro, down_basin, basin_home, send_index, send_count):
    moist_rhs = lateral(moisture).at[0].add(rain)
    heat_rhs = lateral(heat).at[0].add(surface_flux)
    moist_out = column_solve(moist_cond, moist_rhs)
    heat_out = column_solve(heat_cond, heat_rhs)
    runoff = jax.nn.softplus(moist_out[0] - 1.0) * jax.nn.sigmoid(heat_out[0]) + 0.5 * moist_cond[NL - 1] * moist_out[NL - 1]
    group_runoff = runoff.reshape(NLAT, N_LON, LON_DEV).transpose(1, 0, 2).reshape(N_LON, NLAT * LON_DEV)
    group_cells = cell_reach.reshape(NLAT, N_LON, LON_DEV).transpose(1, 0, 2).reshape(N_LON, NLAT * LON_DEV)
    reach_runoff = jax.vmap(lambda vals, where: jax.ops.segment_sum(vals, where, num_segments=REACHES))(group_runoff, group_cells)
    shifted = jnp.concatenate([records[:, :, 1:].astype(jnp.float32), jnp.zeros((N_LON, REACHES, 1), jnp.float32)], axis=2)
    record_out = (shifted + reach_runoff[:, :, None] * unit_hydro.astype(jnp.float32)).astype(jnp.bfloat16)

    def one_group(inputs):
        blocks, counts, basins, homes, group_records = inputs
        offsets = (jnp.arange(N_SEC, dtype=jnp.int32) * R_DEV)[:, None, None]
        reach_rows = (blocks + offsets).astype(jnp.int32)
        usable = jnp.arange(CAP, dtype=jnp.int32)[None, None, :] < counts[:, :, None]
        home_slot = homes[basins[reach_rows]]
        target = jnp.where(usable, home_slot, BASINS).astype(jnp.int32)
        values = group_records[reach_rows].astype(jnp.float32).reshape(N_SEC * N_SEC * CAP, H)
        summed = jax.ops.segment_sum(values, target.reshape(-1), num_segments=BASINS + 1)
        return summed[:BASINS]

    basin_inflow = lax.map(one_group, (send_index, send_count, down_basin, basin_home, record_out))
    return moist_out, heat_out, record_out, basin_inflow
```

```python
import functools

import jax
import jax.numpy as jnp
from jax import lax
from jax.experimental import pallas as pl
from jax.experimental.pallas import tpu as pltpu
from jax.sharding import PartitionSpec as P

LATERAL = 0.2
LANES = 128
F32 = jnp.float32
BF16 = jnp.bfloat16


def params(mib=48):
    return pltpu.CompilerParams(vmem_limit_bytes=mib * 1024 * 1024)


def call(body, outs, *args, smem=(), flops=0, moved=0):
    specs = [
        pl.BlockSpec(memory_space=pltpu.SMEM if i in smem else pltpu.VMEM)
        for i in range(len(args))
    ]
    single = not isinstance(outs, (list, tuple))
    out_list = [outs] if single else list(outs)
    result = pl.pallas_call(
        body,
        out_shape=out_list,
        in_specs=specs,
        out_specs=[pl.BlockSpec(memory_space=pltpu.VMEM) for _ in out_list],
        compiler_params=params(),
        cost_estimate=pl.CostEstimate(flops=flops, bytes_accessed=moved, transcendentals=0),
    )(*args)
    return result[0] if single else result


def edges_body(moist, heat, north, south, west, east):
    layers, rows, cols = moist.shape
    lane = lax.broadcasted_iota(jnp.int32, (rows, LANES), 1)
    west_all = jnp.zeros((rows, LANES), F32)
    east_all = jnp.zeros((rows, LANES), F32)
    for f, ref in enumerate((moist, heat)):
        north[f * layers : (f + 1) * layers, :] = ref[:, 0, :].astype(BF16)
        south[f * layers : (f + 1) * layers, :] = ref[:, rows - 1, :].astype(BF16)
        for layer in range(layers):
            k = f * layers + layer
            west_all = jnp.where(lane == k, ref[layer, :, 0:1], west_all)
            east_all = jnp.where(lane == k, ref[layer, :, cols - 1 : cols], east_all)
    west[...] = west_all.astype(BF16)
    east[...] = east_all.astype(BF16)


def lookup(table, hi, lo):
    out = jnp.zeros(hi.shape, table.dtype)
    for row in range(table.shape[0]):
        line = jnp.broadcast_to(table[row : row + 1, :], hi.shape)
        got = jnp.take_along_axis(line, lo, axis=1)
        out = jnp.where(hi == row, got, out)
    return out


def index_body(listed, count, home, down, order, place):
    pairs, width = order.shape
    pos = lax.broadcasted_iota(jnp.int32, (1, width), 1)
    for m in range(pairs):
        c = count[2 * m]
        first = listed[m : m + 1, :width]
        second = pltpu.roll(listed[m : m + 1, width:], lax.rem(c, width), 1)
        order[m : m + 1, :] = jnp.where(pos < c, first, second)
    slot = lookup(home[...], down[...] >> 7, down[...] & (LANES - 1))
    for t in range(width // LANES):
        at = order[:, t * LANES : (t + 1) * LANES]
        place[:, t * LANES : (t + 1) * LANES] = lookup(slot, at >> 7, at & (LANES - 1))


def shift_time(x):
    steps = x.shape[1]
    lane = lax.broadcasted_iota(jnp.int32, x.shape, 1)
    return jnp.where(lane == steps - 1, 0.0, pltpu.roll(x, steps - 1, 1))


def pack_body(order, records, hydro, rec_packed, hyd_packed):
    tiles = order.shape[0]
    reaches = records.shape[0]
    turned = order[...].astype(F32).T
    group = 4
    for g in range(tiles // group):
        lane = lax.broadcasted_iota(jnp.int32, (LANES, reaches), 1).astype(F32)
        hot = jnp.concatenate(
            [
                jnp.where(lane == turned[:, g * group + i : g * group + i + 1], 1.0, 0.0).astype(BF16)
                for i in range(group)
            ],
            axis=0,
        )
        at = pl.ds(g * group * LANES, group * LANES)
        rec = jnp.dot(hot, records[...], preferred_element_type=F32)
        rec_packed[at, :] = shift_time(rec).astype(BF16)
        hyd_packed[at, :] = jnp.dot(hot, hydro[...], preferred_element_type=F32).astype(BF16)


def land_body(
    moist, heat, moist_k, heat_k, rain, flux, cell, north, south, west, east, ids,
    moist_out, heat_out, terms,
):
    layers, rows, cols = moist.shape
    row = lax.broadcasted_iota(jnp.int32, (rows, cols), 0)
    col = lax.broadcasted_iota(jnp.int32, (rows, cols), 1)
    north_all = north[...].astype(F32)
    south_all = south[...].astype(F32)
    west_all = west[...].astype(F32)
    east_all = east[...].astype(F32)
    for f, (x_ref, k_ref, top, out) in enumerate(
        ((moist, moist_k, rain, moist_out), (heat, heat_k, flux, heat_out))
    ):
        ratio = jnp.zeros((rows, cols), F32)
        value = jnp.zeros((rows, cols), F32)
        below = jnp.zeros((rows, cols), F32)
        ratios, values = [], []
        for layer in range(layers):
            k = f * layers + layer
            x = x_ref[layer]
            up = jnp.where(row == 0, north_all[k : k + 1, :], pltpu.roll(x, 1, 0))
            dn = jnp.where(row == rows - 1, south_all[k : k + 1, :], pltpu.roll(x, rows - 1, 0))
            lf = jnp.where(col == 0, west_all[:, k : k + 1], pltpu.roll(x, 1, 1))
            rt = jnp.where(col == cols - 1, east_all[:, k : k + 1], pltpu.roll(x, cols - 1, 1))
            rhs = x + LATERAL * (up + dn + lf + rt - 4.0 * x)
            if layer == 0:
                rhs = rhs + top[...]
            if layer < layers - 1:
                above = 0.5 * (k_ref[layer] + k_ref[layer + 1])
            else:
                above = jnp.zeros((rows, cols), F32)
            inv = 1.0 / (1.0 + below + above + below * ratio)
            ratio = -above * inv
            value = (rhs + below * value) * inv
            ratios.append(ratio)
            values.append(value)
            below = above
        x = values[-1]
        out[layers - 1] = x
        for layer in range(layers - 2, -1, -1):
            x = values[layer] - ratios[layer] * x
            out[layer] = x
    s = moist_out[0] - 1.0
    soft = jnp.maximum(s, 0.0) + jnp.log1p(jnp.exp(-jnp.abs(s)))
    gate = 1.0 / (1.0 + jnp.exp(-heat_out[0]))
    runoff = soft * gate + 0.5 * moist_k[layers - 1] * moist_out[layers - 1]
    cells = cell[...]
    hi = cells >> 7
    lo = cells & (LANES - 1)
    sections, blocks = terms.shape[0], terms.shape[1] - ids.shape[1]
    his = sections * blocks
    hi_iota = lax.broadcasted_iota(jnp.int32, (his, cols), 0)
    lo_iota = lax.broadcasted_iota(jnp.int32, (LANES, cols), 0)
    acc = jnp.zeros((his, LANES), F32)
    for i in range(rows):
        a = jnp.where(hi_iota == hi[i : i + 1, :], runoff[i : i + 1, :], 0.0).astype(BF16)
        b = jnp.where(lo_iota == lo[i : i + 1, :], 1.0, 0.0).astype(BF16)
        acc = acc + lax.dot_general(a, b, (((1,), (1,)), ((), ())), preferred_element_type=F32)
    terms[:, :blocks, :] = acc.reshape(sections, blocks, LANES).astype(BF16)
    terms[:, blocks:, :] = ids[...]


def send_body(got, order, rec_packed, hyd_packed, ready, runoff):
    blocks = runoff.shape[0]
    total = jnp.sum(got[:, :blocks, :].astype(F32), axis=0)
    runoff[...] = total
    at = order[...]
    turned = lookup(total, at >> 7, at & (LANES - 1)).T
    for t in range(blocks):
        rows = pl.ds(t * LANES, LANES)
        ready[rows, :] = (
            rec_packed[rows, :].astype(F32) + turned[:, t : t + 1] * hyd_packed[rows, :].astype(F32)
        ).astype(BF16)


def record_body(runoff, records, hydro, out):
    turned = runoff[...].T
    for t in range(runoff.shape[0]):
        rows = pl.ds(t * LANES, LANES)
        out[rows, :] = (
            shift_time(records[rows, :].astype(F32)) + turned[:, t : t + 1] * hydro[rows, :].astype(F32)
        ).astype(BF16)


def basin_body(place, rows, out):
    basins = out.shape[0]
    slot = lax.broadcasted_iota(jnp.int32, (basins, LANES), 0).astype(F32)
    hot = jnp.concatenate(
        [
            jnp.where(slot == place[t : t + 1, :], 1.0, 0.0).astype(BF16)
            for t in range(place.shape[0])
        ],
        axis=1,
    )
    out[...] = jnp.dot(hot, rows[...], preferred_element_type=F32).astype(out.dtype)


def per_device(
    moisture, heat, moist_cond, heat_cond, rain, surface_flux, cell_reach,
    records, unit_hydro, down_basin, basin_home, send_index, send_count,
):
    lons = lax.axis_size("lon")
    sections = lax.axis_size("sec")
    layers, lats, cols = moisture.shape
    reaches, steps = records.shape[1:]
    cap = send_index.shape[3]
    half = cap // 2
    pairs = sections // 2
    basins = basin_home.shape[1] // sections
    blocks = reaches // LANES
    shape = jax.ShapeDtypeStruct

    north, south, west, east = call(
        edges_body,
        [
            shape((2 * layers, cols), BF16),
            shape((2 * layers, cols), BF16),
            shape((lats, LANES), BF16),
            shape((lats, LANES), BF16),
        ],
        moisture,
        heat,
        moved=moisture.size * 8,
    )
    up_lon = [(i, i + 1) for i in range(lons - 1)]
    dn_lon = [(i + 1, i) for i in range(lons - 1)]
    up_sec = [(i, i + 1) for i in range(sections - 1)]
    dn_sec = [(i + 1, i) for i in range(sections - 1)]
    from_north = lax.ppermute(south, "sec", up_sec)
    from_south = lax.ppermute(north, "sec", dn_sec)
    from_west = lax.ppermute(east, "lon", up_lon)
    from_east = lax.ppermute(west, "lon", dn_lon)

    order, home_slot = call(
        index_body,
        [shape((pairs, cap), jnp.int32), shape((pairs, cap), jnp.int32)],
        send_index.reshape(pairs, 2 * cap),
        send_count.reshape(sections),
        basin_home.reshape(-1, LANES),
        down_basin.reshape(-1, LANES),
        smem=(1,),
        moved=sections * cap * 16,
    )
    order = order.reshape(-1, LANES)
    chip_place = home_slot - (2 * basins) * jnp.arange(pairs, dtype=jnp.int32)[:, None]
    digits = jnp.stack(
        [(chip_place >> 8).reshape(sections, half), (chip_place & 255).reshape(sections, half)], axis=1
    ).astype(BF16)
    id_rows = -(-(2 * half) // (16 * LANES)) * 16
    ids = jnp.pad(
        digits.reshape(sections, 2 * half), ((0, 0), (0, id_rows * LANES - 2 * half))
    ).reshape(sections, id_rows, LANES)

    rec_packed, hyd_packed = call(
        pack_body,
        [shape((reaches, steps), BF16), shape((reaches, steps), BF16)],
        order,
        records[0],
        unit_hydro[0],
        flops=4 * reaches * reaches * steps,
        moved=reaches * steps * 8,
    )

    moist_out, heat_out, terms = call(
        land_body,
        [
            shape(moisture.shape, F32),
            shape(heat.shape, F32),
            shape((sections, blocks + id_rows, LANES), BF16),
        ],
        moisture, heat, moist_cond, heat_cond, rain, surface_flux, cell_reach,
        from_north, from_south, from_west, from_east, ids,
        moved=moisture.size * 24,
    )

    got = lax.all_to_all(terms, "sec", split_axis=0, concat_axis=0, tiled=True)
    ready, runoff = call(
        send_body,
        [shape((reaches, steps), BF16), shape((blocks, LANES), F32)],
        got,
        order,
        rec_packed,
        hyd_packed,
        moved=reaches * steps * 6,
    )
    arrived = lax.all_to_all(
        ready.reshape(sections, half, steps), "sec", split_axis=0, concat_axis=0, tiled=True
    ).reshape(reaches, steps)

    record_new = call(
        record_body,
        shape((reaches, steps), BF16),
        runoff,
        records[0],
        unit_hydro[0],
        moved=reaches * steps * 6,
    )
    id_digits = (
        got[:, blocks:, :].astype(F32).reshape(sections, id_rows * LANES)[:, : 2 * half].reshape(sections, 2, half)
    )
    spot = (id_digits[:, 0] * 256.0 + id_digits[:, 1]).reshape(-1, LANES)
    core = (lax.axis_index("sec") % 2).astype(F32)
    theirs = call(
        basin_body,
        shape((basins, steps), BF16),
        spot - (1.0 - core) * basins,
        arrived,
        flops=2 * basins * reaches * steps,
        moved=reaches * steps * 2,
    )
    passed = lax.ppermute(theirs, "sec", [(i, i ^ 1) for i in range(sections)])
    mine = call(
        basin_body,
        shape((basins, steps), F32),
        spot - core * basins,
        arrived,
        flops=2 * basins * reaches * steps,
        moved=reaches * steps * 2,
    )
    inflow = mine + passed.astype(F32)
    return (moist_out, heat_out, record_new[None], inflow[None])


def solution(mesh):
    placed = (
        P(None, "sec", "lon"),
        P(None, "sec", "lon"),
        P(None, "sec", "lon"),
        P(None, "sec", "lon"),
        P("sec", "lon"),
        P("sec", "lon"),
        P("sec", "lon"),
        P("lon", "sec", None),
        P("lon", "sec", None),
        P("lon", "sec"),
        P("lon", None),
        P("lon", "sec", None, None),
        P("lon", "sec", None),
    )
    return jax.shard_map(
        per_device,
        mesh=mesh,
        in_specs=placed,
        out_specs=(
            P(None, "sec", "lon"),
            P(None, "sec", "lon"),
            P("lon", "sec", None),
            P("lon", "sec", None),
        ),
        check_vma=False,
    )
```

```python
import jax
import jax.numpy as jnp
from jax import lax
from jax.experimental import pallas as pl
from jax.experimental.pallas import tpu as pltpu
from jax.sharding import PartitionSpec as P

LATERAL = 0.2
LANES = 128
PACK_ROWS = 16
F32 = jnp.float32
BF16 = jnp.bfloat16
I32 = jnp.int32
VMEM = pl.BlockSpec(memory_space=pltpu.VMEM)
HBM = pl.BlockSpec(memory_space=pltpu.HBM)


def call(body, outs, *args, ins=None, out_specs=None, scratch=(), mib=8, flops=0, moved=0):
    ins = list(ins) if ins else [VMEM] * len(args)
    args = [
        pltpu.with_memory_space_constraint(arg, pltpu.HBM) if spec is HBM else arg
        for arg, spec in zip(args, ins)
    ]
    return pl.pallas_call(
        body,
        out_shape=list(outs),
        in_specs=ins,
        out_specs=list(out_specs) if out_specs else [VMEM] * len(outs),
        scratch_shapes=list(scratch),
        compiler_params=pltpu.CompilerParams(vmem_limit_bytes=mib * 1024 * 1024),
        cost_estimate=pl.CostEstimate(flops=flops, bytes_accessed=moved, transcendentals=0),
    )(*args)


def fetch(sources, targets, sems):
    copies = [
        pltpu.make_async_copy(src, dst, sems.at[i])
        for i, (src, dst) in enumerate(zip(sources, targets))
    ]
    for copy in copies:
        copy.start()
    return copies


def parity(axis):
    return lax.rem(lax.axis_index(axis), 2)


def edges_body(
    moist_in, heat_in, home_in, down_in, listed_in,
    moist, heat, home, down, listed, sec_near, sec_far, lon_near, lon_far, sems,
):
    copies = fetch(
        (moist_in, heat_in, home_in, down_in, listed_in), (moist, heat, home, down, listed), sems
    )
    layers, rows, cols = moist.shape
    lane = lax.broadcasted_iota(I32, (rows, LANES), 1)
    west = jnp.zeros((rows, LANES), F32)
    east = jnp.zeros((rows, LANES), F32)
    sec_even = parity("sec") == 0
    for f, ref in enumerate((moist, heat)):
        copies[f].wait()
        north = ref[:, 0, :]
        south = ref[:, rows - 1, :]
        sec_near[f * layers : (f + 1) * layers, :] = jnp.where(sec_even, south, north).astype(BF16)
        sec_far[f * layers : (f + 1) * layers, :] = jnp.where(sec_even, north, south).astype(BF16)
        for layer in range(layers):
            k = f * layers + layer
            west = jnp.where(lane == k, ref[layer, :, 0:1], west)
            east = jnp.where(lane == k, ref[layer, :, cols - 1 : cols], east)
    lon_even = parity("lon") == 0
    lon_near[...] = jnp.where(lon_even, east, west).astype(BF16)
    lon_far[...] = jnp.where(lon_even, west, east).astype(BF16)
    for copy in copies[2:]:
        copy.wait()


def lookup(table, hi, lo):
    out = jnp.zeros(hi.shape, table.dtype)
    for row in range(table.shape[0]):
        line = jnp.broadcast_to(table[row : row + 1, :], hi.shape)
        got = jnp.take_along_axis(line, lo, axis=1)
        out = jnp.where(hi == row, got, out)
    return out


def index_body(
    listed, home, down, count_in, moist_k_in, heat_k_in, rain_in, flux_in, cell_in,
    order, ids, moist_k, heat_k, rain, flux, cell, count, sems,
):
    copies = fetch(
        (count_in, moist_k_in, heat_k_in, rain_in, flux_in, cell_in),
        (count, moist_k, heat_k, rain, flux, cell),
        sems,
    )
    slot = lookup(home[...], down[...] >> 7, down[...] & (LANES - 1))
    copies[0].wait()
    pairs, width = listed.shape[0] // 2, listed.shape[1]
    tiles = width // LANES
    chip = lax.axis_index("sec") // 2
    chip_basins = home.shape[0] * LANES // pairs
    pos = lax.broadcasted_iota(I32, (1, width), 1)
    for m in range(pairs):
        c = count[0, 0, 2 * m]
        second = pltpu.roll(listed[2 * m + 1 : 2 * m + 2, :], lax.rem(c, width), 1)
        line = jnp.where(pos < c, listed[2 * m : 2 * m + 1, :], second)
        away = m ^ chip
        for t in range(tiles):
            order[pl.ds(away * tiles + t, 1), :] = line[:, t * LANES : (t + 1) * LANES]
    at = order[...]
    place = lookup(slot, at >> 7, at & (LANES - 1))
    pad = jnp.zeros((PACK_ROWS - 2 * tiles, LANES), F32)
    for away in range(pairs):
        m = away ^ chip
        mine = place[away * tiles : (away + 1) * tiles, :] - m * chip_basins
        ids[m] = jnp.concatenate(
            [(mine >> 8).astype(F32), (mine & 255).astype(F32), pad], axis=0
        ).astype(BF16)
    for copy in copies[1:]:
        copy.wait()


def shift_time(x):
    steps = x.shape[1]
    lane = lax.broadcasted_iota(I32, x.shape, 1)
    return jnp.where(lane == steps - 1, 0.0, pltpu.roll(x, steps - 1, 1))


def pack_body(order, records_in, hydro_in, rec_packed, hyd_packed, records, hydro, sems):
    copies = fetch((records_in, hydro_in), (records, hydro), sems)
    tiles = order.shape[0]
    reaches = records.shape[0]
    turned = order[...].astype(F32).T
    group = 4
    for g in range(tiles // group):
        lane = lax.broadcasted_iota(I32, (LANES, reaches), 1).astype(F32)
        hot = jnp.concatenate(
            [
                jnp.where(lane == turned[:, g * group + i : g * group + i + 1], 1.0, 0.0).astype(BF16)
                for i in range(group)
            ],
            axis=0,
        )
        at = pl.ds(g * group * LANES, group * LANES)
        if g == 0:
            copies[0].wait()
        rec = jnp.dot(hot, records[...], preferred_element_type=F32)
        rec_packed[at, :] = shift_time(rec).astype(BF16)
        if g == 0:
            copies[1].wait()
        hyd_packed[at, :] = jnp.dot(hot, hydro[...], preferred_element_type=F32).astype(BF16)


def land_body(
    moist, heat, moist_k, heat_k, rain, flux, cell, sec_near, sec_far, lon_near, lon_far, ids,
    moist_out, heat_out, terms,
):
    layers, rows, cols = moist.shape
    row = lax.broadcasted_iota(I32, (rows, cols), 0)
    col = lax.broadcasted_iota(I32, (rows, cols), 1)
    sec_even = parity("sec") == 0
    lon_even = parity("lon") == 0
    south_all = jnp.where(sec_even, sec_near[...].astype(F32), sec_far[...].astype(F32))
    north_all = jnp.where(sec_even, sec_far[...].astype(F32), sec_near[...].astype(F32))
    east_all = jnp.where(lon_even, lon_near[...].astype(F32), lon_far[...].astype(F32))
    west_all = jnp.where(lon_even, lon_far[...].astype(F32), lon_near[...].astype(F32))
    for f, (x_ref, k_ref, top, out) in enumerate(
        ((moist, moist_k, rain, moist_out), (heat, heat_k, flux, heat_out))
    ):
        ratio = jnp.zeros((rows, cols), F32)
        value = jnp.zeros((rows, cols), F32)
        below = jnp.zeros((rows, cols), F32)
        ratios, values = [], []
        for layer in range(layers):
            k = f * layers + layer
            x = x_ref[layer]
            up = jnp.where(row == 0, north_all[k : k + 1, :], pltpu.roll(x, 1, 0))
            dn = jnp.where(row == rows - 1, south_all[k : k + 1, :], pltpu.roll(x, rows - 1, 0))
            lf = jnp.where(col == 0, west_all[:, k : k + 1], pltpu.roll(x, 1, 1))
            rt = jnp.where(col == cols - 1, east_all[:, k : k + 1], pltpu.roll(x, cols - 1, 1))
            rhs = x + LATERAL * (up + dn + lf + rt - 4.0 * x)
            if layer == 0:
                rhs = rhs + top[...]
            if layer < layers - 1:
                above = 0.5 * (k_ref[layer] + k_ref[layer + 1])
            else:
                above = jnp.zeros((rows, cols), F32)
            inv = 1.0 / (1.0 + below + above + below * ratio)
            ratio = -above * inv
            value = (rhs + below * value) * inv
            ratios.append(ratio)
            values.append(value)
            below = above
        x = values[-1]
        out[layers - 1] = x
        for layer in range(layers - 2, -1, -1):
            x = values[layer] - ratios[layer] * x
            out[layer] = x
    s = moist_out[0] - 1.0
    soft = jnp.maximum(s, 0.0) + jnp.log1p(jnp.exp(-jnp.abs(s)))
    gate = 1.0 / (1.0 + jnp.exp(-heat_out[0]))
    runoff = soft * gate + 0.5 * moist_k[layers - 1] * moist_out[layers - 1]
    cells = cell[...]
    hi = cells >> 7
    lo = cells & (LANES - 1)
    sections, blocks = terms.shape[0], terms.shape[1] - PACK_ROWS
    his = sections * blocks
    hi_iota = lax.broadcasted_iota(I32, (his, cols), 0)
    lo_iota = lax.broadcasted_iota(I32, (LANES, cols), 0)
    acc = jnp.zeros((his, LANES), F32)
    for i in range(rows):
        a = jnp.where(hi_iota == hi[i : i + 1, :], runoff[i : i + 1, :], 0.0).astype(BF16)
        b = jnp.where(lo_iota == lo[i : i + 1, :], 1.0, 0.0).astype(BF16)
        acc = acc + lax.dot_general(a, b, (((1,), (1,)), ((), ())), preferred_element_type=F32)
    terms[:, :blocks, :] = acc.reshape(sections, blocks, LANES).astype(BF16)
    for owner in range(sections):
        terms[owner, blocks:, :] = ids[owner // 2]


def send_body(got, order, rec_packed, hyd_packed, runoff, *ready):
    blocks = runoff.shape[0]
    tiles = blocks // len(ready)
    total = jnp.sum(got[:, :blocks, :].astype(F32), axis=0)
    runoff[...] = total
    at = order[...]
    turned = lookup(total, at >> 7, at & (LANES - 1)).T
    for t in range(blocks):
        rows = pl.ds(t * LANES, LANES)
        ready[t // tiles][pl.ds((t % tiles) * LANES, LANES), :] = (
            rec_packed[rows, :].astype(F32) + turned[:, t : t + 1] * hyd_packed[rows, :].astype(F32)
        ).astype(BF16)


def hot_of(got, aways, tiles, basins, other):
    chip = lax.axis_index("sec") // 2
    core = parity("sec")
    base = ((1 - core) if other else core) * basins
    slot = lax.broadcasted_iota(I32, (basins, LANES), 0) + base
    slot = slot.astype(F32)
    blocks = got.shape[1] - PACK_ROWS
    parts = []
    for away in aways:
        digits = got[2 * (away ^ chip) + core, blocks:, :].astype(F32)
        place = digits[:tiles] * 256.0 + digits[tiles : 2 * tiles]
        for t in range(tiles):
            parts.append(jnp.where(slot == place[t : t + 1, :], 1.0, 0.0).astype(BF16))
    return parts[0] if len(parts) == 1 else jnp.concatenate(parts, axis=1)


def summed(got, aways, blocks, basins, other):
    tiles = blocks[0].shape[0] // LANES
    total = None
    for away, block in zip(aways, blocks):
        hot = hot_of(got, [away], tiles, basins, other)
        part = jnp.dot(hot, block[...], preferred_element_type=F32)
        total = part if total is None else total + part
    return total


def record_body(runoff, records_in, hydro_in, got, own, out, theirs, mine, records, hydro, sems):
    copies = fetch((records_in, hydro_in), (records, hydro), sems)
    basins = mine.shape[0]
    theirs[...] = summed(got, [0], [own], basins, True)
    mine[...] = summed(got, [0], [own], basins, False)
    turned = runoff[...].T
    for copy in copies:
        copy.wait()
    for t in range(runoff.shape[0]):
        rows = pl.ds(t * LANES, LANES)
        out[rows, :] = (
            shift_time(records[rows, :].astype(F32)) + turned[:, t : t + 1] * hydro[rows, :].astype(F32)
        ).astype(BF16)


def early_body(aways, theirs_so_far, mine_so_far, got, *refs):
    blocks, (theirs, mine) = refs[: len(aways)], refs[len(aways) :]
    basins = mine.shape[0]
    theirs[...] = theirs_so_far[...] + summed(got, aways, blocks, basins, True)
    mine[...] = mine_so_far[...] + summed(got, aways, blocks, basins, False)


def late_body(aways, other, so_far, got, *refs):
    blocks, out = refs[: len(aways)], refs[len(aways)]
    out[...] = (so_far[...] + summed(got, aways, blocks, out.shape[0], other)).astype(out.dtype)


def final_body(mine, passed, out, held, sems):
    rows = mine.shape[0]
    parts = 2
    size = rows // parts
    copies = []
    for i in range(parts):
        at = pl.ds(i * size, size)
        held[at, :] = mine[at, :] + passed[at, :].astype(F32)
        copy = pltpu.make_async_copy(held.at[at, :], out.at[at, :], sems.at[i])
        copy.start()
        copies.append(copy)
    for copy in copies:
        copy.wait()


def per_device(
    moisture, heat, moist_cond, heat_cond, rain, surface_flux, cell_reach,
    records, unit_hydro, down_basin, basin_home, send_index, send_count,
):
    lons = lax.axis_size("lon")
    sections = lax.axis_size("sec")
    layers, lats, cols = moisture.shape
    reaches, steps = records.shape[1:]
    cap = send_index.shape[3]
    pairs = sections // 2
    basins = basin_home.shape[1] // sections
    blocks = reaches // LANES
    shape = jax.ShapeDtypeStruct
    dma = pltpu.SemaphoreType.DMA

    home = basin_home.reshape(-1, LANES)
    down = down_basin.reshape(-1, LANES)
    listed = send_index.reshape(sections, cap)
    moist_v, heat_v, home_v, down_v, listed_v, sec_near, sec_far, lon_near, lon_far = call(
        edges_body,
        [
            shape(moisture.shape, F32),
            shape(heat.shape, F32),
            shape(home.shape, I32),
            shape(down.shape, I32),
            shape(listed.shape, I32),
            shape((2 * layers, cols), BF16),
            shape((2 * layers, cols), BF16),
            shape((lats, LANES), BF16),
            shape((lats, LANES), BF16),
        ],
        moisture, heat, home, down, listed,
        ins=[HBM] * 5,
        scratch=[dma((5,))],
        moved=moisture.size * 8,
    )
    swap = lambda count: [(i, i ^ 1) for i in range(count)]
    between = lambda count: [(i, i + 1) for i in range(1, count - 1, 2)] + [
        (i + 1, i) for i in range(1, count - 1, 2)
    ]
    got_sec_far = lax.ppermute(sec_far, "sec", between(sections))
    got_sec_near = lax.ppermute(sec_near, "sec", swap(sections))
    got_lon_far = lax.ppermute(lon_far, "lon", between(lons))
    got_lon_near = lax.ppermute(lon_near, "lon", swap(lons))

    order, ids, moist_k, heat_k, rain_v, flux_v, cell_v = call(
        index_body,
        [
            shape((blocks, LANES), I32),
            shape((pairs, PACK_ROWS, LANES), BF16),
            shape(moist_cond.shape, F32),
            shape(heat_cond.shape, F32),
            shape(rain.shape, F32),
            shape(surface_flux.shape, F32),
            shape(cell_reach.shape, I32),
        ],
        listed_v, home_v, down_v, send_count,
        moist_cond, heat_cond, rain, surface_flux, cell_reach,
        ins=[VMEM] * 3 + [HBM] * 6,
        scratch=[pltpu.SMEM(send_count.shape, I32), dma((6,))],
        moved=moisture.size * 16,
    )

    rec_packed, hyd_packed = call(
        pack_body,
        [shape((reaches, steps), BF16), shape((reaches, steps), BF16)],
        order, records[0], unit_hydro[0],
        ins=[VMEM, HBM, HBM],
        scratch=[pltpu.VMEM((reaches, steps), BF16), pltpu.VMEM((reaches, steps), BF16), dma((2,))],
        mib=24,
        flops=4 * reaches * reaches * steps,
        moved=reaches * steps * 8,
    )

    moist_out, heat_out, terms = call(
        land_body,
        [
            shape(moisture.shape, F32),
            shape(heat.shape, F32),
            shape((sections, blocks + PACK_ROWS, LANES), BF16),
        ],
        moist_v, heat_v, moist_k, heat_k, rain_v, flux_v, cell_v,
        got_sec_near, got_sec_far, got_lon_near, got_lon_far, ids,
        moved=moisture.size * 24,
    )

    got = lax.all_to_all(terms, "sec", split_axis=0, concat_axis=0, tiled=True)
    runoff, own, *ready = call(
        send_body,
        [shape((blocks, LANES), F32)] + [shape((cap, steps), BF16)] * pairs,
        got, order, rec_packed, hyd_packed,
        moved=reaches * steps * 6,
    )
    arrived = {}
    for away in range(pairs - 1, 0, -1):
        arrived[away] = lax.ppermute(
            ready[away - 1], "sec", [(i, i ^ (2 * away)) for i in range(sections)]
        )

    record_new, theirs, mine = call(
        record_body,
        [shape((reaches, steps), BF16), shape((basins, steps), F32), shape((basins, steps), F32)],
        runoff, records[0], unit_hydro[0], got, own,
        ins=[VMEM, HBM, HBM, VMEM, VMEM],
        scratch=[pltpu.VMEM((reaches, steps), BF16), pltpu.VMEM((reaches, steps), BF16), dma((2,))],
        mib=16,
        moved=reaches * steps * 6,
    )
    middle = max(2, pairs // 2)
    early = list(range(1, middle))
    late = list(range(middle, pairs))
    theirs, mine = call(
        lambda *refs: early_body(early, *refs),
        [shape((basins, steps), F32), shape((basins, steps), F32)],
        theirs, mine, got, *[arrived[a] for a in early],
        mib=12,
        moved=basins * steps * 16,
    )
    (theirs,) = call(
        lambda *refs: late_body(late, True, *refs),
        [shape((basins, steps), BF16)],
        theirs, got, *[arrived[a] for a in late],
        moved=basins * steps * 8,
    )
    passed = lax.ppermute(theirs, "sec", swap(sections))
    (mine,) = call(
        lambda *refs: late_body(late, False, *refs),
        [shape((basins, steps), F32)],
        mine, got, *[arrived[a] for a in late],
        moved=basins * steps * 8,
    )
    (inflow,) = call(
        final_body,
        [shape((basins, steps), F32)],
        mine, passed,
        out_specs=[HBM],
        scratch=[pltpu.VMEM((basins, steps), F32), dma((2,))],
        moved=basins * steps * 10,
    )
    return (moist_out, heat_out, record_new[None], inflow[None])


def solution(mesh):
    placed = (
        P(None, "sec", "lon"),
        P(None, "sec", "lon"),
        P(None, "sec", "lon"),
        P(None, "sec", "lon"),
        P("sec", "lon"),
        P("sec", "lon"),
        P("sec", "lon"),
        P("lon", "sec", None),
        P("lon", "sec", None),
        P("lon", "sec"),
        P("lon", None),
        P("lon", "sec", None, None),
        P("lon", "sec", None),
    )
    return jax.shard_map(
        per_device,
        mesh=mesh,
        in_specs=placed,
        out_specs=(
            P(None, "sec", "lon"),
            P(None, "sec", "lon"),
            P("lon", "sec", None),
            P("lon", "sec", None),
        ),
        check_vma=False,
    )
```

```python
import jax
import jax.numpy as jnp
from jax import lax
from jax.experimental import pallas as pl
from jax.experimental.pallas import tpu as pltpu
from jax.sharding import PartitionSpec as P

LATERAL = 0.2
LANES = 128
PACK_ROWS = 16
F32 = jnp.float32
BF16 = jnp.bfloat16
I32 = jnp.int32
VMEM = pl.BlockSpec(memory_space=pltpu.VMEM)
HBM = pl.BlockSpec(memory_space=pltpu.HBM)


def call(body, outs, *args, ins=None, out_specs=None, scratch=(), mib=8, flops=0, moved=0):
    ins = list(ins) if ins else [VMEM] * len(args)
    args = [
        pltpu.with_memory_space_constraint(arg, pltpu.HBM) if spec is HBM else arg
        for arg, spec in zip(args, ins)
    ]
    return pl.pallas_call(
        body,
        out_shape=list(outs),
        in_specs=ins,
        out_specs=list(out_specs) if out_specs else [VMEM] * len(outs),
        scratch_shapes=list(scratch),
        compiler_params=pltpu.CompilerParams(vmem_limit_bytes=mib * 1024 * 1024),
        cost_estimate=pl.CostEstimate(flops=flops, bytes_accessed=moved, transcendentals=0),
    )(*args)


def fetch(sources, targets, sems):
    copies = [
        pltpu.make_async_copy(src, dst, sems.at[i])
        for i, (src, dst) in enumerate(zip(sources, targets))
    ]
    for copy in copies:
        copy.start()
    return copies


def parity(axis):
    return lax.rem(lax.axis_index(axis), 2)


def edges_body(
    moist_in, heat_in, home_in, down_in, listed_in,
    moist, heat, home, down, listed, sec_near, sec_far, lon_near, lon_far, sems,
):
    copies = fetch(
        (moist_in, heat_in, home_in, down_in, listed_in), (moist, heat, home, down, listed), sems
    )
    layers, rows, cols = moist.shape
    lane = lax.broadcasted_iota(I32, (rows, LANES), 1)
    west = jnp.zeros((rows, LANES), F32)
    east = jnp.zeros((rows, LANES), F32)
    sec_even = parity("sec") == 0
    for f, ref in enumerate((moist, heat)):
        copies[f].wait()
        north = ref[:, 0, :]
        south = ref[:, rows - 1, :]
        sec_near[f * layers : (f + 1) * layers, :] = jnp.where(sec_even, south, north).astype(BF16)
        sec_far[f * layers : (f + 1) * layers, :] = jnp.where(sec_even, north, south).astype(BF16)
        for layer in range(layers):
            k = f * layers + layer
            west = jnp.where(lane == k, ref[layer, :, 0:1], west)
            east = jnp.where(lane == k, ref[layer, :, cols - 1 : cols], east)
    lon_even = parity("lon") == 0
    lon_near[...] = jnp.where(lon_even, east, west).astype(BF16)
    lon_far[...] = jnp.where(lon_even, west, east).astype(BF16)
    for copy in copies[2:]:
        copy.wait()


def lookup(table, hi, lo):
    out = jnp.zeros(hi.shape, table.dtype)
    for row in range(table.shape[0]):
        line = jnp.broadcast_to(table[row : row + 1, :], hi.shape)
        got = jnp.take_along_axis(line, lo, axis=1)
        out = jnp.where(hi == row, got, out)
    return out


def index_body(
    listed, home, down, count_in, moist_k_in, heat_k_in, rain_in, flux_in, cell_in, records_in, hydro_in,
    order, ids, moist_k, heat_k, rain, flux, cell, records, hydro, count, sems,
):
    copies = fetch(
        (count_in, moist_k_in, heat_k_in, rain_in, flux_in, cell_in, records_in, hydro_in),
        (count, moist_k, heat_k, rain, flux, cell, records, hydro),
        sems,
    )
    slot = lookup(home[...], down[...] >> 7, down[...] & (LANES - 1))
    copies[0].wait()
    pairs, width = listed.shape[0] // 2, listed.shape[1]
    tiles = width // LANES
    chip = lax.axis_index("sec") // 2
    chip_basins = home.shape[0] * LANES // pairs
    pos = lax.broadcasted_iota(I32, (1, width), 1)
    for m in range(pairs):
        c = count[0, 0, 2 * m]
        second = pltpu.roll(listed[2 * m + 1 : 2 * m + 2, :], lax.rem(c, width), 1)
        line = jnp.where(pos < c, listed[2 * m : 2 * m + 1, :], second)
        away = lax.rem(m - chip + pairs, pairs)
        for t in range(tiles):
            order[pl.ds(away * tiles + t, 1), :] = line[:, t * LANES : (t + 1) * LANES]
    at = order[...]
    place = lookup(slot, at >> 7, at & (LANES - 1))
    pad = jnp.zeros((PACK_ROWS - 2 * tiles, LANES), F32)
    for away in range(pairs):
        m = lax.rem(away + chip, pairs)
        mine = place[away * tiles : (away + 1) * tiles, :] - m * chip_basins
        ids[m] = jnp.concatenate(
            [(mine >> 8).astype(F32), (mine & 255).astype(F32), pad], axis=0
        ).astype(BF16)
    for copy in copies[1:]:
        copy.wait()


def shift_time(x):
    steps = x.shape[1]
    lane = lax.broadcasted_iota(I32, x.shape, 1)
    return jnp.where(lane == steps - 1, 0.0, pltpu.roll(x, steps - 1, 1))


def picked(order, away, tiles, reaches):
    turned = order[...].astype(F32).T
    lane = lax.broadcasted_iota(I32, (LANES, reaches), 1).astype(F32)
    parts = [
        jnp.where(lane == turned[:, t : t + 1], 1.0, 0.0).astype(BF16)
        for t in range(away * tiles, (away + 1) * tiles)
    ]
    return parts[0] if len(parts) == 1 else jnp.concatenate(parts, axis=0)


def first_body(away, order, records, hydro, rec_packed, hyd_packed):
    hot = picked(order, away, rec_packed.shape[0] // LANES, records.shape[0])
    rec = jnp.dot(hot, records[...], preferred_element_type=F32)
    rec_packed[...] = shift_time(rec).astype(BF16)
    hyd_packed[...] = jnp.dot(hot, hydro[...], preferred_element_type=F32).astype(BF16)


def land_body(
    moist, heat, moist_k, heat_k, rain, flux, cell, sec_near, sec_far, lon_near, lon_far, ids,
    moist_out, heat_out, terms,
):
    layers, rows, cols = moist.shape
    row = lax.broadcasted_iota(I32, (rows, cols), 0)
    col = lax.broadcasted_iota(I32, (rows, cols), 1)
    sec_even = parity("sec") == 0
    lon_even = parity("lon") == 0
    south_all = jnp.where(sec_even, sec_near[...].astype(F32), sec_far[...].astype(F32))
    north_all = jnp.where(sec_even, sec_far[...].astype(F32), sec_near[...].astype(F32))
    east_all = jnp.where(lon_even, lon_near[...].astype(F32), lon_far[...].astype(F32))
    west_all = jnp.where(lon_even, lon_far[...].astype(F32), lon_near[...].astype(F32))
    for f, (x_ref, k_ref, top, out) in enumerate(
        ((moist, moist_k, rain, moist_out), (heat, heat_k, flux, heat_out))
    ):
        ratio = jnp.zeros((rows, cols), F32)
        value = jnp.zeros((rows, cols), F32)
        below = jnp.zeros((rows, cols), F32)
        ratios, values = [], []
        for layer in range(layers):
            k = f * layers + layer
            x = x_ref[layer]
            up = jnp.where(row == 0, north_all[k : k + 1, :], pltpu.roll(x, 1, 0))
            dn = jnp.where(row == rows - 1, south_all[k : k + 1, :], pltpu.roll(x, rows - 1, 0))
            lf = jnp.where(col == 0, west_all[:, k : k + 1], pltpu.roll(x, 1, 1))
            rt = jnp.where(col == cols - 1, east_all[:, k : k + 1], pltpu.roll(x, cols - 1, 1))
            rhs = x + LATERAL * (up + dn + lf + rt - 4.0 * x)
            if layer == 0:
                rhs = rhs + top[...]
            if layer < layers - 1:
                above = 0.5 * (k_ref[layer] + k_ref[layer + 1])
            else:
                above = jnp.zeros((rows, cols), F32)
            inv = 1.0 / (1.0 + below + above + below * ratio)
            ratio = -above * inv
            value = (rhs + below * value) * inv
            ratios.append(ratio)
            values.append(value)
            below = above
        x = values[-1]
        out[layers - 1] = x
        for layer in range(layers - 2, -1, -1):
            x = values[layer] - ratios[layer] * x
            out[layer] = x
    s = moist_out[0] - 1.0
    soft = jnp.maximum(s, 0.0) + jnp.log1p(jnp.exp(-jnp.abs(s)))
    gate = 1.0 / (1.0 + jnp.exp(-heat_out[0]))
    runoff = soft * gate + 0.5 * moist_k[layers - 1] * moist_out[layers - 1]
    cells = cell[...]
    hi = cells >> 7
    lo = cells & (LANES - 1)
    sections, blocks = terms.shape[0], terms.shape[1] - PACK_ROWS
    his = sections * blocks
    hi_iota = lax.broadcasted_iota(I32, (his, cols), 0)
    lo_iota = lax.broadcasted_iota(I32, (LANES, cols), 0)
    acc = jnp.zeros((his, LANES), F32)
    for i in range(rows):
        a = jnp.where(hi_iota == hi[i : i + 1, :], runoff[i : i + 1, :], 0.0).astype(BF16)
        b = jnp.where(lo_iota == lo[i : i + 1, :], 1.0, 0.0).astype(BF16)
        acc = acc + lax.dot_general(a, b, (((1,), (1,)), ((), ())), preferred_element_type=F32)
    terms[:, :blocks, :] = acc.reshape(sections, blocks, LANES).astype(BF16)
    for owner in range(sections):
        terms[owner, blocks:, :] = ids[owner // 2]


def send_body(away, got, order, rec_packed, hyd_packed, runoff, ready):
    blocks = runoff.shape[0]
    tiles = ready.shape[0] // LANES
    total = jnp.sum(got[:, :blocks, :].astype(F32), axis=0)
    runoff[...] = total
    at = order[...]
    turned = lookup(total, at >> 7, at & (LANES - 1)).T
    for t in range(tiles):
        rows = pl.ds(t * LANES, LANES)
        col = away * tiles + t
        ready[rows, :] = (
            rec_packed[rows, :].astype(F32) + turned[:, col : col + 1] * hyd_packed[rows, :].astype(F32)
        ).astype(BF16)


def record_body(away, runoff, records, hydro, order, out, kept, ready):
    turned = runoff[...].T
    for t in range(runoff.shape[0]):
        rows = pl.ds(t * LANES, LANES)
        fresh = (
            shift_time(records[rows, :].astype(F32)) + turned[:, t : t + 1] * hydro[rows, :].astype(F32)
        ).astype(BF16)
        out[rows, :] = fresh
        kept[rows, :] = fresh
    hot = picked(order, away, ready.shape[0] // LANES, kept.shape[0])
    ready[...] = jnp.dot(hot, kept[...], preferred_element_type=F32).astype(BF16)


def rest_body(aways, order, kept, landed, *ready):
    for away, out in zip(aways, ready):
        hot = picked(order, away, out.shape[0] // LANES, kept.shape[0])
        out[...] = jnp.dot(hot, kept[...], preferred_element_type=F32).astype(BF16)


def hot_of(got, aways, tiles, basins, other):
    chip = lax.axis_index("sec") // 2
    core = parity("sec")
    base = ((1 - core) if other else core) * basins
    slot = lax.broadcasted_iota(I32, (basins, LANES), 0) + base
    slot = slot.astype(F32)
    blocks = got.shape[1] - PACK_ROWS
    parts = []
    pairs = got.shape[0] // 2
    for away in aways:
        digits = got[2 * lax.rem(chip - away + pairs, pairs) + core, blocks:, :].astype(F32)
        place = digits[:tiles] * 256.0 + digits[tiles : 2 * tiles]
        for t in range(tiles):
            parts.append(jnp.where(slot == place[t : t + 1, :], 1.0, 0.0).astype(BF16))
    return parts[0] if len(parts) == 1 else jnp.concatenate(parts, axis=1)


def summed(got, aways, blocks, basins, other):
    tiles = blocks[0].shape[0] // LANES
    total = None
    for away, block in zip(aways, blocks):
        hot = hot_of(got, [away], tiles, basins, other)
        part = jnp.dot(hot, block[...], preferred_element_type=F32)
        total = part if total is None else total + part
    return total


def early_body(aways, got, *refs):
    blocks, (theirs, mine) = refs[: len(aways)], refs[len(aways) :]
    basins = mine.shape[0]
    theirs[...] = summed(got, aways, blocks, basins, True)
    mine[...] = summed(got, aways, blocks, basins, False)


def late_body(aways, other, so_far, got, *refs):
    blocks, out = refs[: len(aways)], refs[len(aways)]
    out[...] = (so_far[...] + summed(got, aways, blocks, out.shape[0], other)).astype(out.dtype)


def final_body(mine, passed, out, held, sems):
    rows = mine.shape[0]
    parts = 2
    size = rows // parts
    copies = []
    for i in range(parts):
        at = pl.ds(i * size, size)
        held[at, :] = mine[at, :] + passed[at, :].astype(F32)
        copy = pltpu.make_async_copy(held.at[at, :], out.at[at, :], sems.at[i])
        copy.start()
        copies.append(copy)
    for copy in copies:
        copy.wait()


def per_device(
    moisture, heat, moist_cond, heat_cond, rain, surface_flux, cell_reach,
    records, unit_hydro, down_basin, basin_home, send_index, send_count,
):
    lons = lax.axis_size("lon")
    sections = lax.axis_size("sec")
    layers, lats, cols = moisture.shape
    reaches, steps = records.shape[1:]
    cap = send_index.shape[3]
    pairs = sections // 2
    basins = basin_home.shape[1] // sections
    blocks = reaches // LANES
    shape = jax.ShapeDtypeStruct
    dma = pltpu.SemaphoreType.DMA

    home = basin_home.reshape(-1, LANES)
    down = down_basin.reshape(-1, LANES)
    listed = send_index.reshape(sections, cap)
    moist_v, heat_v, home_v, down_v, listed_v, sec_near, sec_far, lon_near, lon_far = call(
        edges_body,
        [
            shape(moisture.shape, F32),
            shape(heat.shape, F32),
            shape(home.shape, I32),
            shape(down.shape, I32),
            shape(listed.shape, I32),
            shape((2 * layers, cols), BF16),
            shape((2 * layers, cols), BF16),
            shape((lats, LANES), BF16),
            shape((lats, LANES), BF16),
        ],
        moisture, heat, home, down, listed,
        ins=[HBM] * 5,
        scratch=[dma((5,))],
        moved=moisture.size * 8,
    )
    swap = lambda count: [(i, i ^ 1) for i in range(count)]
    between = lambda count: [(i, i + 1) for i in range(1, count - 1, 2)] + [
        (i + 1, i) for i in range(1, count - 1, 2)
    ]
    got_sec_far = lax.ppermute(sec_far, "sec", between(sections))
    got_sec_near = lax.ppermute(sec_near, "sec", swap(sections))
    got_lon_far = lax.ppermute(lon_far, "lon", between(lons))
    got_lon_near = lax.ppermute(lon_near, "lon", swap(lons))

    order, ids, moist_k, heat_k, rain_v, flux_v, cell_v, records_v, hydro_v = call(
        index_body,
        [
            shape((blocks, LANES), I32),
            shape((pairs, PACK_ROWS, LANES), BF16),
            shape(moist_cond.shape, F32),
            shape(heat_cond.shape, F32),
            shape(rain.shape, F32),
            shape(surface_flux.shape, F32),
            shape(cell_reach.shape, I32),
            shape((reaches, steps), BF16),
            shape((reaches, steps), BF16),
        ],
        listed_v, home_v, down_v, send_count,
        moist_cond, heat_cond, rain, surface_flux, cell_reach, records[0], unit_hydro[0],
        ins=[VMEM] * 3 + [HBM] * 8,
        scratch=[pltpu.SMEM(send_count.shape, I32), dma((8,))],
        mib=12,
        moved=moisture.size * 16,
    )

    aways = []
    for k in range(1, pairs // 2 + 1):
        aways += [k] if 2 * k == pairs else [k, pairs - k]
    rec_packed, hyd_packed = call(
        lambda *refs: first_body(aways[0], *refs),
        [shape((cap, steps), BF16), shape((cap, steps), BF16)],
        order, records_v, hydro_v,
        mib=12,
        flops=4 * cap * reaches * steps,
        moved=reaches * steps * 4,
    )

    moist_out, heat_out, terms = call(
        land_body,
        [
            shape(moisture.shape, F32),
            shape(heat.shape, F32),
            shape((sections, blocks + PACK_ROWS, LANES), BF16),
        ],
        moist_v, heat_v, moist_k, heat_k, rain_v, flux_v, cell_v,
        got_sec_near, got_sec_far, got_lon_near, got_lon_far, ids,
        moved=moisture.size * 24,
    )

    got = lax.all_to_all(terms, "sec", split_axis=0, concat_axis=0, tiled=True)
    runoff, ready = call(
        lambda *refs: send_body(aways[0], *refs),
        [shape((blocks, LANES), F32), shape((cap, steps), BF16)],
        got, order, rec_packed, hyd_packed,
        moved=cap * steps * 6,
    )
    forward = lambda block, away: lax.ppermute(
        block, "sec", [(i, (i + 2 * away) % sections) for i in range(sections)]
    )
    arrived = {aways[0]: forward(ready, aways[0])}
    record_new, kept, ready = call(
        lambda *refs: record_body(aways[1], *refs),
        [shape((reaches, steps), BF16), shape((reaches, steps), BF16), shape((cap, steps), BF16)],
        runoff, records_v, hydro_v, order,
        mib=16,
        flops=2 * cap * reaches * steps,
        moved=reaches * steps * 8,
    )
    arrived[aways[1]] = forward(ready, aways[1])
    rest = aways[2:] + [0]
    *ready, own = call(
        lambda *refs: rest_body(rest, *refs),
        [shape((cap, steps), BF16)] * len(rest),
        order, kept, arrived[aways[0]],
        mib=16,
        flops=2 * cap * reaches * steps * len(rest),
        moved=reaches * steps * 4,
    )
    for away, block in zip(aways[2:], ready):
        arrived[away] = forward(block, away)
    late = aways[-1:]
    early = [0] + aways[:-1]
    arrived[0] = own
    theirs, mine = call(
        lambda *refs: early_body(early, *refs),
        [shape((basins, steps), F32), shape((basins, steps), F32)],
        got, *[arrived[a] for a in early],
        mib=12,
        moved=basins * steps * 16,
    )
    (theirs,) = call(
        lambda *refs: late_body(late, True, *refs),
        [shape((basins, steps), BF16)],
        theirs, got, *[arrived[a] for a in late],
        moved=basins * steps * 8,
    )
    passed = lax.ppermute(theirs, "sec", swap(sections))
    (mine,) = call(
        lambda *refs: late_body(late, False, *refs),
        [shape((basins, steps), F32)],
        mine, got, *[arrived[a] for a in late],
        moved=basins * steps * 8,
    )
    (inflow,) = call(
        final_body,
        [shape((basins, steps), F32)],
        mine, passed,
        out_specs=[HBM],
        scratch=[pltpu.VMEM((basins, steps), F32), dma((2,))],
        moved=basins * steps * 10,
    )
    return (moist_out, heat_out, record_new[None], inflow[None])


def solution(mesh):
    placed = (
        P(None, "sec", "lon"),
        P(None, "sec", "lon"),
        P(None, "sec", "lon"),
        P(None, "sec", "lon"),
        P("sec", "lon"),
        P("sec", "lon"),
        P("sec", "lon"),
        P("lon", "sec", None),
        P("lon", "sec", None),
        P("lon", "sec"),
        P("lon", None),
        P("lon", "sec", None, None),
        P("lon", "sec", None),
    )
    return jax.shard_map(
        per_device,
        mesh=mesh,
        in_specs=placed,
        out_specs=(
            P(None, "sec", "lon"),
            P(None, "sec", "lon"),
            P("lon", "sec", None),
            P("lon", "sec", None),
        ),
        check_vma=False,
    )
```

```python
import jax
import jax.numpy as jnp
from jax import lax
from jax.experimental import pallas as pl
from jax.experimental.pallas import tpu as pltpu
from jax.sharding import PartitionSpec as P

LATERAL = 0.2
LANES = 128
PACK_ROWS = 16
F32 = jnp.float32
BF16 = jnp.bfloat16
I32 = jnp.int32
VMEM = pl.BlockSpec(memory_space=pltpu.VMEM)
HBM = pl.BlockSpec(memory_space=pltpu.HBM)


def call(body, outs, *args, ins=None, out_specs=None, scratch=(), mib=8, flops=0, moved=0):
    ins = list(ins) if ins else [VMEM] * len(args)
    args = [
        pltpu.with_memory_space_constraint(arg, pltpu.HBM) if spec is HBM else arg
        for arg, spec in zip(args, ins)
    ]
    return pl.pallas_call(
        body,
        out_shape=list(outs),
        in_specs=ins,
        out_specs=list(out_specs) if out_specs else [VMEM] * len(outs),
        scratch_shapes=list(scratch),
        compiler_params=pltpu.CompilerParams(vmem_limit_bytes=mib * 1024 * 1024),
        cost_estimate=pl.CostEstimate(flops=flops, bytes_accessed=moved, transcendentals=0),
    )(*args)


def fetch(sources, targets, sems):
    copies = [
        pltpu.make_async_copy(src, dst, sems.at[i])
        for i, (src, dst) in enumerate(zip(sources, targets))
    ]
    for copy in copies:
        copy.start()
    return copies


def parity(axis):
    return lax.rem(lax.axis_index(axis), 2)


def edges_body(*refs):
    count = 10
    targets = refs[count : 2 * count]
    moist, heat = targets[:2]
    sec_near, sec_far, lon_near, lon_far, sems = refs[2 * count :]
    copies = fetch(refs[:count], targets, sems)
    layers, rows, cols = moist.shape
    lane = lax.broadcasted_iota(I32, (rows, LANES), 1)
    west = jnp.zeros((rows, LANES), F32)
    east = jnp.zeros((rows, LANES), F32)
    sec_even = parity("sec") == 0
    for f, ref in enumerate((moist, heat)):
        copies[f].wait()
        north = ref[:, 0, :]
        south = ref[:, rows - 1, :]
        sec_near[f * layers : (f + 1) * layers, :] = jnp.where(sec_even, south, north).astype(BF16)
        sec_far[f * layers : (f + 1) * layers, :] = jnp.where(sec_even, north, south).astype(BF16)
        for layer in range(layers):
            k = f * layers + layer
            west = jnp.where(lane == k, ref[layer, :, 0:1], west)
            east = jnp.where(lane == k, ref[layer, :, cols - 1 : cols], east)
    lon_even = parity("lon") == 0
    lon_near[...] = jnp.where(lon_even, east, west).astype(BF16)
    lon_far[...] = jnp.where(lon_even, west, east).astype(BF16)
    for copy in copies[2:]:
        copy.wait()


def lookup(table, hi, lo):
    out = jnp.zeros(hi.shape, table.dtype)
    for row in range(table.shape[0]):
        line = jnp.broadcast_to(table[row : row + 1, :], hi.shape)
        got = jnp.take_along_axis(line, lo, axis=1)
        out = jnp.where(hi == row, got, out)
    return out


def index_body(listed, home, down, count_in, order, ids, count, sems):
    copies = fetch((count_in,), (count,), sems)
    slot = lookup(home[...], down[...] >> 7, down[...] & (LANES - 1))
    pairs, width = listed.shape[0] // 2, listed.shape[1]
    tiles = width // LANES
    chip = lax.axis_index("sec") // 2
    chip_basins = home.shape[0] * LANES // pairs
    pos = lax.broadcasted_iota(I32, (1, width), 1)
    copies[0].wait()
    for m in range(pairs):
        c = count[0, 0, 2 * m]
        second = pltpu.roll(listed[2 * m + 1 : 2 * m + 2, :], lax.rem(c, width), 1)
        line = jnp.where(pos < c, listed[2 * m : 2 * m + 1, :], second)
        away = lax.rem(m - chip + pairs, pairs)
        for t in range(tiles):
            order[pl.ds(away * tiles + t, 1), :] = line[:, t * LANES : (t + 1) * LANES]
    at = order[...]
    place = lookup(slot, at >> 7, at & (LANES - 1))
    pad = jnp.zeros((PACK_ROWS - 2 * tiles, LANES), F32)
    for away in range(pairs):
        m = lax.rem(away + chip, pairs)
        mine = place[away * tiles : (away + 1) * tiles, :] - m * chip_basins
        ids[away] = jnp.concatenate(
            [(mine >> 8).astype(F32), (mine & 255).astype(F32), pad], axis=0
        ).astype(BF16)


def shift_time(x):
    steps = x.shape[1]
    lane = lax.broadcasted_iota(I32, x.shape, 1)
    return jnp.where(lane == steps - 1, 0.0, pltpu.roll(x, steps - 1, 1))


def picked(order, away, tiles, reaches):
    turned = order[...].astype(F32).T
    lane = lax.broadcasted_iota(I32, (LANES, reaches), 1).astype(F32)
    parts = [
        jnp.where(lane == turned[:, t : t + 1], 1.0, 0.0).astype(BF16)
        for t in range(away * tiles, (away + 1) * tiles)
    ]
    return parts[0] if len(parts) == 1 else jnp.concatenate(parts, axis=0)


def first_body(away, order, records_in, hydro_in, rec_packed, hyd_packed, records, hydro, sems):
    copies = fetch((records_in, hydro_in), (records, hydro), sems)
    hot = picked(order, away, rec_packed.shape[0] // LANES, records.shape[0])
    copies[0].wait()
    rec = jnp.dot(hot, records[...], preferred_element_type=F32)
    copies[1].wait()
    rec_packed[...] = shift_time(rec).astype(BF16)
    hyd_packed[...] = jnp.dot(hot, hydro[...], preferred_element_type=F32).astype(BF16)


def land_body(
    moist, heat, moist_k, heat_k, rain, flux, cell, sec_near, sec_far, lon_near, lon_far,
    moist_out, heat_out, keep, give,
):
    layers, rows, cols = moist.shape
    row = lax.broadcasted_iota(I32, (rows, cols), 0)
    col = lax.broadcasted_iota(I32, (rows, cols), 1)
    sec_even = parity("sec") == 0
    lon_even = parity("lon") == 0
    south_all = jnp.where(sec_even, sec_near[...].astype(F32), sec_far[...].astype(F32))
    north_all = jnp.where(sec_even, sec_far[...].astype(F32), sec_near[...].astype(F32))
    east_all = jnp.where(lon_even, lon_near[...].astype(F32), lon_far[...].astype(F32))
    west_all = jnp.where(lon_even, lon_far[...].astype(F32), lon_near[...].astype(F32))
    for f, (x_ref, k_ref, top, out) in enumerate(
        ((moist, moist_k, rain, moist_out), (heat, heat_k, flux, heat_out))
    ):
        ratio = jnp.zeros((rows, cols), F32)
        value = jnp.zeros((rows, cols), F32)
        below = jnp.zeros((rows, cols), F32)
        ratios, values = [], []
        for layer in range(layers):
            k = f * layers + layer
            x = x_ref[layer]
            up = jnp.where(row == 0, north_all[k : k + 1, :], pltpu.roll(x, 1, 0))
            dn = jnp.where(row == rows - 1, south_all[k : k + 1, :], pltpu.roll(x, rows - 1, 0))
            lf = jnp.where(col == 0, west_all[:, k : k + 1], pltpu.roll(x, 1, 1))
            rt = jnp.where(col == cols - 1, east_all[:, k : k + 1], pltpu.roll(x, cols - 1, 1))
            rhs = x + LATERAL * (up + dn + lf + rt - 4.0 * x)
            if layer == 0:
                rhs = rhs + top[...]
            if layer < layers - 1:
                above = 0.5 * (k_ref[layer] + k_ref[layer + 1])
            else:
                above = jnp.zeros((rows, cols), F32)
            inv = 1.0 / (1.0 + below + above + below * ratio)
            ratio = -above * inv
            value = (rhs + below * value) * inv
            ratios.append(ratio)
            values.append(value)
            below = above
        x = values[-1]
        out[layers - 1] = x
        for layer in range(layers - 2, -1, -1):
            x = values[layer] - ratios[layer] * x
            out[layer] = x
    s = moist_out[0] - 1.0
    soft = jnp.maximum(s, 0.0) + jnp.log1p(jnp.exp(-jnp.abs(s)))
    gate = 1.0 / (1.0 + jnp.exp(-heat_out[0]))
    runoff = soft * gate + 0.5 * moist_k[layers - 1] * moist_out[layers - 1]
    cells = cell[...]
    hi = cells >> 7
    lo = cells & (LANES - 1)
    pairs, blocks = keep.shape[:2]
    his = 2 * pairs * blocks
    hi_iota = lax.broadcasted_iota(I32, (his, cols), 0)
    lo_iota = lax.broadcasted_iota(I32, (LANES, cols), 0)
    acc = jnp.zeros((his, LANES), F32)
    for i in range(rows):
        a = jnp.where(hi_iota == hi[i : i + 1, :], runoff[i : i + 1, :], 0.0).astype(BF16)
        b = jnp.where(lo_iota == lo[i : i + 1, :], 1.0, 0.0).astype(BF16)
        acc = acc + lax.dot_general(a, b, (((1,), (1,)), ((), ())), preferred_element_type=F32)
    both = acc.reshape(pairs, 2, blocks, LANES)
    keep[...] = jnp.where(sec_even, both[:, 0], both[:, 1])
    give[...] = jnp.where(sec_even, both[:, 1], both[:, 0]).astype(BF16)


def terms_body(aways, keep, got, ids, own, *outs):
    pairs, blocks = keep.shape[:2]
    chip = lax.axis_index("sec") // 2
    own[...] = keep[chip] + got[chip].astype(F32)
    for away, out in zip(aways, outs):
        m = lax.rem(chip + away, pairs)
        out[:blocks, :] = (keep[m] + got[m].astype(F32)).astype(BF16)
        out[blocks:, :] = ids[away]


def send_body(away, own, order, rec_packed, hyd_packed, *refs):
    terms, (runoff, ready) = refs[:-2], refs[-2:]
    blocks = runoff.shape[0]
    tiles = ready.shape[0] // LANES
    total = own[...]
    for term in terms:
        total = total + term[:blocks, :].astype(F32)
    runoff[...] = total
    at = order[...]
    turned = lookup(total, at >> 7, at & (LANES - 1)).T
    for t in range(tiles):
        rows = pl.ds(t * LANES, LANES)
        col = away * tiles + t
        ready[rows, :] = (
            rec_packed[rows, :].astype(F32) + turned[:, col : col + 1] * hyd_packed[rows, :].astype(F32)
        ).astype(BF16)


def record_body(away, runoff, records, hydro, order, out, kept, ready):
    turned = runoff[...].T
    for t in range(runoff.shape[0]):
        rows = pl.ds(t * LANES, LANES)
        fresh = (
            shift_time(records[rows, :].astype(F32)) + turned[:, t : t + 1] * hydro[rows, :].astype(F32)
        ).astype(BF16)
        out[rows, :] = fresh
        kept[rows, :] = fresh
    hot = picked(order, away, ready.shape[0] // LANES, kept.shape[0])
    ready[...] = jnp.dot(hot, kept[...], preferred_element_type=F32).astype(BF16)


def rest_body(aways, order, kept, landed, *ready):
    for away, out in zip(aways, ready):
        hot = picked(order, away, out.shape[0] // LANES, kept.shape[0])
        out[...] = jnp.dot(hot, kept[...], preferred_element_type=F32).astype(BF16)


def hot_of(digits, tiles, basins, other):
    core = parity("sec")
    base = ((1 - core) if other else core) * basins
    slot = lax.broadcasted_iota(I32, (basins, LANES), 0) + base
    slot = slot.astype(F32)
    place = digits[:tiles] * 256.0 + digits[tiles : 2 * tiles]
    parts = [jnp.where(slot == place[t : t + 1, :], 1.0, 0.0).astype(BF16) for t in range(tiles)]
    return parts[0] if len(parts) == 1 else jnp.concatenate(parts, axis=1)


def summed(digits, blocks, basins, other):
    tiles = blocks[0].shape[0] // LANES
    total = None
    for digit, block in zip(digits, blocks):
        hot = hot_of(digit, tiles, basins, other)
        part = jnp.dot(hot, block[...], preferred_element_type=F32)
        total = part if total is None else total + part
    return total


def digits_of(terms):
    return [ref[ref.shape[0] - PACK_ROWS :, :].astype(F32) for ref in terms]


def early_body(ids, *refs):
    theirs, mine = refs[-2:]
    n = (len(refs) - 3) // 2
    terms, blocks = refs[:n], refs[n:-2]
    digits = [ids[0].astype(F32)] + digits_of(terms)
    basins = mine.shape[0]
    theirs[...] = summed(digits, blocks, basins, True)
    mine[...] = summed(digits, blocks, basins, False)


def late_body(other, so_far, *refs):
    out = refs[-1]
    terms, blocks = refs[: len(refs) // 2], refs[len(refs) // 2 : -1]
    out[...] = (so_far[...] + summed(digits_of(terms), blocks, out.shape[0], other)).astype(out.dtype)


def final_body(mine, passed, out, held, sems):
    rows = mine.shape[0]
    parts = 2
    size = rows // parts
    copies = []
    for i in range(parts):
        at = pl.ds(i * size, size)
        held[at, :] = mine[at, :] + passed[at, :].astype(F32)
        copy = pltpu.make_async_copy(held.at[at, :], out.at[at, :], sems.at[i])
        copy.start()
        copies.append(copy)
    for copy in copies:
        copy.wait()


def per_device(
    moisture, heat, moist_cond, heat_cond, rain, surface_flux, cell_reach,
    records, unit_hydro, down_basin, basin_home, send_index, send_count,
):
    lons = lax.axis_size("lon")
    sections = lax.axis_size("sec")
    layers, lats, cols = moisture.shape
    reaches, steps = records.shape[1:]
    cap = send_index.shape[3]
    pairs = sections // 2
    basins = basin_home.shape[1] // sections
    blocks = reaches // LANES
    shape = jax.ShapeDtypeStruct
    dma = pltpu.SemaphoreType.DMA

    home = basin_home.reshape(-1, LANES)
    down = down_basin.reshape(-1, LANES)
    listed = send_index.reshape(sections, cap)
    fetched = [
        moisture, heat, moist_cond, heat_cond, rain, surface_flux, cell_reach, home, down, listed
    ]
    *fetched, sec_near, sec_far, lon_near, lon_far = call(
        edges_body,
        [shape(x.shape, x.dtype) for x in fetched]
        + [
            shape((2 * layers, cols), BF16),
            shape((2 * layers, cols), BF16),
            shape((lats, LANES), BF16),
            shape((lats, LANES), BF16),
        ],
        *fetched,
        ins=[HBM] * len(fetched),
        scratch=[dma((len(fetched),))],
        moved=moisture.size * 8,
    )
    *land, home_v, down_v, listed_v = fetched
    swap = lambda count: [(i, i ^ 1) for i in range(count)]
    between = lambda count: [(i, i + 1) for i in range(1, count - 1, 2)] + [
        (i + 1, i) for i in range(1, count - 1, 2)
    ]
    got_sec_far = lax.ppermute(sec_far, "sec", between(sections))
    got_sec_near = lax.ppermute(sec_near, "sec", swap(sections))
    got_lon_far = lax.ppermute(lon_far, "lon", between(lons))
    got_lon_near = lax.ppermute(lon_near, "lon", swap(lons))

    moist_out, heat_out, keep, give = call(
        land_body,
        [
            shape(moisture.shape, F32),
            shape(heat.shape, F32),
            shape((pairs, blocks, LANES), F32),
            shape((pairs, blocks, LANES), BF16),
        ],
        *land,
        got_sec_near, got_sec_far, got_lon_near, got_lon_far,
        moved=moisture.size * 24,
    )
    got = lax.ppermute(give, "sec", swap(sections))
    order, ids = call(
        index_body,
        [shape((blocks, LANES), I32), shape((pairs, PACK_ROWS, LANES), BF16)],
        listed_v, home_v, down_v, send_count,
        ins=[VMEM] * 3 + [HBM],
        scratch=[pltpu.SMEM(send_count.shape, I32), dma((1,))],
        moved=moisture.size * 8,
    )
    aways = []
    for k in range(1, pairs // 2 + 1):
        aways += [k] if 2 * k == pairs else [k, pairs - k]
    own_terms, *terms = call(
        lambda *refs: terms_body(aways, *refs),
        [shape((blocks, LANES), F32)] + [shape((blocks + PACK_ROWS, LANES), BF16)] * len(aways),
        keep, got, ids,
        moved=reaches * 8,
    )
    forward = lambda block, away: lax.ppermute(
        block, "sec", [(i, (i + 2 * away) % sections) for i in range(sections)]
    )
    terms = {away: forward(term, away) for away, term in zip(aways, terms)}
    rec_packed, hyd_packed, records_v, hydro_v = call(
        lambda *refs: first_body(aways[0], *refs),
        [shape((cap, steps), BF16)] * 2 + [shape((reaches, steps), BF16)] * 2,
        order, records[0], unit_hydro[0],
        ins=[VMEM, HBM, HBM],
        scratch=[dma((2,))],
        mib=12,
        flops=4 * cap * reaches * steps,
        moved=reaches * steps * 4,
    )
    runoff, ready = call(
        lambda *refs: send_body(aways[0], *refs),
        [shape((blocks, LANES), F32), shape((cap, steps), BF16)],
        own_terms, order, rec_packed, hyd_packed, *terms.values(),
        moved=cap * steps * 6,
    )
    arrived = {aways[0]: forward(ready, aways[0])}
    record_new, kept, ready = call(
        lambda *refs: record_body(aways[1], *refs),
        [shape((reaches, steps), BF16), shape((reaches, steps), BF16), shape((cap, steps), BF16)],
        runoff, records_v, hydro_v, order,
        mib=16,
        flops=2 * cap * reaches * steps,
        moved=reaches * steps * 8,
    )
    arrived[aways[1]] = forward(ready, aways[1])
    rest = aways[2:] + [0]
    *ready, own = call(
        lambda *refs: rest_body(rest, *refs),
        [shape((cap, steps), BF16)] * len(rest),
        order, kept, arrived[aways[0]],
        mib=16,
        flops=2 * cap * reaches * steps * len(rest),
        moved=reaches * steps * 4,
    )
    for away, block in zip(aways[2:], ready):
        arrived[away] = forward(block, away)
    late = aways[-1:]
    early = aways[:-1]
    theirs, mine = call(
        early_body,
        [shape((basins, steps), F32), shape((basins, steps), F32)],
        ids, *[terms[a] for a in early], own, *[arrived[a] for a in early],
        mib=12,
        moved=basins * steps * 16,
    )
    (theirs,) = call(
        lambda *refs: late_body(True, *refs),
        [shape((basins, steps), BF16)],
        theirs, *[terms[a] for a in late], *[arrived[a] for a in late],
        moved=basins * steps * 8,
    )
    passed = lax.ppermute(theirs, "sec", swap(sections))
    (mine,) = call(
        lambda *refs: late_body(False, *refs),
        [shape((basins, steps), F32)],
        mine, *[terms[a] for a in late], *[arrived[a] for a in late],
        moved=basins * steps * 8,
    )
    (inflow,) = call(
        final_body,
        [shape((basins, steps), F32)],
        mine, passed,
        out_specs=[HBM],
        scratch=[pltpu.VMEM((basins, steps), F32), dma((2,))],
        moved=basins * steps * 10,
    )
    return (moist_out, heat_out, record_new[None], inflow[None])


def solution(mesh):
    placed = (
        P(None, "sec", "lon"),
        P(None, "sec", "lon"),
        P(None, "sec", "lon"),
        P(None, "sec", "lon"),
        P("sec", "lon"),
        P("sec", "lon"),
        P("sec", "lon"),
        P("lon", "sec", None),
        P("lon", "sec", None),
        P("lon", "sec"),
        P("lon", None),
        P("lon", "sec", None, None),
        P("lon", "sec", None),
    )
    return jax.shard_map(
        per_device,
        mesh=mesh,
        in_specs=placed,
        out_specs=(
            P(None, "sec", "lon"),
            P(None, "sec", "lon"),
            P("lon", "sec", None),
            P("lon", "sec", None),
        ),
        check_vma=False,
    )
```

```python
import jax
import jax.numpy as jnp
from jax import lax
from jax.experimental import pallas as pl
from jax.experimental.pallas import tpu as pltpu
from jax.sharding import PartitionSpec as P

LATERAL = 0.2
LANES = 128
PACK_ROWS = 16
F32 = jnp.float32
BF16 = jnp.bfloat16
I32 = jnp.int32
VMEM = pl.BlockSpec(memory_space=pltpu.VMEM)
HBM = pl.BlockSpec(memory_space=pltpu.HBM)


def call(body, outs, *args, ins=None, out_specs=None, scratch=(), mib=8, flops=0, moved=0):
    ins = list(ins) if ins else [VMEM] * len(args)
    args = [
        pltpu.with_memory_space_constraint(arg, pltpu.HBM) if spec is HBM else arg
        for arg, spec in zip(args, ins)
    ]
    return pl.pallas_call(
        body,
        out_shape=list(outs),
        in_specs=ins,
        out_specs=list(out_specs) if out_specs else [VMEM] * len(outs),
        scratch_shapes=list(scratch),
        compiler_params=pltpu.CompilerParams(vmem_limit_bytes=mib * 1024 * 1024),
        cost_estimate=pl.CostEstimate(flops=flops, bytes_accessed=moved, transcendentals=0),
    )(*args)


def fetch(sources, targets, sems):
    copies = [
        pltpu.make_async_copy(src, dst, sems.at[i])
        for i, (src, dst) in enumerate(zip(sources, targets))
    ]
    for copy in copies:
        copy.start()
    return copies


def parity(axis):
    return lax.rem(lax.axis_index(axis), 2)


def edges_body(*refs):
    count = 10
    targets = refs[count : 2 * count]
    moist, heat = targets[:2]
    sec_near, sec_far, lon_near, lon_far, sems = refs[2 * count :]
    copies = fetch(refs[:count], targets, sems)
    layers, rows, cols = moist.shape
    lane = lax.broadcasted_iota(I32, (rows, LANES), 1)
    west = jnp.zeros((rows, LANES), F32)
    east = jnp.zeros((rows, LANES), F32)
    sec_even = parity("sec") == 0
    for f, ref in enumerate((moist, heat)):
        copies[f].wait()
        north = ref[:, 0, :]
        south = ref[:, rows - 1, :]
        sec_near[f * layers : (f + 1) * layers, :] = jnp.where(sec_even, south, north).astype(BF16)
        sec_far[f * layers : (f + 1) * layers, :] = jnp.where(sec_even, north, south).astype(BF16)
        for layer in range(layers):
            k = f * layers + layer
            west = jnp.where(lane == k, ref[layer, :, 0:1], west)
            east = jnp.where(lane == k, ref[layer, :, cols - 1 : cols], east)
    lon_even = parity("lon") == 0
    lon_near[...] = jnp.where(lon_even, east, west).astype(BF16)
    lon_far[...] = jnp.where(lon_even, west, east).astype(BF16)
    for copy in copies[2:]:
        copy.wait()


def lookup(table, hi, lo):
    out = jnp.zeros(hi.shape, table.dtype)
    for row in range(table.shape[0]):
        line = jnp.broadcast_to(table[row : row + 1, :], hi.shape)
        got = jnp.take_along_axis(line, lo, axis=1)
        out = jnp.where(hi == row, got, out)
    return out


def index_body(listed, home, down, count_in, order, ids, count, sems):
    copies = fetch((count_in,), (count,), sems)
    slot = lookup(home[...], down[...] >> 7, down[...] & (LANES - 1))
    pairs, width = listed.shape[0] // 2, listed.shape[1]
    tiles = width // LANES
    chip = lax.axis_index("sec") // 2
    chip_basins = home.shape[0] * LANES // pairs
    pos = lax.broadcasted_iota(I32, (1, width), 1)
    copies[0].wait()
    for m in range(pairs):
        c = count[0, 0, 2 * m]
        second = pltpu.roll(listed[2 * m + 1 : 2 * m + 2, :], lax.rem(c, width), 1)
        line = jnp.where(pos < c, listed[2 * m : 2 * m + 1, :], second)
        away = lax.rem(m - chip + pairs, pairs)
        for t in range(tiles):
            order[pl.ds(away * tiles + t, 1), :] = line[:, t * LANES : (t + 1) * LANES]
    at = order[...]
    place = lookup(slot, at >> 7, at & (LANES - 1))
    pad = jnp.zeros((PACK_ROWS - 2 * tiles, LANES), F32)
    for away in range(pairs):
        m = lax.rem(away + chip, pairs)
        mine = place[away * tiles : (away + 1) * tiles, :] - m * chip_basins
        ids[away] = jnp.concatenate(
            [(mine >> 8).astype(F32), (mine & 255).astype(F32), pad], axis=0
        ).astype(BF16)


def shift_time(x):
    steps = x.shape[1]
    lane = lax.broadcasted_iota(I32, x.shape, 1)
    return jnp.where(lane == steps - 1, 0.0, pltpu.roll(x, steps - 1, 1))


def picked(order, away, tiles, reaches):
    turned = order[...].astype(F32).T
    lane = lax.broadcasted_iota(I32, (LANES, reaches), 1).astype(F32)
    parts = [
        jnp.where(lane == turned[:, t : t + 1], 1.0, 0.0).astype(BF16)
        for t in range(away * tiles, (away + 1) * tiles)
    ]
    return parts[0] if len(parts) == 1 else jnp.concatenate(parts, axis=0)


def first_body(away, order, records, hydro, rec_packed, hyd_packed):
    hot = picked(order, away, rec_packed.shape[0] // LANES, records.shape[0])
    rec = jnp.dot(hot, records[...], preferred_element_type=F32)
    rec_packed[...] = shift_time(rec).astype(BF16)
    hyd_packed[...] = jnp.dot(hot, hydro[...], preferred_element_type=F32).astype(BF16)


def land_body(
    moist, heat, moist_k, heat_k, rain, flux, cell, sec_near, sec_far, lon_near, lon_far, records_in, hydro_in,
    moist_out, heat_out, keep, give, records, hydro, sems,
):
    pieces = sems.shape[0] // 2
    size = records.shape[0] // pieces
    cuts = [pl.ds(i * size, size) for i in range(pieces)]
    copies = fetch(
        [ref.at[cut, :] for ref in (records_in, hydro_in) for cut in cuts],
        [ref.at[cut, :] for ref in (records, hydro) for cut in cuts],
        sems,
    )
    layers, rows, cols = moist.shape
    row = lax.broadcasted_iota(I32, (rows, cols), 0)
    col = lax.broadcasted_iota(I32, (rows, cols), 1)
    sec_even = parity("sec") == 0
    lon_even = parity("lon") == 0
    south_all = jnp.where(sec_even, sec_near[...].astype(F32), sec_far[...].astype(F32))
    north_all = jnp.where(sec_even, sec_far[...].astype(F32), sec_near[...].astype(F32))
    east_all = jnp.where(lon_even, lon_near[...].astype(F32), lon_far[...].astype(F32))
    west_all = jnp.where(lon_even, lon_far[...].astype(F32), lon_near[...].astype(F32))
    for f, (x_ref, k_ref, top, out) in enumerate(
        ((moist, moist_k, rain, moist_out), (heat, heat_k, flux, heat_out))
    ):
        ratio = jnp.zeros((rows, cols), F32)
        value = jnp.zeros((rows, cols), F32)
        below = jnp.zeros((rows, cols), F32)
        ratios, values = [], []
        for layer in range(layers):
            k = f * layers + layer
            x = x_ref[layer]
            up = jnp.where(row == 0, north_all[k : k + 1, :], pltpu.roll(x, 1, 0))
            dn = jnp.where(row == rows - 1, south_all[k : k + 1, :], pltpu.roll(x, rows - 1, 0))
            lf = jnp.where(col == 0, west_all[:, k : k + 1], pltpu.roll(x, 1, 1))
            rt = jnp.where(col == cols - 1, east_all[:, k : k + 1], pltpu.roll(x, cols - 1, 1))
            rhs = x + LATERAL * (up + dn + lf + rt - 4.0 * x)
            if layer == 0:
                rhs = rhs + top[...]
            if layer < layers - 1:
                above = 0.5 * (k_ref[layer] + k_ref[layer + 1])
            else:
                above = jnp.zeros((rows, cols), F32)
            inv = 1.0 / (1.0 + below + above + below * ratio)
            ratio = -above * inv
            value = (rhs + below * value) * inv
            ratios.append(ratio)
            values.append(value)
            below = above
        x = values[-1]
        out[layers - 1] = x
        for layer in range(layers - 2, -1, -1):
            x = values[layer] - ratios[layer] * x
            out[layer] = x
    s = moist_out[0] - 1.0
    soft = jnp.maximum(s, 0.0) + jnp.log1p(jnp.exp(-jnp.abs(s)))
    gate = 1.0 / (1.0 + jnp.exp(-heat_out[0]))
    runoff = soft * gate + 0.5 * moist_k[layers - 1] * moist_out[layers - 1]
    cells = cell[...]
    hi = cells >> 7
    lo = cells & (LANES - 1)
    pairs, blocks = keep.shape[:2]
    his = 2 * pairs * blocks
    hi_iota = lax.broadcasted_iota(I32, (his, cols), 0)
    lo_iota = lax.broadcasted_iota(I32, (LANES, cols), 0)
    acc = jnp.zeros((his, LANES), F32)
    for i in range(rows):
        a = jnp.where(hi_iota == hi[i : i + 1, :], runoff[i : i + 1, :], 0.0).astype(BF16)
        b = jnp.where(lo_iota == lo[i : i + 1, :], 1.0, 0.0).astype(BF16)
        acc = acc + lax.dot_general(a, b, (((1,), (1,)), ((), ())), preferred_element_type=F32)
    both = acc.reshape(pairs, 2, blocks, LANES)
    keep[...] = jnp.where(sec_even, both[:, 0], both[:, 1])
    give[...] = jnp.where(sec_even, both[:, 1], both[:, 0]).astype(BF16)
    for copy in copies:
        copy.wait()


def terms_body(keep, got, ids, own, *outs):
    pairs, blocks = keep.shape[:2]
    chip = lax.axis_index("sec") // 2
    own[...] = keep[chip] + got[chip].astype(F32)
    for flip, out in enumerate(outs, 1):
        m = chip ^ flip
        out[:blocks, :] = (keep[m] + got[m].astype(F32)).astype(BF16)
        out[blocks:, :] = ids[lax.rem(m - chip + pairs, pairs)]


def send_body(away, own, order, ids, rec_packed, hyd_packed, *refs):
    terms, (runoff, ready, places) = refs[:-3], refs[-3:]
    pairs = places.shape[0]
    chip = lax.axis_index("sec") // 2
    places[0] = ids[0]
    for flip, term in enumerate(terms, 1):
        back = lax.rem(chip - (chip ^ flip) + pairs, pairs)
        places[back] = term[term.shape[0] - PACK_ROWS :, :]
    blocks = runoff.shape[0]
    tiles = ready.shape[0] // LANES
    total = own[...]
    for term in terms:
        total = total + term[:blocks, :].astype(F32)
    runoff[...] = total
    at = order[...]
    turned = lookup(total, at >> 7, at & (LANES - 1)).T
    for t in range(tiles):
        rows = pl.ds(t * LANES, LANES)
        col = away * tiles + t
        ready[rows, :] = (
            rec_packed[rows, :].astype(F32) + turned[:, col : col + 1] * hyd_packed[rows, :].astype(F32)
        ).astype(BF16)


def record_body(aways, runoff, records, hydro, order, kept, *ready):
    turned = runoff[...].T
    for t in range(runoff.shape[0]):
        rows = pl.ds(t * LANES, LANES)
        kept[rows, :] = (
            shift_time(records[rows, :].astype(F32)) + turned[:, t : t + 1] * hydro[rows, :].astype(F32)
        ).astype(BF16)
    for away, out in zip(aways, ready):
        hot = picked(order, away, out.shape[0] // LANES, kept.shape[0])
        out[...] = jnp.dot(hot, kept[...], preferred_element_type=F32).astype(BF16)


def rest_body(order, kept, landed, out, own, sem):
    copy = pltpu.make_async_copy(kept, out, sem)
    copy.start()
    hot = picked(order, 0, own.shape[0] // LANES, kept.shape[0])
    own[...] = jnp.dot(hot, kept[...], preferred_element_type=F32).astype(BF16)
    copy.wait()


def hot_of(digits, tiles, basins, other):
    core = parity("sec")
    base = ((1 - core) if other else core) * basins
    slot = lax.broadcasted_iota(I32, (basins, LANES), 0) + base
    slot = slot.astype(F32)
    place = digits[:tiles] * 256.0 + digits[tiles : 2 * tiles]
    parts = [jnp.where(slot == place[t : t + 1, :], 1.0, 0.0).astype(BF16) for t in range(tiles)]
    return parts[0] if len(parts) == 1 else jnp.concatenate(parts, axis=1)


def summed(digits, blocks, basins, other):
    tiles = blocks[0].shape[0] // LANES
    total = None
    for digit, block in zip(digits, blocks):
        hot = hot_of(digit, tiles, basins, other)
        part = jnp.dot(hot, block[...], preferred_element_type=F32)
        total = part if total is None else total + part
    return total


def early_body(aways, places, *refs):
    blocks, (theirs, mine) = refs[:-2], refs[-2:]
    digits = [places[away].astype(F32) for away in aways]
    basins = mine.shape[0]
    theirs[...] = summed(digits, blocks, basins, True)
    mine[...] = summed(digits, blocks, basins, False)


def late_body(aways, other, so_far, places, *refs):
    blocks, out = refs[:-1], refs[-1]
    digits = [places[away].astype(F32) for away in aways]
    out[...] = (so_far[...] + summed(digits, blocks, out.shape[0], other)).astype(out.dtype)


def final_body(mine, passed, out, held, sems):
    rows = mine.shape[0]
    parts = 2
    size = rows // parts
    copies = []
    for i in range(parts):
        at = pl.ds(i * size, size)
        held[at, :] = mine[at, :] + passed[at, :].astype(F32)
        copy = pltpu.make_async_copy(held.at[at, :], out.at[at, :], sems.at[i])
        copy.start()
        copies.append(copy)
    for copy in copies:
        copy.wait()


def per_device(
    moisture, heat, moist_cond, heat_cond, rain, surface_flux, cell_reach,
    records, unit_hydro, down_basin, basin_home, send_index, send_count,
):
    lons = lax.axis_size("lon")
    sections = lax.axis_size("sec")
    layers, lats, cols = moisture.shape
    reaches, steps = records.shape[1:]
    cap = send_index.shape[3]
    pairs = sections // 2
    basins = basin_home.shape[1] // sections
    blocks = reaches // LANES
    shape = jax.ShapeDtypeStruct
    dma = pltpu.SemaphoreType.DMA

    home = basin_home.reshape(-1, LANES)
    down = down_basin.reshape(-1, LANES)
    listed = send_index.reshape(sections, cap)
    fetched = [
        moisture, heat, moist_cond, heat_cond, rain, surface_flux, cell_reach, home, down, listed
    ]
    *fetched, sec_near, sec_far, lon_near, lon_far = call(
        edges_body,
        [shape(x.shape, x.dtype) for x in fetched]
        + [
            shape((2 * layers, cols), BF16),
            shape((2 * layers, cols), BF16),
            shape((lats, LANES), BF16),
            shape((lats, LANES), BF16),
        ],
        *fetched,
        ins=[HBM] * len(fetched),
        scratch=[dma((len(fetched),))],
        moved=moisture.size * 8,
    )
    *land, home_v, down_v, listed_v = fetched
    swap = lambda count: [(i, i ^ 1) for i in range(count)]
    between = lambda count: [(i, i + 1) for i in range(1, count - 1, 2)] + [
        (i + 1, i) for i in range(1, count - 1, 2)
    ]
    got_sec_far = lax.ppermute(sec_far, "sec", between(sections))
    got_sec_near = lax.ppermute(sec_near, "sec", swap(sections))
    got_lon_far = lax.ppermute(lon_far, "lon", between(lons))
    got_lon_near = lax.ppermute(lon_near, "lon", swap(lons))

    moist_out, heat_out, keep, give, records_v, hydro_v = call(
        land_body,
        [
            shape(moisture.shape, F32),
            shape(heat.shape, F32),
            shape((pairs, blocks, LANES), F32),
            shape((pairs, blocks, LANES), BF16),
            shape((reaches, steps), BF16),
            shape((reaches, steps), BF16),
        ],
        *land,
        got_sec_near, got_sec_far, got_lon_near, got_lon_far, records[0], unit_hydro[0],
        ins=[VMEM] * (len(land) + 4) + [HBM] * 2,
        scratch=[dma((8,))],
        mib=12,
        moved=moisture.size * 24,
    )
    got = lax.ppermute(give, "sec", swap(sections))
    order, ids = call(
        index_body,
        [shape((blocks, LANES), I32), shape((pairs, PACK_ROWS, LANES), BF16)],
        listed_v, home_v, down_v, send_count,
        ins=[VMEM] * 3 + [HBM],
        scratch=[pltpu.SMEM(send_count.shape, I32), dma((1,))],
        moved=moisture.size * 8,
    )
    aways = []
    for k in range(1, pairs // 2 + 1):
        aways += [k] if 2 * k == pairs else [k, pairs - k]
    own_terms, *terms = call(
        terms_body,
        [shape((blocks, LANES), F32)] + [shape((blocks + PACK_ROWS, LANES), BF16)] * (pairs - 1),
        keep, got, ids,
        moved=reaches * 8,
    )
    forward = lambda block, away: lax.ppermute(
        block, "sec", [(i, (i + 2 * away) % sections) for i in range(sections)]
    )
    terms = [
        lax.ppermute(term, "sec", [(i, i ^ (2 * flip)) for i in range(sections)])
        for flip, term in enumerate(terms, 1)
    ]
    rec_packed, hyd_packed = call(
        lambda *refs: first_body(aways[0], *refs),
        [shape((cap, steps), BF16)] * 2,
        order, records_v, hydro_v,
        mib=12,
        flops=4 * cap * reaches * steps,
        moved=reaches * steps * 4,
    )
    runoff, ready, places = call(
        lambda *refs: send_body(aways[0], *refs),
        [shape((blocks, LANES), F32), shape((cap, steps), BF16), shape(ids.shape, BF16)],
        own_terms, order, ids, rec_packed, hyd_packed, *terms,
        moved=cap * steps * 6,
    )
    arrived = {aways[0]: forward(ready, aways[0])}
    kept, *ready = call(
        lambda *refs: record_body(aways[1:], *refs),
        [shape((reaches, steps), BF16)] + [shape((cap, steps), BF16)] * (len(aways) - 1),
        runoff, records_v, hydro_v, order,
        mib=16,
        flops=2 * cap * reaches * steps,
        moved=reaches * steps * 8,
    )
    for away, block in zip(aways[1:], ready):
        arrived[away] = forward(block, away)
    record_new, own = call(
        rest_body,
        [shape((reaches, steps), BF16), shape((cap, steps), BF16)],
        order, kept, arrived[aways[0]],
        out_specs=[HBM, VMEM],
        scratch=[dma(())],
        mib=16,
        flops=2 * cap * reaches * steps,
        moved=reaches * steps * 4,
    )
    late = aways[-1:]
    early = [0] + aways[:-1]
    arrived[0] = own
    theirs, mine = call(
        lambda *refs: early_body(early, *refs),
        [shape((basins, steps), F32), shape((basins, steps), F32)],
        places, *[arrived[a] for a in early],
        mib=12,
        moved=basins * steps * 16,
    )
    (theirs,) = call(
        lambda *refs: late_body(late, True, *refs),
        [shape((basins, steps), BF16)],
        theirs, places, *[arrived[a] for a in late],
        moved=basins * steps * 8,
    )
    passed = lax.ppermute(theirs, "sec", swap(sections))
    (mine,) = call(
        lambda *refs: late_body(late, False, *refs),
        [shape((basins, steps), F32)],
        mine, places, *[arrived[a] for a in late],
        moved=basins * steps * 8,
    )
    (inflow,) = call(
        final_body,
        [shape((basins, steps), F32)],
        mine, passed,
        out_specs=[HBM],
        scratch=[pltpu.VMEM((basins, steps), F32), dma((2,))],
        moved=basins * steps * 10,
    )
    return (moist_out, heat_out, record_new[None], inflow[None])


def solution(mesh):
    placed = (
        P(None, "sec", "lon"),
        P(None, "sec", "lon"),
        P(None, "sec", "lon"),
        P(None, "sec", "lon"),
        P("sec", "lon"),
        P("sec", "lon"),
        P("sec", "lon"),
        P("lon", "sec", None),
        P("lon", "sec", None),
        P("lon", "sec"),
        P("lon", None),
        P("lon", "sec", None, None),
        P("lon", "sec", None),
    )
    return jax.shard_map(
        per_device,
        mesh=mesh,
        in_specs=placed,
        out_specs=(
            P(None, "sec", "lon"),
            P(None, "sec", "lon"),
            P("lon", "sec", None),
            P("lon", "sec", None),
        ),
        check_vma=False,
    )
```

```python
import jax
import jax.numpy as jnp
from jax import lax
from jax.experimental import pallas as pl
from jax.experimental.pallas import tpu as pltpu
from jax.sharding import PartitionSpec as P

LATERAL = 0.2
LANES = 128
PACK_ROWS = 16
F32 = jnp.float32
BF16 = jnp.bfloat16
I32 = jnp.int32
VMEM = pl.BlockSpec(memory_space=pltpu.VMEM)
HBM = pl.BlockSpec(memory_space=pltpu.HBM)


def call(body, outs, *args, ins=None, out_specs=None, scratch=(), mib=8, flops=0, moved=0):
    ins = list(ins) if ins else [VMEM] * len(args)
    args = [
        pltpu.with_memory_space_constraint(arg, pltpu.HBM) if spec is HBM else arg
        for arg, spec in zip(args, ins)
    ]
    return pl.pallas_call(
        body,
        out_shape=list(outs),
        in_specs=ins,
        out_specs=list(out_specs) if out_specs else [VMEM] * len(outs),
        scratch_shapes=list(scratch),
        compiler_params=pltpu.CompilerParams(vmem_limit_bytes=mib * 1024 * 1024),
        cost_estimate=pl.CostEstimate(flops=flops, bytes_accessed=moved, transcendentals=0),
    )(*args)


def fetch(sources, targets, sems):
    copies = [
        pltpu.make_async_copy(src, dst, sems.at[i])
        for i, (src, dst) in enumerate(zip(sources, targets))
    ]
    for copy in copies:
        copy.start()
    return copies


def parity(axis):
    return lax.rem(lax.axis_index(axis), 2)


def edges_body(*refs):
    count = 10
    targets = refs[count : 2 * count]
    moist, heat = targets[:2]
    sec_near, sec_far, lon_near, lon_far, sems = refs[2 * count :]
    copies = fetch(refs[:count], targets, sems)
    layers, rows, cols = moist.shape
    lane = lax.broadcasted_iota(I32, (rows, LANES), 1)
    west = jnp.zeros((rows, LANES), F32)
    east = jnp.zeros((rows, LANES), F32)
    sec_even = parity("sec") == 0
    for f, ref in enumerate((moist, heat)):
        copies[f].wait()
        north = ref[:, 0, :]
        south = ref[:, rows - 1, :]
        sec_near[f * layers : (f + 1) * layers, :] = jnp.where(sec_even, south, north).astype(BF16)
        sec_far[f * layers : (f + 1) * layers, :] = jnp.where(sec_even, north, south).astype(BF16)
        for layer in range(layers):
            k = f * layers + layer
            west = jnp.where(lane == k, ref[layer, :, 0:1], west)
            east = jnp.where(lane == k, ref[layer, :, cols - 1 : cols], east)
    lon_even = parity("lon") == 0
    lon_near[...] = jnp.where(lon_even, east, west).astype(BF16)
    lon_far[...] = jnp.where(lon_even, west, east).astype(BF16)
    for copy in copies[2:]:
        copy.wait()


def lookup(table, hi, lo):
    out = jnp.zeros(hi.shape, table.dtype)
    for row in range(table.shape[0]):
        line = jnp.broadcast_to(table[row : row + 1, :], hi.shape)
        got = jnp.take_along_axis(line, lo, axis=1)
        out = jnp.where(hi == row, got, out)
    return out


def index_body(listed, home, down, count_in, order, ids, count, sems):
    copies = fetch((count_in,), (count,), sems)
    slot = lookup(home[...], down[...] >> 7, down[...] & (LANES - 1))
    pairs, width = listed.shape[0] // 2, listed.shape[1]
    tiles = width // LANES
    chip = lax.axis_index("sec") // 2
    chip_basins = home.shape[0] * LANES // pairs
    pos = lax.broadcasted_iota(I32, (1, width), 1)
    copies[0].wait()
    for m in range(pairs):
        c = count[0, 0, 2 * m]
        second = pltpu.roll(listed[2 * m + 1 : 2 * m + 2, :], lax.rem(c, width), 1)
        line = jnp.where(pos < c, listed[2 * m : 2 * m + 1, :], second)
        away = m ^ chip
        for t in range(tiles):
            order[pl.ds(away * tiles + t, 1), :] = line[:, t * LANES : (t + 1) * LANES]
    at = order[...]
    place = lookup(slot, at >> 7, at & (LANES - 1))
    pad = jnp.zeros((PACK_ROWS - 2 * tiles, LANES), F32)
    for away in range(pairs):
        m = away ^ chip
        mine = place[away * tiles : (away + 1) * tiles, :] - m * chip_basins
        ids[away] = jnp.concatenate(
            [(mine >> 8).astype(F32), (mine & 255).astype(F32), pad], axis=0
        ).astype(BF16)


def shift_time(x):
    steps = x.shape[1]
    lane = lax.broadcasted_iota(I32, x.shape, 1)
    return jnp.where(lane == steps - 1, 0.0, pltpu.roll(x, steps - 1, 1))


def picked(order, away, tiles, reaches):
    turned = order[...].astype(F32).T
    lane = lax.broadcasted_iota(I32, (LANES, reaches), 1).astype(F32)
    parts = [
        jnp.where(lane == turned[:, t : t + 1], 1.0, 0.0).astype(BF16)
        for t in range(away * tiles, (away + 1) * tiles)
    ]
    return parts[0] if len(parts) == 1 else jnp.concatenate(parts, axis=0)


def first_body(away, order, records, hydro, rec_packed, hyd_packed):
    hot = picked(order, away, rec_packed.shape[0] // LANES, records.shape[0])
    rec = jnp.dot(hot, records[...], preferred_element_type=F32)
    rec_packed[...] = shift_time(rec).astype(BF16)
    hyd_packed[...] = jnp.dot(hot, hydro[...], preferred_element_type=F32).astype(BF16)


def land_body(
    moist, heat, moist_k, heat_k, rain, flux, cell, sec_near, sec_far, lon_near, lon_far,
    moist_out, heat_out, keep, give,
):
    layers, rows, cols = moist.shape
    row = lax.broadcasted_iota(I32, (rows, cols), 0)
    col = lax.broadcasted_iota(I32, (rows, cols), 1)
    sec_even = parity("sec") == 0
    lon_even = parity("lon") == 0
    south_all = jnp.where(sec_even, sec_near[...].astype(F32), sec_far[...].astype(F32))
    north_all = jnp.where(sec_even, sec_far[...].astype(F32), sec_near[...].astype(F32))
    east_all = jnp.where(lon_even, lon_near[...].astype(F32), lon_far[...].astype(F32))
    west_all = jnp.where(lon_even, lon_far[...].astype(F32), lon_near[...].astype(F32))
    for f, (x_ref, k_ref, top, out) in enumerate(
        ((moist, moist_k, rain, moist_out), (heat, heat_k, flux, heat_out))
    ):
        ratio = jnp.zeros((rows, cols), F32)
        value = jnp.zeros((rows, cols), F32)
        below = jnp.zeros((rows, cols), F32)
        ratios, values = [], []
        for layer in range(layers):
            k = f * layers + layer
            x = x_ref[layer]
            up = jnp.where(row == 0, north_all[k : k + 1, :], pltpu.roll(x, 1, 0))
            dn = jnp.where(row == rows - 1, south_all[k : k + 1, :], pltpu.roll(x, rows - 1, 0))
            lf = jnp.where(col == 0, west_all[:, k : k + 1], pltpu.roll(x, 1, 1))
            rt = jnp.where(col == cols - 1, east_all[:, k : k + 1], pltpu.roll(x, cols - 1, 1))
            rhs = x + LATERAL * (up + dn + lf + rt - 4.0 * x)
            if layer == 0:
                rhs = rhs + top[...]
            if layer < layers - 1:
                above = 0.5 * (k_ref[layer] + k_ref[layer + 1])
            else:
                above = jnp.zeros((rows, cols), F32)
            inv = 1.0 / (1.0 + below + above + below * ratio)
            ratio = -above * inv
            value = (rhs + below * value) * inv
            ratios.append(ratio)
            values.append(value)
            below = above
        x = values[-1]
        out[layers - 1] = x
        for layer in range(layers - 2, -1, -1):
            x = values[layer] - ratios[layer] * x
            out[layer] = x
    s = moist_out[0] - 1.0
    soft = jnp.maximum(s, 0.0) + jnp.log1p(jnp.exp(-jnp.abs(s)))
    gate = 1.0 / (1.0 + jnp.exp(-heat_out[0]))
    runoff = soft * gate + 0.5 * moist_k[layers - 1] * moist_out[layers - 1]
    cells = cell[...]
    hi = cells >> 7
    lo = cells & (LANES - 1)
    pairs, blocks = keep.shape[:2]
    his = 2 * pairs * blocks
    hi_iota = lax.broadcasted_iota(I32, (his, cols), 0)
    lo_iota = lax.broadcasted_iota(I32, (LANES, cols), 0)
    acc = jnp.zeros((his, LANES), F32)
    for i in range(rows):
        a = jnp.where(hi_iota == hi[i : i + 1, :], runoff[i : i + 1, :], 0.0).astype(BF16)
        b = jnp.where(lo_iota == lo[i : i + 1, :], 1.0, 0.0).astype(BF16)
        acc = acc + lax.dot_general(a, b, (((1,), (1,)), ((), ())), preferred_element_type=F32)
    both = acc.reshape(pairs, 2, blocks, LANES)
    keep[...] = jnp.where(sec_even, both[:, 0], both[:, 1])
    give[...] = jnp.where(sec_even, both[:, 1], both[:, 0]).astype(BF16)


def terms_body(keep, got, ids, own, *outs):
    pairs, blocks = keep.shape[:2]
    chip = lax.axis_index("sec") // 2
    own[...] = keep[chip] + got[chip].astype(F32)
    for flip, out in enumerate(outs, 1):
        m = chip ^ flip
        out[:blocks, :] = (keep[m] + got[m].astype(F32)).astype(BF16)
        out[blocks:, :] = ids[flip]


def send_body(away, own, order, ids, rec_packed, hyd_packed, *refs):
    terms, (runoff, ready, places) = refs[:-3], refs[-3:]
    places[0] = ids[0]
    for flip, term in enumerate(terms, 1):
        places[flip] = term[term.shape[0] - PACK_ROWS :, :]
    blocks = runoff.shape[0]
    tiles = ready.shape[0] // LANES
    total = own[...]
    for term in terms:
        total = total + term[:blocks, :].astype(F32)
    runoff[...] = total
    at = order[...]
    turned = lookup(total, at >> 7, at & (LANES - 1)).T
    for t in range(tiles):
        rows = pl.ds(t * LANES, LANES)
        col = away * tiles + t
        ready[rows, :] = (
            rec_packed[rows, :].astype(F32) + turned[:, col : col + 1] * hyd_packed[rows, :].astype(F32)
        ).astype(BF16)


def record_body(aways, runoff, records, hydro, order, kept, *ready):
    turned = runoff[...].T
    for t in range(runoff.shape[0]):
        rows = pl.ds(t * LANES, LANES)
        kept[rows, :] = (
            shift_time(records[rows, :].astype(F32)) + turned[:, t : t + 1] * hydro[rows, :].astype(F32)
        ).astype(BF16)
    for away, out in zip(aways, ready):
        hot = picked(order, away, out.shape[0] // LANES, kept.shape[0])
        out[...] = jnp.dot(hot, kept[...], preferred_element_type=F32).astype(BF16)


def rest_body(order, kept, landed, out, own, sem):
    copy = pltpu.make_async_copy(kept, out, sem)
    copy.start()
    hot = picked(order, 0, own.shape[0] // LANES, kept.shape[0])
    own[...] = jnp.dot(hot, kept[...], preferred_element_type=F32).astype(BF16)
    copy.wait()


def hot_of(digits, tiles, basins, other):
    core = parity("sec")
    base = ((1 - core) if other else core) * basins
    slot = lax.broadcasted_iota(I32, (basins, LANES), 0) + base
    slot = slot.astype(F32)
    place = digits[:tiles] * 256.0 + digits[tiles : 2 * tiles]
    parts = [jnp.where(slot == place[t : t + 1, :], 1.0, 0.0).astype(BF16) for t in range(tiles)]
    return parts[0] if len(parts) == 1 else jnp.concatenate(parts, axis=1)


def summed(digits, blocks, basins, other):
    tiles = blocks[0].shape[0] // LANES
    total = None
    for digit, block in zip(digits, blocks):
        hot = hot_of(digit, tiles, basins, other)
        part = jnp.dot(hot, block[...], preferred_element_type=F32)
        total = part if total is None else total + part
    return total


def early_body(aways, places, *refs):
    blocks, (theirs, mine) = refs[:-2], refs[-2:]
    digits = [places[away].astype(F32) for away in aways]
    basins = mine.shape[0]
    theirs[...] = summed(digits, blocks, basins, True)
    mine[...] = summed(digits, blocks, basins, False)


def late_body(aways, other, so_far, places, *refs):
    blocks, out = refs[:-1], refs[-1]
    digits = [places[away].astype(F32) for away in aways]
    out[...] = (so_far[...] + summed(digits, blocks, out.shape[0], other)).astype(out.dtype)


def final_body(mine, passed, out, held, sems):
    rows = mine.shape[0]
    parts = 2
    size = rows // parts
    copies = []
    for i in range(parts):
        at = pl.ds(i * size, size)
        held[at, :] = mine[at, :] + passed[at, :].astype(F32)
        copy = pltpu.make_async_copy(held.at[at, :], out.at[at, :], sems.at[i])
        copy.start()
        copies.append(copy)
    for copy in copies:
        copy.wait()


def per_device(
    moisture, heat, moist_cond, heat_cond, rain, surface_flux, cell_reach,
    records, unit_hydro, down_basin, basin_home, send_index, send_count,
):
    lons = lax.axis_size("lon")
    sections = lax.axis_size("sec")
    layers, lats, cols = moisture.shape
    reaches, steps = records.shape[1:]
    cap = send_index.shape[3]
    pairs = sections // 2
    basins = basin_home.shape[1] // sections
    blocks = reaches // LANES
    shape = jax.ShapeDtypeStruct
    dma = pltpu.SemaphoreType.DMA

    home = basin_home.reshape(-1, LANES)
    down = down_basin.reshape(-1, LANES)
    listed = send_index.reshape(sections, cap)
    fetched = [
        moisture, heat, moist_cond, heat_cond, rain, surface_flux, cell_reach, home, down, listed
    ]
    *fetched, sec_near, sec_far, lon_near, lon_far = call(
        edges_body,
        [shape(x.shape, x.dtype) for x in fetched]
        + [
            shape((2 * layers, cols), BF16),
            shape((2 * layers, cols), BF16),
            shape((lats, LANES), BF16),
            shape((lats, LANES), BF16),
        ],
        *fetched,
        ins=[HBM] * len(fetched),
        scratch=[dma((len(fetched),))],
        moved=moisture.size * 8,
    )
    *land, home_v, down_v, listed_v = fetched
    swap = lambda count: [(i, i ^ 1) for i in range(count)]
    between = lambda count: [(i, i + 1) for i in range(1, count - 1, 2)] + [
        (i + 1, i) for i in range(1, count - 1, 2)
    ]
    got_sec_far = lax.ppermute(sec_far, "sec", between(sections))
    got_sec_near = lax.ppermute(sec_near, "sec", swap(sections))
    got_lon_far = lax.ppermute(lon_far, "lon", between(lons))
    got_lon_near = lax.ppermute(lon_near, "lon", swap(lons))

    moist_out, heat_out, keep, give = call(
        land_body,
        [
            shape(moisture.shape, F32),
            shape(heat.shape, F32),
            shape((pairs, blocks, LANES), F32),
            shape((pairs, blocks, LANES), BF16),
        ],
        *land,
        got_sec_near, got_sec_far, got_lon_near, got_lon_far,
        moved=moisture.size * 24,
    )
    got = lax.ppermute(give, "sec", swap(sections))
    order, ids = call(
        index_body,
        [shape((blocks, LANES), I32), shape((pairs, PACK_ROWS, LANES), BF16)],
        listed_v, home_v, down_v, send_count,
        ins=[VMEM] * 3 + [HBM],
        scratch=[pltpu.SMEM(send_count.shape, I32), dma((1,))],
        moved=moisture.size * 8,
    )
    aways = []
    for k in range(1, pairs // 2 + 1):
        aways += [k] if 2 * k == pairs else [pairs - k, k]
    own_terms, *terms = call(
        terms_body,
        [shape((blocks, LANES), F32)] + [shape((blocks + PACK_ROWS, LANES), BF16)] * (pairs - 1),
        keep, got, ids,
        moved=reaches * 8,
    )
    forward = lambda block, away: lax.ppermute(
        block, "sec", [(i, i ^ (2 * away)) for i in range(sections)]
    )
    terms = [forward(term, flip) for flip, term in enumerate(terms, 1)]
    rec_packed, hyd_packed = call(
        lambda *refs: first_body(aways[0], *refs),
        [shape((cap, steps), BF16)] * 2,
        order, records[0], unit_hydro[0],
        mib=12,
        flops=4 * cap * reaches * steps,
        moved=reaches * steps * 4,
    )
    runoff, ready, places = call(
        lambda *refs: send_body(aways[0], *refs),
        [shape((blocks, LANES), F32), shape((cap, steps), BF16), shape(ids.shape, BF16)],
        own_terms, order, ids, rec_packed, hyd_packed, *terms,
        moved=cap * steps * 6,
    )
    arrived = {aways[0]: forward(ready, aways[0])}
    kept, *ready = call(
        lambda *refs: record_body(aways[1:], *refs),
        [shape((reaches, steps), BF16)] + [shape((cap, steps), BF16)] * (len(aways) - 1),
        runoff, records[0], unit_hydro[0], order,
        mib=16,
        flops=2 * cap * reaches * steps,
        moved=reaches * steps * 8,
    )
    for away, block in zip(aways[1:], ready):
        arrived[away] = forward(block, away)
    record_new, own = call(
        rest_body,
        [shape((reaches, steps), BF16), shape((cap, steps), BF16)],
        order, kept, arrived[aways[0]],
        out_specs=[HBM, VMEM],
        scratch=[dma(())],
        mib=16,
        flops=2 * cap * reaches * steps,
        moved=reaches * steps * 4,
    )
    late = aways[-1:]
    early = [0] + aways[:-1]
    arrived[0] = own
    theirs, mine = call(
        lambda *refs: early_body(early, *refs),
        [shape((basins, steps), F32), shape((basins, steps), F32)],
        places, *[arrived[a] for a in early],
        mib=12,
        moved=basins * steps * 16,
    )
    (theirs,) = call(
        lambda *refs: late_body(late, True, *refs),
        [shape((basins, steps), BF16)],
        theirs, places, *[arrived[a] for a in late],
        moved=basins * steps * 8,
    )
    passed = lax.ppermute(theirs, "sec", swap(sections))
    (mine,) = call(
        lambda *refs: late_body(late, False, *refs),
        [shape((basins, steps), F32)],
        mine, places, *[arrived[a] for a in late],
        moved=basins * steps * 8,
    )
    (inflow,) = call(
        final_body,
        [shape((basins, steps), F32)],
        mine, passed,
        out_specs=[HBM],
        scratch=[pltpu.VMEM((basins, steps), F32), dma((2,))],
        moved=basins * steps * 10,
    )
    return (moist_out, heat_out, record_new[None], inflow[None])


def solution(mesh):
    placed = (
        P(None, "sec", "lon"),
        P(None, "sec", "lon"),
        P(None, "sec", "lon"),
        P(None, "sec", "lon"),
        P("sec", "lon"),
        P("sec", "lon"),
        P("sec", "lon"),
        P("lon", "sec", None),
        P("lon", "sec", None),
        P("lon", "sec"),
        P("lon", None),
        P("lon", "sec", None, None),
        P("lon", "sec", None),
    )
    return jax.shard_map(
        per_device,
        mesh=mesh,
        in_specs=placed,
        out_specs=(
            P(None, "sec", "lon"),
            P(None, "sec", "lon"),
            P("lon", "sec", None),
            P("lon", "sec", None),
        ),
        check_vma=False,
    )
```

```python
import jax
import jax.numpy as jnp
from jax import lax
from jax.experimental import pallas as pl
from jax.experimental.pallas import tpu as pltpu
from jax.sharding import PartitionSpec as P

LATERAL = 0.2
LANES = 128
PACK_ROWS = 16
F32 = jnp.float32
BF16 = jnp.bfloat16
I32 = jnp.int32
VMEM = pl.BlockSpec(memory_space=pltpu.VMEM)
HBM = pl.BlockSpec(memory_space=pltpu.HBM)


def call(body, outs, *args, ins=None, out_specs=None, scratch=(), mib=8, flops=0, moved=0):
    ins = list(ins) if ins else [VMEM] * len(args)
    args = [
        pltpu.with_memory_space_constraint(arg, pltpu.HBM) if spec is HBM else arg
        for arg, spec in zip(args, ins)
    ]
    return pl.pallas_call(
        body,
        out_shape=list(outs),
        in_specs=ins,
        out_specs=list(out_specs) if out_specs else [VMEM] * len(outs),
        scratch_shapes=list(scratch),
        compiler_params=pltpu.CompilerParams(vmem_limit_bytes=mib * 1024 * 1024),
        cost_estimate=pl.CostEstimate(flops=flops, bytes_accessed=moved, transcendentals=0),
    )(*args)


def fetch(sources, targets, sems):
    copies = [
        pltpu.make_async_copy(src, dst, sems.at[i])
        for i, (src, dst) in enumerate(zip(sources, targets))
    ]
    for copy in copies:
        copy.start()
    return copies


def parity(axis):
    return lax.rem(lax.axis_index(axis), 2)


def edges_body(*refs):
    count = 10
    targets = refs[count : 2 * count]
    moist, heat = targets[:2]
    sec_near, sec_far, lon_near, lon_far, sems = refs[2 * count :]
    copies = fetch(refs[:count], targets, sems)
    layers, rows, cols = moist.shape
    lane = lax.broadcasted_iota(I32, (rows, LANES), 1)
    west = jnp.zeros((rows, LANES), F32)
    east = jnp.zeros((rows, LANES), F32)
    sec_even = parity("sec") == 0
    for f, ref in enumerate((moist, heat)):
        copies[f].wait()
        north = ref[:, 0, :]
        south = ref[:, rows - 1, :]
        sec_near[f * layers : (f + 1) * layers, :] = jnp.where(sec_even, south, north).astype(BF16)
        sec_far[f * layers : (f + 1) * layers, :] = jnp.where(sec_even, north, south).astype(BF16)
        for layer in range(layers):
            k = f * layers + layer
            west = jnp.where(lane == k, ref[layer, :, 0:1], west)
            east = jnp.where(lane == k, ref[layer, :, cols - 1 : cols], east)
    lon_even = parity("lon") == 0
    lon_near[...] = jnp.where(lon_even, east, west).astype(BF16)
    lon_far[...] = jnp.where(lon_even, west, east).astype(BF16)
    for copy in copies[2:]:
        copy.wait()


def lookup(table, hi, lo):
    out = jnp.zeros(hi.shape, table.dtype)
    for row in range(table.shape[0]):
        line = jnp.broadcast_to(table[row : row + 1, :], hi.shape)
        got = jnp.take_along_axis(line, lo, axis=1)
        out = jnp.where(hi == row, got, out)
    return out


def index_body(listed, home, down, count_in, order, ids, count, sems):
    copies = fetch((count_in,), (count,), sems)
    slot = lookup(home[...], down[...] >> 7, down[...] & (LANES - 1))
    pairs, width = listed.shape[0] // 2, listed.shape[1]
    tiles = width // LANES
    chip = lax.axis_index("sec") // 2
    chip_basins = home.shape[0] * LANES // pairs
    pos = lax.broadcasted_iota(I32, (1, width), 1)
    copies[0].wait()
    for m in range(pairs):
        c = count[0, 0, 2 * m]
        second = pltpu.roll(listed[2 * m + 1 : 2 * m + 2, :], lax.rem(c, width), 1)
        line = jnp.where(pos < c, listed[2 * m : 2 * m + 1, :], second)
        away = m ^ chip
        for t in range(tiles):
            order[pl.ds(away * tiles + t, 1), :] = line[:, t * LANES : (t + 1) * LANES]
    at = order[...]
    place = lookup(slot, at >> 7, at & (LANES - 1))
    pad = jnp.zeros((PACK_ROWS - 2 * tiles, LANES), F32)
    for away in range(pairs):
        m = away ^ chip
        mine = place[away * tiles : (away + 1) * tiles, :] - m * chip_basins
        ids[away] = jnp.concatenate(
            [(mine >> 8).astype(F32), (mine & 255).astype(F32), pad], axis=0
        ).astype(BF16)


def shift_time(x):
    steps = x.shape[1]
    lane = lax.broadcasted_iota(I32, x.shape, 1)
    return jnp.where(lane == steps - 1, 0.0, pltpu.roll(x, steps - 1, 1))


def picked(order, away, tiles, reaches):
    turned = order[...].astype(F32).T
    lane = lax.broadcasted_iota(I32, (LANES, reaches), 1).astype(F32)
    parts = [
        jnp.where(lane == turned[:, t : t + 1], 1.0, 0.0).astype(BF16)
        for t in range(away * tiles, (away + 1) * tiles)
    ]
    return parts[0] if len(parts) == 1 else jnp.concatenate(parts, axis=0)


def first_body(away, shifted, order, rows, packed):
    hot = picked(order, away, packed.shape[0] // LANES, rows.shape[0])
    out = jnp.dot(hot, rows[...], preferred_element_type=F32)
    packed[...] = (shift_time(out) if shifted else out).astype(BF16)


def land_body(
    moist, heat, moist_k, heat_k, rain, flux, cell, sec_near, sec_far, lon_near, lon_far,
    moist_out, heat_out, keep, give,
):
    layers, rows, cols = moist.shape
    row = lax.broadcasted_iota(I32, (rows, cols), 0)
    col = lax.broadcasted_iota(I32, (rows, cols), 1)
    sec_even = parity("sec") == 0
    lon_even = parity("lon") == 0
    south_all = jnp.where(sec_even, sec_near[...].astype(F32), sec_far[...].astype(F32))
    north_all = jnp.where(sec_even, sec_far[...].astype(F32), sec_near[...].astype(F32))
    east_all = jnp.where(lon_even, lon_near[...].astype(F32), lon_far[...].astype(F32))
    west_all = jnp.where(lon_even, lon_far[...].astype(F32), lon_near[...].astype(F32))
    for f, (x_ref, k_ref, top, out) in enumerate(
        ((moist, moist_k, rain, moist_out), (heat, heat_k, flux, heat_out))
    ):
        ratio = jnp.zeros((rows, cols), F32)
        value = jnp.zeros((rows, cols), F32)
        below = jnp.zeros((rows, cols), F32)
        ratios, values = [], []
        for layer in range(layers):
            k = f * layers + layer
            x = x_ref[layer]
            up = jnp.where(row == 0, north_all[k : k + 1, :], pltpu.roll(x, 1, 0))
            dn = jnp.where(row == rows - 1, south_all[k : k + 1, :], pltpu.roll(x, rows - 1, 0))
            lf = jnp.where(col == 0, west_all[:, k : k + 1], pltpu.roll(x, 1, 1))
            rt = jnp.where(col == cols - 1, east_all[:, k : k + 1], pltpu.roll(x, cols - 1, 1))
            rhs = x + LATERAL * (up + dn + lf + rt - 4.0 * x)
            if layer == 0:
                rhs = rhs + top[...]
            if layer < layers - 1:
                above = 0.5 * (k_ref[layer] + k_ref[layer + 1])
            else:
                above = jnp.zeros((rows, cols), F32)
            inv = 1.0 / (1.0 + below + above + below * ratio)
            ratio = -above * inv
            value = (rhs + below * value) * inv
            ratios.append(ratio)
            values.append(value)
            below = above
        x = values[-1]
        out[layers - 1] = x
        for layer in range(layers - 2, -1, -1):
            x = values[layer] - ratios[layer] * x
            out[layer] = x
    s = moist_out[0] - 1.0
    soft = jnp.maximum(s, 0.0) + jnp.log1p(jnp.exp(-jnp.abs(s)))
    gate = 1.0 / (1.0 + jnp.exp(-heat_out[0]))
    runoff = soft * gate + 0.5 * moist_k[layers - 1] * moist_out[layers - 1]
    cells = cell[...]
    hi = cells >> 7
    lo = cells & (LANES - 1)
    pairs, blocks = keep.shape[:2]
    his = 2 * pairs * blocks
    hi_iota = lax.broadcasted_iota(I32, (his, cols), 0)
    lo_iota = lax.broadcasted_iota(I32, (LANES, cols), 0)
    acc = jnp.zeros((his, LANES), F32)
    for i in range(rows):
        a = jnp.where(hi_iota == hi[i : i + 1, :], runoff[i : i + 1, :], 0.0).astype(BF16)
        b = jnp.where(lo_iota == lo[i : i + 1, :], 1.0, 0.0).astype(BF16)
        acc = acc + lax.dot_general(a, b, (((1,), (1,)), ((), ())), preferred_element_type=F32)
    both = acc.reshape(pairs, 2, blocks, LANES)
    keep[...] = jnp.where(sec_even, both[:, 0], both[:, 1])
    give[...] = jnp.where(sec_even, both[:, 1], both[:, 0]).astype(BF16)


def sources(bits):
    found = [(0, None)]
    for i, bit in enumerate(bits):
        found += [(chip ^ bit, (i, slot)) for slot, (chip, _) in enumerate(found)]
    return found


def digits_at(ids, gots, where, dest, blocks):
    if where is None:
        return ids[dest]
    exchange, slot = where
    start = blocks + slot * PACK_ROWS
    return gots[exchange][dest, start : start + PACK_ROWS, :]


def terms_body(bits, *refs):
    kept, give = refs[-2:]
    ids, gots = refs[-3], refs[1 : len(bits)]
    bit, blocks = bits[-1], kept.shape[1]
    for dest in range(2 * bit):
        if not gots:
            keep, got = refs[0]
            m = (lax.axis_index("sec") // 2) ^ dest
            term = keep[m] + got[m].astype(F32)
        else:
            term = refs[0][dest] + gots[-1][dest, :blocks, :].astype(F32)
        if dest < bit:
            kept[dest] = term
        else:
            give[dest - bit, :blocks, :] = term.astype(BF16)
            for slot, (_, where) in enumerate(sources(bits[:-1])):
                start = blocks + slot * PACK_ROWS
                give[dest - bit, start : start + PACK_ROWS, :] = digits_at(ids, gots, where, dest, blocks)


def send_body(bits, away, own, order, ids, rec_packed, hyd_packed, *refs):
    gots, (runoff, ready, places) = refs[:-3], refs[-3:]
    blocks = runoff.shape[0]
    tiles = ready.shape[0] // LANES
    total = own[0] + gots[-1][0, :blocks, :].astype(F32)
    for chip, where in sources(bits):
        places[chip] = digits_at(ids, gots, where, 0, blocks)
    runoff[...] = total
    at = order[...]
    turned = lookup(total, at >> 7, at & (LANES - 1)).T
    for t in range(tiles):
        rows = pl.ds(t * LANES, LANES)
        col = away * tiles + t
        ready[rows, :] = (
            rec_packed[rows, :].astype(F32) + turned[:, col : col + 1] * hyd_packed[rows, :].astype(F32)
        ).astype(BF16)


def record_body(aways, runoff, records, hydro, order, kept, *ready):
    turned = runoff[...].T
    for t in range(runoff.shape[0]):
        rows = pl.ds(t * LANES, LANES)
        kept[rows, :] = (
            shift_time(records[rows, :].astype(F32)) + turned[:, t : t + 1] * hydro[rows, :].astype(F32)
        ).astype(BF16)
    for away, out in zip(aways, ready):
        hot = picked(order, away, out.shape[0] // LANES, kept.shape[0])
        out[...] = jnp.dot(hot, kept[...], preferred_element_type=F32).astype(BF16)


def rest_body(order, kept, landed, out, own, sem):
    copy = pltpu.make_async_copy(kept, out, sem)
    copy.start()
    hot = picked(order, 0, own.shape[0] // LANES, kept.shape[0])
    own[...] = jnp.dot(hot, kept[...], preferred_element_type=F32).astype(BF16)
    copy.wait()


def hot_of(digits, tiles, basins, other):
    core = parity("sec")
    base = ((1 - core) if other else core) * basins
    slot = lax.broadcasted_iota(I32, (basins, LANES), 0) + base
    slot = slot.astype(F32)
    place = digits[:tiles] * 256.0 + digits[tiles : 2 * tiles]
    parts = [jnp.where(slot == place[t : t + 1, :], 1.0, 0.0).astype(BF16) for t in range(tiles)]
    return parts[0] if len(parts) == 1 else jnp.concatenate(parts, axis=1)


def summed(digits, blocks, basins, other):
    tiles = blocks[0].shape[0] // LANES
    total = None
    for digit, block in zip(digits, blocks):
        hot = hot_of(digit, tiles, basins, other)
        part = jnp.dot(hot, block[...], preferred_element_type=F32)
        total = part if total is None else total + part
    return total


def early_body(aways, places, *refs):
    blocks, (theirs, mine) = refs[:-2], refs[-2:]
    digits = [places[away].astype(F32) for away in aways]
    basins = mine.shape[0]
    theirs[...] = summed(digits, blocks, basins, True)
    mine[...] = summed(digits, blocks, basins, False)


def late_body(aways, other, so_far, places, *refs):
    blocks, out = refs[:-1], refs[-1]
    digits = [places[away].astype(F32) for away in aways]
    out[...] = (so_far[...] + summed(digits, blocks, out.shape[0], other)).astype(out.dtype)


def final_body(mine, passed, out, held, sems):
    rows = mine.shape[0]
    parts = 2
    size = rows // parts
    copies = []
    for i in range(parts):
        at = pl.ds(i * size, size)
        held[at, :] = mine[at, :] + passed[at, :].astype(F32)
        copy = pltpu.make_async_copy(held.at[at, :], out.at[at, :], sems.at[i])
        copy.start()
        copies.append(copy)
    for copy in copies:
        copy.wait()


def per_device(
    moisture, heat, moist_cond, heat_cond, rain, surface_flux, cell_reach,
    records, unit_hydro, down_basin, basin_home, send_index, send_count,
):
    lons = lax.axis_size("lon")
    sections = lax.axis_size("sec")
    layers, lats, cols = moisture.shape
    reaches, steps = records.shape[1:]
    cap = send_index.shape[3]
    pairs = sections // 2
    basins = basin_home.shape[1] // sections
    blocks = reaches // LANES
    shape = jax.ShapeDtypeStruct
    dma = pltpu.SemaphoreType.DMA

    home = basin_home.reshape(-1, LANES)
    down = down_basin.reshape(-1, LANES)
    listed = send_index.reshape(sections, cap)
    fetched = [
        moisture, heat, moist_cond, heat_cond, rain, surface_flux, cell_reach, home, down, listed
    ]
    *fetched, sec_near, sec_far, lon_near, lon_far = call(
        edges_body,
        [shape(x.shape, x.dtype) for x in fetched]
        + [
            shape((2 * layers, cols), BF16),
            shape((2 * layers, cols), BF16),
            shape((lats, LANES), BF16),
            shape((lats, LANES), BF16),
        ],
        *fetched,
        ins=[HBM] * len(fetched),
        scratch=[dma((len(fetched),))],
        moved=moisture.size * 8,
    )
    *land, home_v, down_v, listed_v = fetched
    swap = lambda count: [(i, i ^ 1) for i in range(count)]
    between = lambda count: [(i, i + 1) for i in range(1, count - 1, 2)] + [
        (i + 1, i) for i in range(1, count - 1, 2)
    ]
    got_sec_far = lax.ppermute(sec_far, "sec", between(sections))
    got_sec_near = lax.ppermute(sec_near, "sec", swap(sections))
    got_lon_far = lax.ppermute(lon_far, "lon", between(lons))
    got_lon_near = lax.ppermute(lon_near, "lon", swap(lons))

    moist_out, heat_out, keep, give = call(
        land_body,
        [
            shape(moisture.shape, F32),
            shape(heat.shape, F32),
            shape((pairs, blocks, LANES), F32),
            shape((pairs, blocks, LANES), BF16),
        ],
        *land,
        got_sec_near, got_sec_far, got_lon_near, got_lon_far,
        moved=moisture.size * 24,
    )
    got = lax.ppermute(give, "sec", swap(sections))
    order, ids = call(
        index_body,
        [shape((blocks, LANES), I32), shape((pairs, PACK_ROWS, LANES), BF16)],
        listed_v, home_v, down_v, send_count,
        ins=[VMEM] * 3 + [HBM],
        scratch=[pltpu.SMEM(send_count.shape, I32), dma((1,))],
        moved=moisture.size * 8,
    )
    aways = []
    for k in range(1, pairs // 2 + 1):
        aways += [k] if 2 * k == pairs else [pairs - k, k]
    forward = lambda block, away: lax.ppermute(
        block, "sec", [(i, i ^ (2 * away)) for i in range(sections)]
    )
    pack_first = lambda rows, shifted: call(
        lambda *refs: first_body(aways[0], shifted, *refs),
        [shape((cap, steps), BF16)],
        order, rows,
        mib=12,
        flops=2 * cap * reaches * steps,
        moved=reaches * steps * 2,
    )[0]
    rec_packed = pack_first(records[0], True)
    bits = [pairs >> i for i in range(1, pairs.bit_length())]
    gots, held = [], None
    for i, bit in enumerate(bits):
        first = [keep, got] if i == 0 else [held, rec_packed]
        body = lambda *refs, i=i, part=bits[: i + 1]: terms_body(
            part, refs[:2] if i == 0 else refs[0], *refs[2:]
        )
        held, give = call(
            body,
            [
                shape((bit, blocks, LANES), F32),
                shape((bit, blocks + 2**i * PACK_ROWS, LANES), BF16),
            ],
            *first, *gots, ids,
            moved=reaches * 8,
        )
        gots.append(forward(give, bit))
    hyd_packed = pack_first(unit_hydro[0], False)
    runoff, ready, places = call(
        lambda *refs: send_body(bits, aways[0], *refs),
        [shape((blocks, LANES), F32), shape((cap, steps), BF16), shape(ids.shape, BF16)],
        held, order, ids, rec_packed, hyd_packed, *gots,
        moved=cap * steps * 6,
    )
    arrived = {aways[0]: forward(ready, aways[0])}
    kept, *ready = call(
        lambda *refs: record_body(aways[1:], *refs),
        [shape((reaches, steps), BF16)] + [shape((cap, steps), BF16)] * (len(aways) - 1),
        runoff, records[0], unit_hydro[0], order,
        mib=16,
        flops=2 * cap * reaches * steps,
        moved=reaches * steps * 8,
    )
    for away, block in zip(aways[1:], ready):
        arrived[away] = forward(block, away)
    record_new, own = call(
        rest_body,
        [shape((reaches, steps), BF16), shape((cap, steps), BF16)],
        order, kept, arrived[aways[0]],
        out_specs=[HBM, VMEM],
        scratch=[dma(())],
        mib=16,
        flops=2 * cap * reaches * steps,
        moved=reaches * steps * 4,
    )
    late = aways[-1:]
    early = [0] + aways[:-1]
    arrived[0] = own
    theirs, mine = call(
        lambda *refs: early_body(early, *refs),
        [shape((basins, steps), F32), shape((basins, steps), F32)],
        places, *[arrived[a] for a in early],
        mib=12,
        moved=basins * steps * 16,
    )
    (theirs,) = call(
        lambda *refs: late_body(late, True, *refs),
        [shape((basins, steps), BF16)],
        theirs, places, *[arrived[a] for a in late],
        moved=basins * steps * 8,
    )
    passed = lax.ppermute(theirs, "sec", swap(sections))
    (mine,) = call(
        lambda *refs: late_body(late, False, *refs),
        [shape((basins, steps), F32)],
        mine, places, *[arrived[a] for a in late],
        moved=basins * steps * 8,
    )
    (inflow,) = call(
        final_body,
        [shape((basins, steps), F32)],
        mine, passed,
        out_specs=[HBM],
        scratch=[pltpu.VMEM((basins, steps), F32), dma((2,))],
        moved=basins * steps * 10,
    )
    return (moist_out, heat_out, record_new[None], inflow[None])


def solution(mesh):
    placed = (
        P(None, "sec", "lon"),
        P(None, "sec", "lon"),
        P(None, "sec", "lon"),
        P(None, "sec", "lon"),
        P("sec", "lon"),
        P("sec", "lon"),
        P("sec", "lon"),
        P("lon", "sec", None),
        P("lon", "sec", None),
        P("lon", "sec"),
        P("lon", None),
        P("lon", "sec", None, None),
        P("lon", "sec", None),
    )
    return jax.shard_map(
        per_device,
        mesh=mesh,
        in_specs=placed,
        out_specs=(
            P(None, "sec", "lon"),
            P(None, "sec", "lon"),
            P("lon", "sec", None),
            P("lon", "sec", None),
        ),
        check_vma=False,
    )
```

```python
import jax
import jax.numpy as jnp
from jax import lax
from jax.experimental import pallas as pl
from jax.experimental.pallas import tpu as pltpu
from jax.sharding import PartitionSpec as P

LATERAL = 0.2
LANES = 128
PACK_ROWS = 16
F32 = jnp.float32
BF16 = jnp.bfloat16
I32 = jnp.int32
VMEM = pl.BlockSpec(memory_space=pltpu.VMEM)
HBM = pl.BlockSpec(memory_space=pltpu.HBM)


def call(body, outs, *args, ins=None, out_specs=None, scratch=(), mib=8, flops=0, moved=0):
    ins = list(ins) if ins else [VMEM] * len(args)
    args = [
        pltpu.with_memory_space_constraint(arg, pltpu.HBM) if spec is HBM else arg
        for arg, spec in zip(args, ins)
    ]
    return pl.pallas_call(
        body,
        out_shape=list(outs),
        in_specs=ins,
        out_specs=list(out_specs) if out_specs else [VMEM] * len(outs),
        scratch_shapes=list(scratch),
        compiler_params=pltpu.CompilerParams(vmem_limit_bytes=mib * 1024 * 1024),
        cost_estimate=pl.CostEstimate(flops=flops, bytes_accessed=moved, transcendentals=0),
    )(*args)


def fetch(sources, targets, sems):
    copies = [
        pltpu.make_async_copy(src, dst, sems.at[i])
        for i, (src, dst) in enumerate(zip(sources, targets))
    ]
    for copy in copies:
        copy.start()
    return copies


def parity(axis):
    return lax.rem(lax.axis_index(axis), 2)


def edges_body(*refs):
    count = 10
    targets = refs[count : 2 * count]
    moist, heat = targets[:2]
    sec_near, sec_far, lon_near, lon_far, sems = refs[2 * count :]
    copies = fetch(refs[:count], targets, sems)
    layers, rows, cols = moist.shape
    lane = lax.broadcasted_iota(I32, (rows, LANES), 1)
    west = jnp.zeros((rows, LANES), F32)
    east = jnp.zeros((rows, LANES), F32)
    sec_even = parity("sec") == 0
    for f, ref in enumerate((moist, heat)):
        copies[f].wait()
        north = ref[:, 0, :]
        south = ref[:, rows - 1, :]
        sec_near[f * layers : (f + 1) * layers, :] = jnp.where(sec_even, south, north).astype(BF16)
        sec_far[f * layers : (f + 1) * layers, :] = jnp.where(sec_even, north, south).astype(BF16)
        for layer in range(layers):
            k = f * layers + layer
            west = jnp.where(lane == k, ref[layer, :, 0:1], west)
            east = jnp.where(lane == k, ref[layer, :, cols - 1 : cols], east)
    lon_even = parity("lon") == 0
    lon_near[...] = jnp.where(lon_even, east, west).astype(BF16)
    lon_far[...] = jnp.where(lon_even, west, east).astype(BF16)
    for copy in copies[2:]:
        copy.wait()


def lookup(table, hi, lo):
    out = jnp.zeros(hi.shape, table.dtype)
    for row in range(table.shape[0]):
        line = jnp.broadcast_to(table[row : row + 1, :], hi.shape)
        got = jnp.take_along_axis(line, lo, axis=1)
        out = jnp.where(hi == row, got, out)
    return out


def index_body(listed, home, down, count_in, order, ids, count, sems):
    copies = fetch((count_in,), (count,), sems)
    slot = lookup(home[...], down[...] >> 7, down[...] & (LANES - 1))
    pairs, width = listed.shape[0] // 2, listed.shape[1]
    tiles = width // LANES
    chip = lax.axis_index("sec") // 2
    chip_basins = home.shape[0] * LANES // pairs
    pos = lax.broadcasted_iota(I32, (1, width), 1)
    copies[0].wait()
    for m in range(pairs):
        c = count[0, 0, 2 * m]
        second = pltpu.roll(listed[2 * m + 1 : 2 * m + 2, :], lax.rem(c, width), 1)
        line = jnp.where(pos < c, listed[2 * m : 2 * m + 1, :], second)
        away = m ^ chip
        for t in range(tiles):
            order[pl.ds(away * tiles + t, 1), :] = line[:, t * LANES : (t + 1) * LANES]
    at = order[...]
    place = lookup(slot, at >> 7, at & (LANES - 1))
    pad = jnp.zeros((PACK_ROWS - 2 * tiles, LANES), F32)
    for away in range(pairs):
        m = away ^ chip
        mine = place[away * tiles : (away + 1) * tiles, :] - m * chip_basins
        ids[away] = jnp.concatenate(
            [(mine >> 8).astype(F32), (mine & 255).astype(F32), pad], axis=0
        ).astype(BF16)


def shift_time(x):
    steps = x.shape[1]
    lane = lax.broadcasted_iota(I32, x.shape, 1)
    return jnp.where(lane == steps - 1, 0.0, pltpu.roll(x, steps - 1, 1))


def picked(order, away, tiles, reaches):
    turned = order[...].astype(F32).T
    lane = lax.broadcasted_iota(I32, (LANES, reaches), 1).astype(F32)
    parts = [
        jnp.where(lane == turned[:, t : t + 1], 1.0, 0.0).astype(BF16)
        for t in range(away * tiles, (away + 1) * tiles)
    ]
    return parts[0] if len(parts) == 1 else jnp.concatenate(parts, axis=0)


def first_body(away, order, records, hydro, rec_packed, hyd_packed):
    hot = picked(order, away, rec_packed.shape[0] // LANES, records.shape[0])
    rec = jnp.dot(hot, records[...], preferred_element_type=F32)
    rec_packed[...] = shift_time(rec).astype(BF16)
    hyd_packed[...] = jnp.dot(hot, hydro[...], preferred_element_type=F32).astype(BF16)


def land_body(
    moist, heat, moist_k, heat_k, rain, flux, cell, sec_near, sec_far, lon_near, lon_far,
    moist_out, heat_out, keep, give,
):
    layers, rows, cols = moist.shape
    row = lax.broadcasted_iota(I32, (rows, cols), 0)
    col = lax.broadcasted_iota(I32, (rows, cols), 1)
    sec_even = parity("sec") == 0
    lon_even = parity("lon") == 0
    south_all = jnp.where(sec_even, sec_near[...].astype(F32), sec_far[...].astype(F32))
    north_all = jnp.where(sec_even, sec_far[...].astype(F32), sec_near[...].astype(F32))
    lon = lax.axis_index("lon")
    outer = (lon == 0) | (lon == lax.axis_size("lon") - 1)
    lon_beyond = jnp.where(outer, 0.0, lon_far[...].astype(F32))
    east_all = jnp.where(lon_even, lon_near[...].astype(F32), lon_beyond)
    west_all = jnp.where(lon_even, lon_beyond, lon_near[...].astype(F32))
    for f, (x_ref, k_ref, top, out) in enumerate(
        ((moist, moist_k, rain, moist_out), (heat, heat_k, flux, heat_out))
    ):
        ratio = jnp.zeros((rows, cols), F32)
        value = jnp.zeros((rows, cols), F32)
        below = jnp.zeros((rows, cols), F32)
        ratios, values = [], []
        for layer in range(layers):
            k = f * layers + layer
            x = x_ref[layer]
            up = jnp.where(row == 0, north_all[k : k + 1, :], pltpu.roll(x, 1, 0))
            dn = jnp.where(row == rows - 1, south_all[k : k + 1, :], pltpu.roll(x, rows - 1, 0))
            lf = jnp.where(col == 0, west_all[:, k : k + 1], pltpu.roll(x, 1, 1))
            rt = jnp.where(col == cols - 1, east_all[:, k : k + 1], pltpu.roll(x, cols - 1, 1))
            rhs = x + LATERAL * (up + dn + lf + rt - 4.0 * x)
            if layer == 0:
                rhs = rhs + top[...]
            if layer < layers - 1:
                above = 0.5 * (k_ref[layer] + k_ref[layer + 1])
            else:
                above = jnp.zeros((rows, cols), F32)
            inv = 1.0 / (1.0 + below + above + below * ratio)
            ratio = -above * inv
            value = (rhs + below * value) * inv
            ratios.append(ratio)
            values.append(value)
            below = above
        x = values[-1]
        out[layers - 1] = x
        for layer in range(layers - 2, -1, -1):
            x = values[layer] - ratios[layer] * x
            out[layer] = x
    s = moist_out[0] - 1.0
    soft = jnp.maximum(s, 0.0) + jnp.log1p(jnp.exp(-jnp.abs(s)))
    gate = 1.0 / (1.0 + jnp.exp(-heat_out[0]))
    runoff = soft * gate + 0.5 * moist_k[layers - 1] * moist_out[layers - 1]
    cells = cell[...]
    hi = cells >> 7
    lo = cells & (LANES - 1)
    pairs, blocks = keep.shape[:2]
    his = 2 * pairs * blocks
    hi_iota = lax.broadcasted_iota(I32, (his, cols), 0)
    lo_iota = lax.broadcasted_iota(I32, (LANES, cols), 0)
    acc = jnp.zeros((his, LANES), F32)
    for i in range(rows):
        a = jnp.where(hi_iota == hi[i : i + 1, :], runoff[i : i + 1, :], 0.0).astype(BF16)
        b = jnp.where(lo_iota == lo[i : i + 1, :], 1.0, 0.0).astype(BF16)
        acc = acc + lax.dot_general(a, b, (((1,), (1,)), ((), ())), preferred_element_type=F32)
    both = acc.reshape(pairs, 2, blocks, LANES)
    keep[...] = jnp.where(sec_even, both[:, 0], both[:, 1])
    give[...] = jnp.where(sec_even, both[:, 1], both[:, 0]).astype(BF16)


def terms_body(keep, got, ids, own, *outs):
    pairs, blocks = keep.shape[:2]
    chip = lax.axis_index("sec") // 2
    own[...] = keep[chip] + got[chip].astype(F32)
    for flip, out in zip(range(len(outs), 0, -1), outs):
        m = chip ^ flip
        out[:blocks, :] = (keep[m] + got[m].astype(F32)).astype(BF16)
        out[blocks:, :] = ids[flip]


def send_body(away, own, order, ids, rec_packed, hyd_packed, *refs):
    terms, (runoff, ready, places) = refs[:-3], refs[-3:]
    places[0] = ids[0]
    for flip, term in zip(range(len(terms), 0, -1), terms):
        places[flip] = term[term.shape[0] - PACK_ROWS :, :]
    blocks = runoff.shape[0]
    tiles = ready.shape[0] // LANES
    total = own[...]
    for term in terms:
        total = total + term[:blocks, :].astype(F32)
    runoff[...] = total
    at = order[...]
    turned = lookup(total, at >> 7, at & (LANES - 1)).T
    for t in range(tiles):
        rows = pl.ds(t * LANES, LANES)
        col = away * tiles + t
        ready[rows, :] = (
            rec_packed[rows, :].astype(F32) + turned[:, col : col + 1] * hyd_packed[rows, :].astype(F32)
        ).astype(BF16)


def record_body(aways, runoff, records, hydro, order, kept, *ready):
    turned = runoff[...].T
    for t in range(runoff.shape[0]):
        rows = pl.ds(t * LANES, LANES)
        kept[rows, :] = (
            shift_time(records[rows, :].astype(F32)) + turned[:, t : t + 1] * hydro[rows, :].astype(F32)
        ).astype(BF16)
    for away, out in zip(aways, ready):
        hot = picked(order, away, out.shape[0] // LANES, kept.shape[0])
        out[...] = jnp.dot(hot, kept[...], preferred_element_type=F32).astype(BF16)


def hot_of(digits, tiles, basins, other):
    core = parity("sec")
    base = ((1 - core) if other else core) * basins
    slot = lax.broadcasted_iota(I32, (basins, LANES), 0) + base
    slot = slot.astype(F32)
    place = digits[:tiles] * 256.0 + digits[tiles : 2 * tiles]
    parts = [jnp.where(slot == place[t : t + 1, :], 1.0, 0.0).astype(BF16) for t in range(tiles)]
    return parts[0] if len(parts) == 1 else jnp.concatenate(parts, axis=1)


def summed(digits, blocks, basins, other):
    tiles = blocks[0].shape[0] // LANES
    total = None
    for digit, block in zip(digits, blocks):
        hot = hot_of(digit, tiles, basins, other)
        part = jnp.dot(hot, block[...], preferred_element_type=F32)
        total = part if total is None else total + part
    return total


def rest_body(near, order, kept, places, landed, out, theirs, mine, own, sem):
    copy = pltpu.make_async_copy(kept, out, sem)
    copy.start()
    hot = picked(order, 0, own.shape[0] // LANES, kept.shape[0])
    own[...] = jnp.dot(hot, kept[...], preferred_element_type=F32).astype(BF16)
    digits = [places[away].astype(F32) for away in (0, near)]
    basins = mine.shape[0]
    theirs[...] = summed(digits, [own, landed], basins, True)
    mine[...] = summed(digits, [own, landed], basins, False)
    copy.wait()


def early_body(aways, theirs_so_far, mine_so_far, places, *refs):
    blocks, (theirs, mine) = refs[:-2], refs[-2:]
    digits = [places[away].astype(F32) for away in aways]
    basins = mine.shape[0]
    theirs[...] = theirs_so_far[...] + summed(digits, blocks, basins, True)
    mine[...] = mine_so_far[...] + summed(digits, blocks, basins, False)


def late_body(aways, other, so_far, places, *refs):
    blocks, out = refs[:-1], refs[-1]
    digits = [places[away].astype(F32) for away in aways]
    out[...] = (so_far[...] + summed(digits, blocks, out.shape[0], other)).astype(out.dtype)


def final_body(mine, passed, out, held, sems):
    rows = mine.shape[0]
    parts = 2
    size = rows // parts
    copies = []
    for i in range(parts):
        at = pl.ds(i * size, size)
        held[at, :] = mine[at, :] + passed[at, :].astype(F32)
        copy = pltpu.make_async_copy(held.at[at, :], out.at[at, :], sems.at[i])
        copy.start()
        copies.append(copy)
    for copy in copies:
        copy.wait()


def per_device(
    moisture, heat, moist_cond, heat_cond, rain, surface_flux, cell_reach,
    records, unit_hydro, down_basin, basin_home, send_index, send_count,
):
    lons = lax.axis_size("lon")
    sections = lax.axis_size("sec")
    layers, lats, cols = moisture.shape
    reaches, steps = records.shape[1:]
    cap = send_index.shape[3]
    pairs = sections // 2
    basins = basin_home.shape[1] // sections
    blocks = reaches // LANES
    shape = jax.ShapeDtypeStruct
    dma = pltpu.SemaphoreType.DMA

    home = basin_home.reshape(-1, LANES)
    down = down_basin.reshape(-1, LANES)
    listed = send_index.reshape(sections, cap)
    fetched = [
        moisture, heat, moist_cond, heat_cond, rain, surface_flux, cell_reach, home, down, listed
    ]
    *fetched, sec_near, sec_far, lon_near, lon_far = call(
        edges_body,
        [shape(x.shape, x.dtype) for x in fetched]
        + [
            shape((2 * layers, cols), BF16),
            shape((2 * layers, cols), BF16),
            shape((lats, LANES), BF16),
            shape((lats, LANES), BF16),
        ],
        *fetched,
        ins=[HBM] * len(fetched),
        scratch=[dma((len(fetched),))],
        moved=moisture.size * 8,
    )
    *land, home_v, down_v, listed_v = fetched
    swap = lambda count: [(i, i ^ 1) for i in range(count)]
    between = lambda count: [(i, i + 1) for i in range(1, count - 1, 2)] + [
        (i + 1, i) for i in range(1, count - 1, 2)
    ]
    got_sec_far = lax.ppermute(sec_far, "sec", between(sections))
    got_sec_near = lax.ppermute(sec_near, "sec", swap(sections))
    got_lon_far = lax.ppermute(
        lon_far, "lon", [(i, (i - 1 + 2 * (i % 2)) % lons) for i in range(lons)]
    )
    got_lon_near = lax.ppermute(lon_near, "lon", swap(lons))

    moist_out, heat_out, keep, give = call(
        land_body,
        [
            shape(moisture.shape, F32),
            shape(heat.shape, F32),
            shape((pairs, blocks, LANES), F32),
            shape((pairs, blocks, LANES), BF16),
        ],
        *land,
        got_sec_near, got_sec_far, got_lon_near, got_lon_far,
        moved=moisture.size * 24,
    )
    got = lax.ppermute(give, "sec", swap(sections))
    order, ids = call(
        index_body,
        [shape((blocks, LANES), I32), shape((pairs, PACK_ROWS, LANES), BF16)],
        listed_v, home_v, down_v, send_count,
        ins=[VMEM] * 3 + [HBM],
        scratch=[pltpu.SMEM(send_count.shape, I32), dma((1,))],
        moved=moisture.size * 8,
    )
    aways = []
    for k in range(1, pairs // 2 + 1):
        aways += [k] if 2 * k == pairs else [pairs - k, k]
    own_terms, *terms = call(
        terms_body,
        [shape((blocks, LANES), F32)] + [shape((blocks + PACK_ROWS, LANES), BF16)] * (pairs - 1),
        keep, got, ids,
        moved=reaches * 8,
    )
    forward = lambda block, away: lax.ppermute(
        block, "sec", [(i, i ^ (2 * away)) for i in range(sections)]
    )
    terms = [forward(term, flip) for flip, term in zip(range(pairs - 1, 0, -1), terms)]
    rec_packed, hyd_packed = call(
        lambda *refs: first_body(aways[0], *refs),
        [shape((cap, steps), BF16)] * 2,
        order, records[0], unit_hydro[0],
        mib=12,
        flops=4 * cap * reaches * steps,
        moved=reaches * steps * 4,
    )
    runoff, ready, places = call(
        lambda *refs: send_body(aways[0], *refs),
        [shape((blocks, LANES), F32), shape((cap, steps), BF16), shape(ids.shape, BF16)],
        own_terms, order, ids, rec_packed, hyd_packed, *terms,
        moved=cap * steps * 6,
    )
    arrived = {aways[0]: forward(ready, aways[0])}
    kept, *ready = call(
        lambda *refs: record_body(aways[1:], *refs),
        [shape((reaches, steps), BF16)] + [shape((cap, steps), BF16)] * (len(aways) - 1),
        runoff, records[0], unit_hydro[0], order,
        mib=16,
        flops=2 * cap * reaches * steps,
        moved=reaches * steps * 8,
    )
    for away, block in zip(aways[1:], ready):
        arrived[away] = forward(block, away)
    near, late = aways[0], aways[-1:]
    record_new, theirs, mine = call(
        lambda *refs: rest_body(near, *refs),
        [shape((reaches, steps), BF16), shape((basins, steps), F32), shape((basins, steps), F32)],
        order, kept, places, arrived[near],
        out_specs=[HBM, VMEM, VMEM],
        scratch=[pltpu.VMEM((cap, steps), BF16), dma(())],
        mib=16,
        flops=2 * cap * reaches * steps,
        moved=reaches * steps * 4,
    )
    early = [a for a in aways[:-1] if a != near]
    theirs, mine = call(
        lambda *refs: early_body(early, *refs),
        [shape((basins, steps), F32), shape((basins, steps), F32)],
        theirs, mine, places, *[arrived[a] for a in early],
        mib=12,
        moved=basins * steps * 16,
    )
    (theirs,) = call(
        lambda *refs: late_body(late, True, *refs),
        [shape((basins, steps), BF16)],
        theirs, places, *[arrived[a] for a in late],
        moved=basins * steps * 8,
    )
    passed = lax.ppermute(theirs, "sec", swap(sections))
    (mine,) = call(
        lambda *refs: late_body(late, False, *refs),
        [shape((basins, steps), F32)],
        mine, places, *[arrived[a] for a in late],
        moved=basins * steps * 8,
    )
    (inflow,) = call(
        final_body,
        [shape((basins, steps), F32)],
        mine, passed,
        out_specs=[HBM],
        scratch=[pltpu.VMEM((basins, steps), F32), dma((2,))],
        moved=basins * steps * 10,
    )
    return (moist_out, heat_out, record_new[None], inflow[None])


def solution(mesh):
    placed = (
        P(None, "sec", "lon"),
        P(None, "sec", "lon"),
        P(None, "sec", "lon"),
        P(None, "sec", "lon"),
        P("sec", "lon"),
        P("sec", "lon"),
        P("sec", "lon"),
        P("lon", "sec", None),
        P("lon", "sec", None),
        P("lon", "sec"),
        P("lon", None),
        P("lon", "sec", None, None),
        P("lon", "sec", None),
    )
    return jax.shard_map(
        per_device,
        mesh=mesh,
        in_specs=placed,
        out_specs=(
            P(None, "sec", "lon"),
            P(None, "sec", "lon"),
            P("lon", "sec", None),
            P("lon", "sec", None),
        ),
        check_vma=False,
    )
```

```python
import jax
import jax.numpy as jnp
from jax import lax
from jax.experimental import pallas as pl
from jax.experimental.pallas import tpu as pltpu
from jax.sharding import PartitionSpec as P

LATERAL = 0.2
LANES = 128
PACK_ROWS = 16
F32 = jnp.float32
BF16 = jnp.bfloat16
I32 = jnp.int32
VMEM = pl.BlockSpec(memory_space=pltpu.VMEM)
HBM = pl.BlockSpec(memory_space=pltpu.HBM)


def call(body, outs, *args, ins=None, out_specs=None, scratch=(), mib=8, flops=0, moved=0):
    ins = list(ins) if ins else [VMEM] * len(args)
    args = [
        pltpu.with_memory_space_constraint(arg, pltpu.HBM) if spec is HBM else arg
        for arg, spec in zip(args, ins)
    ]
    return pl.pallas_call(
        body,
        out_shape=list(outs),
        in_specs=ins,
        out_specs=list(out_specs) if out_specs else [VMEM] * len(outs),
        scratch_shapes=list(scratch),
        compiler_params=pltpu.CompilerParams(vmem_limit_bytes=mib * 1024 * 1024),
        cost_estimate=pl.CostEstimate(flops=flops, bytes_accessed=moved, transcendentals=0),
    )(*args)


def fetch(sources, targets, sems):
    copies = [
        pltpu.make_async_copy(src, dst, sems.at[i])
        for i, (src, dst) in enumerate(zip(sources, targets))
    ]
    for copy in copies:
        copy.start()
    return copies


def parity(axis):
    return lax.rem(lax.axis_index(axis), 2)


def edges_body(*refs):
    count = 10
    targets = refs[count : 2 * count]
    moist, heat = targets[:2]
    sec_near, sec_far, lon_near, lon_far, sems = refs[2 * count :]
    copies = fetch(refs[:count], targets, sems)
    layers, rows, cols = moist.shape
    lane = lax.broadcasted_iota(I32, (rows, LANES), 1)
    west = jnp.zeros((rows, LANES), F32)
    east = jnp.zeros((rows, LANES), F32)
    sec_even = parity("sec") == 0
    for f, ref in enumerate((moist, heat)):
        copies[f].wait()
        north = ref[:, 0, :]
        south = ref[:, rows - 1, :]
        sec_near[f * layers : (f + 1) * layers, :] = jnp.where(sec_even, south, north).astype(BF16)
        sec_far[f * layers : (f + 1) * layers, :] = jnp.where(sec_even, north, south).astype(BF16)
        for layer in range(layers):
            k = f * layers + layer
            west = jnp.where(lane == k, ref[layer, :, 0:1], west)
            east = jnp.where(lane == k, ref[layer, :, cols - 1 : cols], east)
    lon_even = parity("lon") == 0
    lon_near[...] = jnp.where(lon_even, east, west).astype(BF16)
    lon_far[...] = jnp.where(lon_even, west, east).astype(BF16)
    for copy in copies[2:]:
        copy.wait()


def lookup(table, hi, lo):
    out = jnp.zeros(hi.shape, table.dtype)
    for row in range(table.shape[0]):
        line = jnp.broadcast_to(table[row : row + 1, :], hi.shape)
        got = jnp.take_along_axis(line, lo, axis=1)
        out = jnp.where(hi == row, got, out)
    return out


def index_body(listed, home, down, count_in, order, ids, count, sems):
    copies = fetch((count_in,), (count,), sems)
    slot = lookup(home[...], down[...] >> 7, down[...] & (LANES - 1))
    pairs, width = listed.shape[0] // 2, listed.shape[1]
    tiles = width // LANES
    chip = lax.axis_index("sec") // 2
    chip_basins = home.shape[0] * LANES // pairs
    pos = lax.broadcasted_iota(I32, (1, width), 1)
    copies[0].wait()
    for m in range(pairs):
        c = count[0, 0, 2 * m]
        second = pltpu.roll(listed[2 * m + 1 : 2 * m + 2, :], lax.rem(c, width), 1)
        line = jnp.where(pos < c, listed[2 * m : 2 * m + 1, :], second)
        away = m ^ chip
        for t in range(tiles):
            order[pl.ds(away * tiles + t, 1), :] = line[:, t * LANES : (t + 1) * LANES]
    at = order[...]
    place = lookup(slot, at >> 7, at & (LANES - 1))
    pad = jnp.zeros((PACK_ROWS - 2 * tiles, LANES), F32)
    for away in range(pairs):
        m = away ^ chip
        mine = place[away * tiles : (away + 1) * tiles, :] - m * chip_basins
        ids[away] = jnp.concatenate(
            [(mine >> 8).astype(F32), (mine & 255).astype(F32), pad], axis=0
        ).astype(BF16)


def shift_time(x):
    steps = x.shape[1]
    lane = lax.broadcasted_iota(I32, x.shape, 1)
    return jnp.where(lane == steps - 1, 0.0, pltpu.roll(x, steps - 1, 1))


def picked(order, away, tiles, reaches):
    turned = order[...].astype(F32).T
    lane = lax.broadcasted_iota(I32, (LANES, reaches), 1).astype(F32)
    parts = [
        jnp.where(lane == turned[:, t : t + 1], 1.0, 0.0).astype(BF16)
        for t in range(away * tiles, (away + 1) * tiles)
    ]
    return parts[0] if len(parts) == 1 else jnp.concatenate(parts, axis=0)


def first_body(away, order, records, hydro, rec_packed, hyd_packed):
    hot = picked(order, away, rec_packed.shape[0] // LANES, records.shape[0])
    rec = jnp.dot(hot, records[...], preferred_element_type=F32)
    rec_packed[...] = shift_time(rec).astype(BF16)
    hyd_packed[...] = jnp.dot(hot, hydro[...], preferred_element_type=F32).astype(BF16)


def land_body(
    moist, heat, moist_k, heat_k, rain, flux, cell, sec_near, sec_far, lon_near, lon_far,
    moist_out, heat_out, keep, give,
):
    layers, rows, cols = moist.shape
    row = lax.broadcasted_iota(I32, (rows, cols), 0)
    col = lax.broadcasted_iota(I32, (rows, cols), 1)
    sec_even = parity("sec") == 0
    lon_even = parity("lon") == 0
    outer = lambda axis: (lax.axis_index(axis) == 0) | (
        lax.axis_index(axis) == lax.axis_size(axis) - 1
    )
    sec_beyond = jnp.where(outer("sec"), 0.0, sec_far[...].astype(F32))
    lon_beyond = jnp.where(outer("lon"), 0.0, lon_far[...].astype(F32))
    south_all = jnp.where(sec_even, sec_near[...].astype(F32), sec_beyond)
    north_all = jnp.where(sec_even, sec_beyond, sec_near[...].astype(F32))
    east_all = jnp.where(lon_even, lon_near[...].astype(F32), lon_beyond)
    west_all = jnp.where(lon_even, lon_beyond, lon_near[...].astype(F32))
    for f, (x_ref, k_ref, top, out) in enumerate(
        ((moist, moist_k, rain, moist_out), (heat, heat_k, flux, heat_out))
    ):
        ratio = jnp.zeros((rows, cols), F32)
        value = jnp.zeros((rows, cols), F32)
        below = jnp.zeros((rows, cols), F32)
        ratios, values = [], []
        for layer in range(layers):
            k = f * layers + layer
            x = x_ref[layer]
            up = jnp.where(row == 0, north_all[k : k + 1, :], pltpu.roll(x, 1, 0))
            dn = jnp.where(row == rows - 1, south_all[k : k + 1, :], pltpu.roll(x, rows - 1, 0))
            lf = jnp.where(col == 0, west_all[:, k : k + 1], pltpu.roll(x, 1, 1))
            rt = jnp.where(col == cols - 1, east_all[:, k : k + 1], pltpu.roll(x, cols - 1, 1))
            rhs = x + LATERAL * (up + dn + lf + rt - 4.0 * x)
            if layer == 0:
                rhs = rhs + top[...]
            if layer < layers - 1:
                above = 0.5 * (k_ref[layer] + k_ref[layer + 1])
            else:
                above = jnp.zeros((rows, cols), F32)
            inv = 1.0 / (1.0 + below + above + below * ratio)
            ratio = -above * inv
            value = (rhs + below * value) * inv
            ratios.append(ratio)
            values.append(value)
            below = above
        x = values[-1]
        out[layers - 1] = x
        for layer in range(layers - 2, -1, -1):
            x = values[layer] - ratios[layer] * x
            out[layer] = x
    s = moist_out[0] - 1.0
    soft = jnp.maximum(s, 0.0) + jnp.log1p(jnp.exp(-jnp.abs(s)))
    gate = 1.0 / (1.0 + jnp.exp(-heat_out[0]))
    runoff = soft * gate + 0.5 * moist_k[layers - 1] * moist_out[layers - 1]
    cells = cell[...]
    hi = cells >> 7
    lo = cells & (LANES - 1)
    pairs, blocks = keep.shape[:2]
    his = 2 * pairs * blocks
    hi_iota = lax.broadcasted_iota(I32, (his, cols), 0)
    lo_iota = lax.broadcasted_iota(I32, (LANES, cols), 0)
    acc = jnp.zeros((his, LANES), F32)
    for i in range(rows):
        a = jnp.where(hi_iota == hi[i : i + 1, :], runoff[i : i + 1, :], 0.0).astype(BF16)
        b = jnp.where(lo_iota == lo[i : i + 1, :], 1.0, 0.0).astype(BF16)
        acc = acc + lax.dot_general(a, b, (((1,), (1,)), ((), ())), preferred_element_type=F32)
    both = acc.reshape(pairs, 2, blocks, LANES)
    keep[...] = jnp.where(sec_even, both[:, 0], both[:, 1])
    give[...] = jnp.where(sec_even, both[:, 1], both[:, 0]).astype(BF16)


def terms_body(keep, got, ids, own, *outs):
    pairs, blocks = keep.shape[:2]
    chip = lax.axis_index("sec") // 2
    own[...] = keep[chip] + got[chip].astype(F32)
    for flip, out in zip(range(len(outs), 0, -1), outs):
        m = chip ^ flip
        out[:blocks, :] = (keep[m] + got[m].astype(F32)).astype(BF16)
        out[blocks:, :] = ids[flip]


def send_body(away, own, order, ids, rec_packed, hyd_packed, *refs):
    terms, (runoff, ready, places) = refs[:-3], refs[-3:]
    places[0] = ids[0]
    for flip, term in zip(range(len(terms), 0, -1), terms):
        places[flip] = term[term.shape[0] - PACK_ROWS :, :]
    blocks = runoff.shape[0]
    tiles = ready.shape[0] // LANES
    total = own[...]
    for term in terms:
        total = total + term[:blocks, :].astype(F32)
    runoff[...] = total
    at = order[...]
    turned = lookup(total, at >> 7, at & (LANES - 1)).T
    for t in range(tiles):
        rows = pl.ds(t * LANES, LANES)
        col = away * tiles + t
        ready[rows, :] = (
            rec_packed[rows, :].astype(F32) + turned[:, col : col + 1] * hyd_packed[rows, :].astype(F32)
        ).astype(BF16)


def record_body(aways, runoff, records, hydro, order, places, out, theirs, mine, *refs):
    ready, (kept, own, sem) = refs[:-3], refs[-3:]
    turned = runoff[...].T
    for t in range(runoff.shape[0]):
        rows = pl.ds(t * LANES, LANES)
        kept[rows, :] = (
            shift_time(records[rows, :].astype(F32)) + turned[:, t : t + 1] * hydro[rows, :].astype(F32)
        ).astype(BF16)
    copy = pltpu.make_async_copy(kept, out, sem)
    copy.start()
    for away, block in zip(aways + [0], list(ready) + [own]):
        hot = picked(order, away, block.shape[0] // LANES, kept.shape[0])
        block[...] = jnp.dot(hot, kept[...], preferred_element_type=F32).astype(BF16)
    digits = [places[0].astype(F32)]
    theirs[...] = summed(digits, [own], mine.shape[0], True)
    mine[...] = summed(digits, [own], mine.shape[0], False)
    copy.wait()


def hot_of(digits, tiles, basins, other):
    core = parity("sec")
    base = ((1 - core) if other else core) * basins
    slot = lax.broadcasted_iota(I32, (basins, LANES), 0) + base
    slot = slot.astype(F32)
    place = digits[:tiles] * 256.0 + digits[tiles : 2 * tiles]
    parts = [jnp.where(slot == place[t : t + 1, :], 1.0, 0.0).astype(BF16) for t in range(tiles)]
    return parts[0] if len(parts) == 1 else jnp.concatenate(parts, axis=1)


def summed(digits, blocks, basins, other):
    tiles = blocks[0].shape[0] // LANES
    total = None
    for digit, block in zip(digits, blocks):
        hot = hot_of(digit, tiles, basins, other)
        part = jnp.dot(hot, block[...], preferred_element_type=F32)
        total = part if total is None else total + part
    return total


def early_body(aways, theirs_so_far, mine_so_far, places, *refs):
    blocks, (theirs, mine) = refs[:-2], refs[-2:]
    digits = [places[away].astype(F32) for away in aways]
    basins = mine.shape[0]
    theirs[...] = theirs_so_far[...] + summed(digits, blocks, basins, True)
    mine[...] = mine_so_far[...] + summed(digits, blocks, basins, False)


def late_body(aways, other, so_far, places, *refs):
    blocks, out = refs[:-1], refs[-1]
    digits = [places[away].astype(F32) for away in aways]
    out[...] = (so_far[...] + summed(digits, blocks, out.shape[0], other)).astype(out.dtype)


def final_body(mine, passed, out, held, sems):
    rows = mine.shape[0]
    parts = 2
    size = rows // parts
    copies = []
    for i in range(parts):
        at = pl.ds(i * size, size)
        held[at, :] = mine[at, :] + passed[at, :].astype(F32)
        copy = pltpu.make_async_copy(held.at[at, :], out.at[at, :], sems.at[i])
        copy.start()
        copies.append(copy)
    for copy in copies:
        copy.wait()


def per_device(
    moisture, heat, moist_cond, heat_cond, rain, surface_flux, cell_reach,
    records, unit_hydro, down_basin, basin_home, send_index, send_count,
):
    lons = lax.axis_size("lon")
    sections = lax.axis_size("sec")
    layers, lats, cols = moisture.shape
    reaches, steps = records.shape[1:]
    cap = send_index.shape[3]
    pairs = sections // 2
    basins = basin_home.shape[1] // sections
    blocks = reaches // LANES
    shape = jax.ShapeDtypeStruct
    dma = pltpu.SemaphoreType.DMA

    home = basin_home.reshape(-1, LANES)
    down = down_basin.reshape(-1, LANES)
    listed = send_index.reshape(sections, cap)
    fetched = [
        moisture, heat, moist_cond, heat_cond, rain, surface_flux, cell_reach, home, down, listed
    ]
    *fetched, sec_near, sec_far, lon_near, lon_far = call(
        edges_body,
        [shape(x.shape, x.dtype) for x in fetched]
        + [
            shape((2 * layers, cols), BF16),
            shape((2 * layers, cols), BF16),
            shape((lats, LANES), BF16),
            shape((lats, LANES), BF16),
        ],
        *fetched,
        ins=[HBM] * len(fetched),
        scratch=[dma((len(fetched),))],
        moved=moisture.size * 8,
    )
    *land, home_v, down_v, listed_v = fetched
    swap = lambda count: [(i, i ^ 1) for i in range(count)]
    between = lambda count: [
        (i, j if 0 <= j < count else i) for i, j in ((i, i - 1 + 2 * (i % 2)) for i in range(count))
    ]
    got_sec_far = lax.ppermute(sec_far, "sec", between(sections))
    got_sec_near = lax.ppermute(sec_near, "sec", swap(sections))
    got_lon_far = lax.ppermute(lon_far, "lon", between(lons))
    got_lon_near = lax.ppermute(lon_near, "lon", swap(lons))

    moist_out, heat_out, keep, give = call(
        land_body,
        [
            shape(moisture.shape, F32),
            shape(heat.shape, F32),
            shape((pairs, blocks, LANES), F32),
            shape((pairs, blocks, LANES), BF16),
        ],
        *land,
        got_sec_near, got_sec_far, got_lon_near, got_lon_far,
        moved=moisture.size * 24,
    )
    got = lax.ppermute(give, "sec", swap(sections))
    order, ids = call(
        index_body,
        [shape((blocks, LANES), I32), shape((pairs, PACK_ROWS, LANES), BF16)],
        listed_v, home_v, down_v, send_count,
        ins=[VMEM] * 3 + [HBM],
        scratch=[pltpu.SMEM(send_count.shape, I32), dma((1,))],
        moved=moisture.size * 8,
    )
    aways = []
    for k in range(1, pairs // 2 + 1):
        aways += [k] if 2 * k == pairs else [pairs - k, k]
    own_terms, *terms = call(
        terms_body,
        [shape((blocks, LANES), F32)] + [shape((blocks + PACK_ROWS, LANES), BF16)] * (pairs - 1),
        keep, got, ids,
        moved=reaches * 8,
    )
    forward = lambda block, away: lax.ppermute(
        block, "sec", [(i, i ^ (2 * away)) for i in range(sections)]
    )
    terms = [forward(term, flip) for flip, term in zip(range(pairs - 1, 0, -1), terms)]
    rec_packed, hyd_packed = call(
        lambda *refs: first_body(aways[0], *refs),
        [shape((cap, steps), BF16)] * 2,
        order, records[0], unit_hydro[0],
        mib=12,
        flops=4 * cap * reaches * steps,
        moved=reaches * steps * 4,
    )
    runoff, ready, places = call(
        lambda *refs: send_body(aways[0], *refs),
        [shape((blocks, LANES), F32), shape((cap, steps), BF16), shape(ids.shape, BF16)],
        own_terms, order, ids, rec_packed, hyd_packed, *terms,
        moved=cap * steps * 6,
    )
    arrived = {aways[0]: forward(ready, aways[0])}
    record_new, theirs, mine, *ready = call(
        lambda *refs: record_body(aways[1:], *refs),
        [shape((reaches, steps), BF16), shape((basins, steps), F32), shape((basins, steps), F32)]
        + [shape((cap, steps), BF16)] * (len(aways) - 1),
        runoff, records[0], unit_hydro[0], order, places,
        out_specs=[HBM] + [VMEM] * (len(aways) + 1),
        scratch=[pltpu.VMEM((reaches, steps), BF16), pltpu.VMEM((cap, steps), BF16), dma(())],
        mib=16,
        flops=2 * cap * reaches * steps,
        moved=reaches * steps * 8,
    )
    for away, block in zip(aways[1:], ready):
        arrived[away] = forward(block, away)
    early, late = aways[:1], aways[1:]
    theirs, mine = call(
        lambda *refs: early_body(early, *refs),
        [shape((basins, steps), F32), shape((basins, steps), F32)],
        theirs, mine, places, *[arrived[a] for a in early],
        mib=12,
        moved=basins * steps * 16,
    )
    (theirs,) = call(
        lambda *refs: late_body(late, True, *refs),
        [shape((basins, steps), BF16)],
        theirs, places, *[arrived[a] for a in late],
        moved=basins * steps * 8,
    )
    passed = lax.ppermute(theirs, "sec", swap(sections))
    (mine,) = call(
        lambda *refs: late_body(late, False, *refs),
        [shape((basins, steps), F32)],
        mine, places, *[arrived[a] for a in late],
        moved=basins * steps * 8,
    )
    (inflow,) = call(
        final_body,
        [shape((basins, steps), F32)],
        mine, passed,
        out_specs=[HBM],
        scratch=[pltpu.VMEM((basins, steps), F32), dma((2,))],
        moved=basins * steps * 10,
    )
    return (moist_out, heat_out, record_new[None], inflow[None])


def solution(mesh):
    placed = (
        P(None, "sec", "lon"),
        P(None, "sec", "lon"),
        P(None, "sec", "lon"),
        P(None, "sec", "lon"),
        P("sec", "lon"),
        P("sec", "lon"),
        P("sec", "lon"),
        P("lon", "sec", None),
        P("lon", "sec", None),
        P("lon", "sec"),
        P("lon", None),
        P("lon", "sec", None, None),
        P("lon", "sec", None),
    )
    return jax.shard_map(
        per_device,
        mesh=mesh,
        in_specs=placed,
        out_specs=(
            P(None, "sec", "lon"),
            P(None, "sec", "lon"),
            P("lon", "sec", None),
            P("lon", "sec", None),
        ),
        check_vma=False,
    )
```

```python
import jax
import jax.numpy as jnp
from jax import lax
from jax.experimental import pallas as pl
from jax.experimental.pallas import tpu as pltpu
from jax.sharding import PartitionSpec as P

LATERAL = 0.2
LANES = 128
PACK_ROWS = 16
F32 = jnp.float32
BF16 = jnp.bfloat16
I32 = jnp.int32
VMEM = pl.BlockSpec(memory_space=pltpu.VMEM)
HBM = pl.BlockSpec(memory_space=pltpu.HBM)


def call(body, outs, *args, ins=None, out_specs=None, scratch=(), mib=8, flops=0, moved=0):
    ins = list(ins) if ins else [VMEM] * len(args)
    args = [
        pltpu.with_memory_space_constraint(arg, pltpu.HBM) if spec is HBM else arg
        for arg, spec in zip(args, ins)
    ]
    return pl.pallas_call(
        body,
        out_shape=list(outs),
        in_specs=ins,
        out_specs=list(out_specs) if out_specs else [VMEM] * len(outs),
        scratch_shapes=list(scratch),
        compiler_params=pltpu.CompilerParams(vmem_limit_bytes=mib * 1024 * 1024),
        cost_estimate=pl.CostEstimate(flops=flops, bytes_accessed=moved, transcendentals=0),
    )(*args)


def fetch(sources, targets, sems):
    copies = [
        pltpu.make_async_copy(src, dst, sems.at[i])
        for i, (src, dst) in enumerate(zip(sources, targets))
    ]
    for copy in copies:
        copy.start()
    return copies


def parity(axis):
    return lax.rem(lax.axis_index(axis), 2)


def gray(place):
    return place ^ (place >> 1)


def ring_place(chip, count):
    shift = 1
    while 2**shift <= count:
        chip = chip ^ (chip >> shift)
        shift *= 2
    return chip


def steps_on(chip, other, count):
    return (ring_place(other, count) - ring_place(chip, count) + count) & (count - 1)


def edges_body(*refs):
    count = 10
    targets = refs[count : 2 * count]
    moist, heat = targets[:2]
    sec_near, sec_far, lon_near, lon_far, sems = refs[2 * count :]
    copies = fetch(refs[:count], targets, sems)
    layers, rows, cols = moist.shape
    lane = lax.broadcasted_iota(I32, (rows, LANES), 1)
    west = jnp.zeros((rows, LANES), F32)
    east = jnp.zeros((rows, LANES), F32)
    sec_even = parity("sec") == 0
    for f, ref in enumerate((moist, heat)):
        copies[f].wait()
        north = ref[:, 0, :]
        south = ref[:, rows - 1, :]
        sec_near[f * layers : (f + 1) * layers, :] = jnp.where(sec_even, south, north).astype(BF16)
        sec_far[f * layers : (f + 1) * layers, :] = jnp.where(sec_even, north, south).astype(BF16)
        for layer in range(layers):
            k = f * layers + layer
            west = jnp.where(lane == k, ref[layer, :, 0:1], west)
            east = jnp.where(lane == k, ref[layer, :, cols - 1 : cols], east)
    lon_even = parity("lon") == 0
    lon_near[...] = jnp.where(lon_even, east, west).astype(BF16)
    lon_far[...] = jnp.where(lon_even, west, east).astype(BF16)
    for copy in copies[2:]:
        copy.wait()


def lookup(table, hi, lo):
    out = jnp.zeros(hi.shape, table.dtype)
    for row in range(table.shape[0]):
        line = jnp.broadcast_to(table[row : row + 1, :], hi.shape)
        got = jnp.take_along_axis(line, lo, axis=1)
        out = jnp.where(hi == row, got, out)
    return out


def index_body(listed, home, down, count_in, order, ids, count, sems):
    copies = fetch((count_in,), (count,), sems)
    slot = lookup(home[...], down[...] >> 7, down[...] & (LANES - 1))
    pairs, width = listed.shape[0] // 2, listed.shape[1]
    tiles = width // LANES
    chip = lax.axis_index("sec") // 2
    chip_basins = home.shape[0] * LANES // pairs
    pos = lax.broadcasted_iota(I32, (1, width), 1)
    copies[0].wait()
    for m in range(pairs):
        c = count[0, 0, 2 * m]
        second = pltpu.roll(listed[2 * m + 1 : 2 * m + 2, :], lax.rem(c, width), 1)
        line = jnp.where(pos < c, listed[2 * m : 2 * m + 1, :], second)
        away = steps_on(chip, m, pairs)
        for t in range(tiles):
            order[pl.ds(away * tiles + t, 1), :] = line[:, t * LANES : (t + 1) * LANES]
    at = order[...]
    place = lookup(slot, at >> 7, at & (LANES - 1))
    pad = jnp.zeros((PACK_ROWS - 2 * tiles, LANES), F32)
    for away in range(pairs):
        m = gray((ring_place(chip, pairs) + away) & (pairs - 1))
        mine = place[away * tiles : (away + 1) * tiles, :] - m * chip_basins
        ids[away] = jnp.concatenate(
            [(mine >> 8).astype(F32), (mine & 255).astype(F32), pad], axis=0
        ).astype(BF16)


def shift_time(x):
    steps = x.shape[1]
    lane = lax.broadcasted_iota(I32, x.shape, 1)
    return jnp.where(lane == steps - 1, 0.0, pltpu.roll(x, steps - 1, 1))


def picked(order, away, tiles, reaches):
    turned = order[...].astype(F32).T
    lane = lax.broadcasted_iota(I32, (LANES, reaches), 1).astype(F32)
    parts = [
        jnp.where(lane == turned[:, t : t + 1], 1.0, 0.0).astype(BF16)
        for t in range(away * tiles, (away + 1) * tiles)
    ]
    return parts[0] if len(parts) == 1 else jnp.concatenate(parts, axis=0)


def first_body(away, order, records, hydro, rec_packed, hyd_packed):
    hot = picked(order, away, rec_packed.shape[0] // LANES, records.shape[0])
    rec = jnp.dot(hot, records[...], preferred_element_type=F32)
    rec_packed[...] = shift_time(rec).astype(BF16)
    hyd_packed[...] = jnp.dot(hot, hydro[...], preferred_element_type=F32).astype(BF16)


def land_body(
    moist, heat, moist_k, heat_k, rain, flux, cell, sec_near, sec_far, lon_near, lon_far,
    moist_out, heat_out, keep, give,
):
    layers, rows, cols = moist.shape
    row = lax.broadcasted_iota(I32, (rows, cols), 0)
    col = lax.broadcasted_iota(I32, (rows, cols), 1)
    sec_even = parity("sec") == 0
    lon_even = parity("lon") == 0
    south_all = jnp.where(sec_even, sec_near[...].astype(F32), sec_far[...].astype(F32))
    north_all = jnp.where(sec_even, sec_far[...].astype(F32), sec_near[...].astype(F32))
    lon = lax.axis_index("lon")
    outer = (lon == 0) | (lon == lax.axis_size("lon") - 1)
    lon_beyond = jnp.where(outer, 0.0, lon_far[...].astype(F32))
    east_all = jnp.where(lon_even, lon_near[...].astype(F32), lon_beyond)
    west_all = jnp.where(lon_even, lon_beyond, lon_near[...].astype(F32))
    for f, (x_ref, k_ref, top, out) in enumerate(
        ((moist, moist_k, rain, moist_out), (heat, heat_k, flux, heat_out))
    ):
        ratio = jnp.zeros((rows, cols), F32)
        value = jnp.zeros((rows, cols), F32)
        below = jnp.zeros((rows, cols), F32)
        ratios, values = [], []
        for layer in range(layers):
            k = f * layers + layer
            x = x_ref[layer]
            up = jnp.where(row == 0, north_all[k : k + 1, :], pltpu.roll(x, 1, 0))
            dn = jnp.where(row == rows - 1, south_all[k : k + 1, :], pltpu.roll(x, rows - 1, 0))
            lf = jnp.where(col == 0, west_all[:, k : k + 1], pltpu.roll(x, 1, 1))
            rt = jnp.where(col == cols - 1, east_all[:, k : k + 1], pltpu.roll(x, cols - 1, 1))
            rhs = x + LATERAL * (up + dn + lf + rt - 4.0 * x)
            if layer == 0:
                rhs = rhs + top[...]
            if layer < layers - 1:
                above = 0.5 * (k_ref[layer] + k_ref[layer + 1])
            else:
                above = jnp.zeros((rows, cols), F32)
            inv = 1.0 / (1.0 + below + above + below * ratio)
            ratio = -above * inv
            value = (rhs + below * value) * inv
            ratios.append(ratio)
            values.append(value)
            below = above
        x = values[-1]
        out[layers - 1] = x
        for layer in range(layers - 2, -1, -1):
            x = values[layer] - ratios[layer] * x
            out[layer] = x
    s = moist_out[0] - 1.0
    soft = jnp.maximum(s, 0.0) + jnp.log1p(jnp.exp(-jnp.abs(s)))
    gate = 1.0 / (1.0 + jnp.exp(-heat_out[0]))
    runoff = soft * gate + 0.5 * moist_k[layers - 1] * moist_out[layers - 1]
    cells = cell[...]
    hi = cells >> 7
    lo = cells & (LANES - 1)
    pairs, blocks = keep.shape[:2]
    his = 2 * pairs * blocks
    hi_iota = lax.broadcasted_iota(I32, (his, cols), 0)
    lo_iota = lax.broadcasted_iota(I32, (LANES, cols), 0)
    acc = jnp.zeros((his, LANES), F32)
    for i in range(rows):
        a = jnp.where(hi_iota == hi[i : i + 1, :], runoff[i : i + 1, :], 0.0).astype(BF16)
        b = jnp.where(lo_iota == lo[i : i + 1, :], 1.0, 0.0).astype(BF16)
        acc = acc + lax.dot_general(a, b, (((1,), (1,)), ((), ())), preferred_element_type=F32)
    both = acc.reshape(pairs, 2, blocks, LANES)
    keep[...] = jnp.where(sec_even, both[:, 0], both[:, 1])
    give[...] = jnp.where(sec_even, both[:, 1], both[:, 0]).astype(BF16)


def terms_body(keep, got, ids, own, *outs):
    pairs, blocks = keep.shape[:2]
    chip = lax.axis_index("sec") // 2
    own[...] = keep[chip] + got[chip].astype(F32)
    for flip, out in zip(range(len(outs), 0, -1), outs):
        m = chip ^ flip
        out[:blocks, :] = (keep[m] + got[m].astype(F32)).astype(BF16)
        out[blocks:, :] = ids[steps_on(chip, m, pairs)]


def send_body(away, own, order, ids, rec_packed, hyd_packed, *refs):
    terms, (runoff, ready, places) = refs[:-3], refs[-3:]
    pairs = places.shape[0]
    chip = lax.axis_index("sec") // 2
    places[0] = ids[0]
    for flip, term in zip(range(len(terms), 0, -1), terms):
        places[steps_on(chip ^ flip, chip, pairs)] = term[term.shape[0] - PACK_ROWS :, :]
    blocks = runoff.shape[0]
    tiles = ready.shape[0] // LANES
    total = own[...]
    for term in terms:
        total = total + term[:blocks, :].astype(F32)
    runoff[...] = total
    at = order[...]
    turned = lookup(total, at >> 7, at & (LANES - 1)).T
    for t in range(tiles):
        rows = pl.ds(t * LANES, LANES)
        col = away * tiles + t
        ready[rows, :] = (
            rec_packed[rows, :].astype(F32) + turned[:, col : col + 1] * hyd_packed[rows, :].astype(F32)
        ).astype(BF16)


def record_body(aways, runoff, records, hydro, order, kept, *ready):
    turned = runoff[...].T
    for t in range(runoff.shape[0]):
        rows = pl.ds(t * LANES, LANES)
        kept[rows, :] = (
            shift_time(records[rows, :].astype(F32)) + turned[:, t : t + 1] * hydro[rows, :].astype(F32)
        ).astype(BF16)
    for away, out in zip(aways, ready):
        hot = picked(order, away, out.shape[0] // LANES, kept.shape[0])
        out[...] = jnp.dot(hot, kept[...], preferred_element_type=F32).astype(BF16)


def hot_of(digits, tiles, basins, other):
    core = parity("sec")
    base = ((1 - core) if other else core) * basins
    slot = lax.broadcasted_iota(I32, (basins, LANES), 0) + base
    slot = slot.astype(F32)
    place = digits[:tiles] * 256.0 + digits[tiles : 2 * tiles]
    parts = [jnp.where(slot == place[t : t + 1, :], 1.0, 0.0).astype(BF16) for t in range(tiles)]
    return parts[0] if len(parts) == 1 else jnp.concatenate(parts, axis=1)


def summed(digits, blocks, basins, other):
    tiles = blocks[0].shape[0] // LANES
    total = None
    for digit, block in zip(digits, blocks):
        hot = hot_of(digit, tiles, basins, other)
        part = jnp.dot(hot, block[...], preferred_element_type=F32)
        total = part if total is None else total + part
    return total


def rest_body(near, order, kept, places, landed, out, theirs, mine, own, sem):
    copy = pltpu.make_async_copy(kept, out, sem)
    copy.start()
    hot = picked(order, 0, own.shape[0] // LANES, kept.shape[0])
    own[...] = jnp.dot(hot, kept[...], preferred_element_type=F32).astype(BF16)
    digits = [places[away].astype(F32) for away in (0, near)]
    basins = mine.shape[0]
    theirs[...] = summed(digits, [own, landed], basins, True)
    mine[...] = summed(digits, [own, landed], basins, False)
    copy.wait()


def early_body(aways, theirs_so_far, mine_so_far, places, *refs):
    blocks, (theirs, mine) = refs[:-2], refs[-2:]
    digits = [places[away].astype(F32) for away in aways]
    basins = mine.shape[0]
    theirs[...] = theirs_so_far[...] + summed(digits, blocks, basins, True)
    mine[...] = mine_so_far[...] + summed(digits, blocks, basins, False)


def late_body(aways, other, so_far, places, *refs):
    blocks, out = refs[:-1], refs[-1]
    digits = [places[away].astype(F32) for away in aways]
    out[...] = (so_far[...] + summed(digits, blocks, out.shape[0], other)).astype(out.dtype)


def final_body(mine, passed, out, held, sems):
    rows = mine.shape[0]
    parts = 2
    size = rows // parts
    copies = []
    for i in range(parts):
        at = pl.ds(i * size, size)
        held[at, :] = mine[at, :] + passed[at, :].astype(F32)
        copy = pltpu.make_async_copy(held.at[at, :], out.at[at, :], sems.at[i])
        copy.start()
        copies.append(copy)
    for copy in copies:
        copy.wait()


def per_device(
    moisture, heat, moist_cond, heat_cond, rain, surface_flux, cell_reach,
    records, unit_hydro, down_basin, basin_home, send_index, send_count,
):
    lons = lax.axis_size("lon")
    sections = lax.axis_size("sec")
    layers, lats, cols = moisture.shape
    reaches, steps = records.shape[1:]
    cap = send_index.shape[3]
    pairs = sections // 2
    basins = basin_home.shape[1] // sections
    blocks = reaches // LANES
    shape = jax.ShapeDtypeStruct
    dma = pltpu.SemaphoreType.DMA

    home = basin_home.reshape(-1, LANES)
    down = down_basin.reshape(-1, LANES)
    listed = send_index.reshape(sections, cap)
    fetched = [
        moisture, heat, moist_cond, heat_cond, rain, surface_flux, cell_reach, home, down, listed
    ]
    *fetched, sec_near, sec_far, lon_near, lon_far = call(
        edges_body,
        [shape(x.shape, x.dtype) for x in fetched]
        + [
            shape((2 * layers, cols), BF16),
            shape((2 * layers, cols), BF16),
            shape((lats, LANES), BF16),
            shape((lats, LANES), BF16),
        ],
        *fetched,
        ins=[HBM] * len(fetched),
        scratch=[dma((len(fetched),))],
        moved=moisture.size * 8,
    )
    *land, home_v, down_v, listed_v = fetched
    swap = lambda count: [(i, i ^ 1) for i in range(count)]
    between = lambda count: [(i, i + 1) for i in range(1, count - 1, 2)] + [
        (i + 1, i) for i in range(1, count - 1, 2)
    ]
    got_sec_far = lax.ppermute(sec_far, "sec", between(sections))
    got_sec_near = lax.ppermute(sec_near, "sec", swap(sections))
    got_lon_far = lax.ppermute(
        lon_far, "lon", [(i, (i - 1 + 2 * (i % 2)) % lons) for i in range(lons)]
    )
    got_lon_near = lax.ppermute(lon_near, "lon", swap(lons))

    moist_out, heat_out, keep, give = call(
        land_body,
        [
            shape(moisture.shape, F32),
            shape(heat.shape, F32),
            shape((pairs, blocks, LANES), F32),
            shape((pairs, blocks, LANES), BF16),
        ],
        *land,
        got_sec_near, got_sec_far, got_lon_near, got_lon_far,
        moved=moisture.size * 24,
    )
    got = lax.ppermute(give, "sec", swap(sections))
    order, ids = call(
        index_body,
        [shape((blocks, LANES), I32), shape((pairs, PACK_ROWS, LANES), BF16)],
        listed_v, home_v, down_v, send_count,
        ins=[VMEM] * 3 + [HBM],
        scratch=[pltpu.SMEM(send_count.shape, I32), dma((1,))],
        moved=moisture.size * 8,
    )
    aways = [pairs // 2]
    for k in range(1, pairs // 2):
        aways += [k, pairs - k]
    own_terms, *terms = call(
        terms_body,
        [shape((blocks, LANES), F32)] + [shape((blocks + PACK_ROWS, LANES), BF16)] * (pairs - 1),
        keep, got, ids,
        moved=reaches * 8,
    )
    forward = lambda block, away: lax.ppermute(
        block,
        "sec",
        [
            (2 * gray(i) + core, 2 * gray((i + away) % pairs) + core)
            for i in range(pairs)
            for core in range(2)
        ],
    )
    terms = [
        lax.ppermute(term, "sec", [(i, i ^ (2 * flip)) for i in range(sections)])
        for flip, term in zip(range(pairs - 1, 0, -1), terms)
    ]
    rec_packed, hyd_packed = call(
        lambda *refs: first_body(aways[0], *refs),
        [shape((cap, steps), BF16)] * 2,
        order, records[0], unit_hydro[0],
        mib=12,
        flops=4 * cap * reaches * steps,
        moved=reaches * steps * 4,
    )
    runoff, ready, places = call(
        lambda *refs: send_body(aways[0], *refs),
        [shape((blocks, LANES), F32), shape((cap, steps), BF16), shape(ids.shape, BF16)],
        own_terms, order, ids, rec_packed, hyd_packed, *terms,
        moved=cap * steps * 6,
    )
    arrived = {aways[0]: forward(ready, aways[0])}
    kept, *ready = call(
        lambda *refs: record_body(aways[1:], *refs),
        [shape((reaches, steps), BF16)] + [shape((cap, steps), BF16)] * (len(aways) - 1),
        runoff, records[0], unit_hydro[0], order,
        mib=16,
        flops=2 * cap * reaches * steps,
        moved=reaches * steps * 8,
    )
    for away, block in zip(aways[1:], ready):
        arrived[away] = forward(block, away)
    near, late = aways[0], aways[-1:]
    record_new, theirs, mine = call(
        lambda *refs: rest_body(near, *refs),
        [shape((reaches, steps), BF16), shape((basins, steps), F32), shape((basins, steps), F32)],
        order, kept, places, arrived[near],
        out_specs=[HBM, VMEM, VMEM],
        scratch=[pltpu.VMEM((cap, steps), BF16), dma(())],
        mib=16,
        flops=2 * cap * reaches * steps,
        moved=reaches * steps * 4,
    )
    early = [a for a in aways[:-1] if a != near]
    theirs, mine = call(
        lambda *refs: early_body(early, *refs),
        [shape((basins, steps), F32), shape((basins, steps), F32)],
        theirs, mine, places, *[arrived[a] for a in early],
        mib=12,
        moved=basins * steps * 16,
    )
    (theirs,) = call(
        lambda *refs: late_body(late, True, *refs),
        [shape((basins, steps), BF16)],
        theirs, places, *[arrived[a] for a in late],
        moved=basins * steps * 8,
    )
    passed = lax.ppermute(theirs, "sec", swap(sections))
    (mine,) = call(
        lambda *refs: late_body(late, False, *refs),
        [shape((basins, steps), F32)],
        mine, places, *[arrived[a] for a in late],
        moved=basins * steps * 8,
    )
    (inflow,) = call(
        final_body,
        [shape((basins, steps), F32)],
        mine, passed,
        out_specs=[HBM],
        scratch=[pltpu.VMEM((basins, steps), F32), dma((2,))],
        moved=basins * steps * 10,
    )
    return (moist_out, heat_out, record_new[None], inflow[None])


def solution(mesh):
    placed = (
        P(None, "sec", "lon"),
        P(None, "sec", "lon"),
        P(None, "sec", "lon"),
        P(None, "sec", "lon"),
        P("sec", "lon"),
        P("sec", "lon"),
        P("sec", "lon"),
        P("lon", "sec", None),
        P("lon", "sec", None),
        P("lon", "sec"),
        P("lon", None),
        P("lon", "sec", None, None),
        P("lon", "sec", None),
    )
    return jax.shard_map(
        per_device,
        mesh=mesh,
        in_specs=placed,
        out_specs=(
            P(None, "sec", "lon"),
            P(None, "sec", "lon"),
            P("lon", "sec", None),
            P("lon", "sec", None),
        ),
        check_vma=False,
    )
```

```python
import jax
import jax.numpy as jnp
from jax import lax
from jax.experimental import pallas as pl
from jax.experimental.pallas import tpu as pltpu
from jax.sharding import PartitionSpec as P

LATERAL = 0.2
LANES = 128
PACK_ROWS = 16
F32 = jnp.float32
BF16 = jnp.bfloat16
I32 = jnp.int32
VMEM = pl.BlockSpec(memory_space=pltpu.VMEM)
HBM = pl.BlockSpec(memory_space=pltpu.HBM)


def call(body, outs, *args, ins=None, out_specs=None, scratch=(), mib=8, flops=0, moved=0):
    ins = list(ins) if ins else [VMEM] * len(args)
    args = [
        pltpu.with_memory_space_constraint(arg, pltpu.HBM) if spec is HBM else arg
        for arg, spec in zip(args, ins)
    ]
    return pl.pallas_call(
        body,
        out_shape=list(outs),
        in_specs=ins,
        out_specs=list(out_specs) if out_specs else [VMEM] * len(outs),
        scratch_shapes=list(scratch),
        compiler_params=pltpu.CompilerParams(vmem_limit_bytes=mib * 1024 * 1024),
        cost_estimate=pl.CostEstimate(flops=flops, bytes_accessed=moved, transcendentals=0),
    )(*args)


def fetch(sources, targets, sems):
    copies = [
        pltpu.make_async_copy(src, dst, sems.at[i])
        for i, (src, dst) in enumerate(zip(sources, targets))
    ]
    for copy in copies:
        copy.start()
    return copies


def parity(axis):
    return lax.rem(lax.axis_index(axis), 2)


def edges_body(*refs):
    count = 2
    targets = refs[count : 2 * count]
    moist, heat = targets[:2]
    sec_near, sec_far, lon_near, lon_far, sems = refs[2 * count :]
    copies = fetch(refs[:count], targets, sems)
    layers, rows, cols = moist.shape
    lane = lax.broadcasted_iota(I32, (rows, LANES), 1)
    west = jnp.zeros((rows, LANES), F32)
    east = jnp.zeros((rows, LANES), F32)
    sec_even = parity("sec") == 0
    for f, ref in enumerate((moist, heat)):
        copies[f].wait()
        north = ref[:, 0, :]
        south = ref[:, rows - 1, :]
        sec_near[f * layers : (f + 1) * layers, :] = jnp.where(sec_even, south, north).astype(BF16)
        sec_far[f * layers : (f + 1) * layers, :] = jnp.where(sec_even, north, south).astype(BF16)
        for layer in range(layers):
            k = f * layers + layer
            west = jnp.where(lane == k, ref[layer, :, 0:1], west)
            east = jnp.where(lane == k, ref[layer, :, cols - 1 : cols], east)
    lon_even = parity("lon") == 0
    lon_near[...] = jnp.where(lon_even, east, west).astype(BF16)
    lon_far[...] = jnp.where(lon_even, west, east).astype(BF16)
    for copy in copies[2:]:
        copy.wait()


def lookup(table, hi, lo):
    out = jnp.zeros(hi.shape, table.dtype)
    for row in range(table.shape[0]):
        line = jnp.broadcast_to(table[row : row + 1, :], hi.shape)
        got = jnp.take_along_axis(line, lo, axis=1)
        out = jnp.where(hi == row, got, out)
    return out


def index_body(*refs):
    count_in, home_in, down_in, listed_in = refs[:4]
    order, ids = refs[9:11]
    count, home, down, listed, sems = refs[16:]
    copies = fetch(refs[:9], (count, home, down, listed, *refs[11:16]), sems)
    pairs, width = listed.shape[0] // 2, listed.shape[1]
    tiles = width // LANES
    chip = lax.axis_index("sec") // 2
    chip_basins = home.shape[0] * LANES // pairs
    for copy in copies[:4]:
        copy.wait()
    slot = lookup(home[...], down[...] >> 7, down[...] & (LANES - 1))
    pos = lax.broadcasted_iota(I32, (1, width), 1)
    for m in range(pairs):
        c = count[0, 0, 2 * m]
        second = pltpu.roll(listed[2 * m + 1 : 2 * m + 2, :], lax.rem(c, width), 1)
        line = jnp.where(pos < c, listed[2 * m : 2 * m + 1, :], second)
        away = m ^ chip
        for t in range(tiles):
            order[pl.ds(away * tiles + t, 1), :] = line[:, t * LANES : (t + 1) * LANES]
    at = order[...]
    place = lookup(slot, at >> 7, at & (LANES - 1))
    pad = jnp.zeros((PACK_ROWS - 2 * tiles, LANES), F32)
    for away in range(pairs):
        m = away ^ chip
        mine = place[away * tiles : (away + 1) * tiles, :] - m * chip_basins
        ids[away] = jnp.concatenate(
            [(mine >> 8).astype(F32), (mine & 255).astype(F32), pad], axis=0
        ).astype(BF16)
    for copy in copies[4:]:
        copy.wait()


def shift_time(x):
    steps = x.shape[1]
    lane = lax.broadcasted_iota(I32, x.shape, 1)
    return jnp.where(lane == steps - 1, 0.0, pltpu.roll(x, steps - 1, 1))


def picked(order, away, tiles, reaches):
    turned = order[...].astype(F32).T
    lane = lax.broadcasted_iota(I32, (LANES, reaches), 1).astype(F32)
    parts = [
        jnp.where(lane == turned[:, t : t + 1], 1.0, 0.0).astype(BF16)
        for t in range(away * tiles, (away + 1) * tiles)
    ]
    return parts[0] if len(parts) == 1 else jnp.concatenate(parts, axis=0)


def first_body(away, order, records, hydro, rec_packed, hyd_packed):
    hot = picked(order, away, rec_packed.shape[0] // LANES, records.shape[0])
    rec = jnp.dot(hot, records[...], preferred_element_type=F32)
    rec_packed[...] = shift_time(rec).astype(BF16)
    hyd_packed[...] = jnp.dot(hot, hydro[...], preferred_element_type=F32).astype(BF16)


def land_body(
    moist, heat, moist_k, heat_k, rain, flux, cell, sec_near, sec_far, lon_near, lon_far,
    moist_out, heat_out, keep, give,
):
    layers, rows, cols = moist.shape
    row = lax.broadcasted_iota(I32, (rows, cols), 0)
    col = lax.broadcasted_iota(I32, (rows, cols), 1)
    sec_even = parity("sec") == 0
    lon_even = parity("lon") == 0
    south_all = jnp.where(sec_even, sec_near[...].astype(F32), sec_far[...].astype(F32))
    north_all = jnp.where(sec_even, sec_far[...].astype(F32), sec_near[...].astype(F32))
    lon = lax.axis_index("lon")
    outer = (lon == 0) | (lon == lax.axis_size("lon") - 1)
    lon_beyond = jnp.where(outer, 0.0, lon_far[...].astype(F32))
    east_all = jnp.where(lon_even, lon_near[...].astype(F32), lon_beyond)
    west_all = jnp.where(lon_even, lon_beyond, lon_near[...].astype(F32))
    for f, (x_ref, k_ref, top, out) in enumerate(
        ((moist, moist_k, rain, moist_out), (heat, heat_k, flux, heat_out))
    ):
        ratio = jnp.zeros((rows, cols), F32)
        value = jnp.zeros((rows, cols), F32)
        below = jnp.zeros((rows, cols), F32)
        ratios, values = [], []
        for layer in range(layers):
            k = f * layers + layer
            x = x_ref[layer]
            up = jnp.where(row == 0, north_all[k : k + 1, :], pltpu.roll(x, 1, 0))
            dn = jnp.where(row == rows - 1, south_all[k : k + 1, :], pltpu.roll(x, rows - 1, 0))
            lf = jnp.where(col == 0, west_all[:, k : k + 1], pltpu.roll(x, 1, 1))
            rt = jnp.where(col == cols - 1, east_all[:, k : k + 1], pltpu.roll(x, cols - 1, 1))
            rhs = x + LATERAL * (up + dn + lf + rt - 4.0 * x)
            if layer == 0:
                rhs = rhs + top[...]
            if layer < layers - 1:
                above = 0.5 * (k_ref[layer] + k_ref[layer + 1])
            else:
                above = jnp.zeros((rows, cols), F32)
            inv = 1.0 / (1.0 + below + above + below * ratio)
            ratio = -above * inv
            value = (rhs + below * value) * inv
            ratios.append(ratio)
            values.append(value)
            below = above
        x = values[-1]
        out[layers - 1] = x
        for layer in range(layers - 2, -1, -1):
            x = values[layer] - ratios[layer] * x
            out[layer] = x
    s = moist_out[0] - 1.0
    soft = jnp.maximum(s, 0.0) + jnp.log1p(jnp.exp(-jnp.abs(s)))
    gate = 1.0 / (1.0 + jnp.exp(-heat_out[0]))
    runoff = soft * gate + 0.5 * moist_k[layers - 1] * moist_out[layers - 1]
    cells = cell[...]
    hi = cells >> 7
    lo = cells & (LANES - 1)
    pairs, blocks = keep.shape[:2]
    his = 2 * pairs * blocks
    hi_iota = lax.broadcasted_iota(I32, (his, cols), 0)
    lo_iota = lax.broadcasted_iota(I32, (LANES, cols), 0)
    acc = jnp.zeros((his, LANES), F32)
    for i in range(rows):
        a = jnp.where(hi_iota == hi[i : i + 1, :], runoff[i : i + 1, :], 0.0).astype(BF16)
        b = jnp.where(lo_iota == lo[i : i + 1, :], 1.0, 0.0).astype(BF16)
        acc = acc + lax.dot_general(a, b, (((1,), (1,)), ((), ())), preferred_element_type=F32)
    both = acc.reshape(pairs, 2, blocks, LANES)
    keep[...] = jnp.where(sec_even, both[:, 0], both[:, 1])
    give[...] = jnp.where(sec_even, both[:, 1], both[:, 0]).astype(BF16)


def terms_body(keep, got, ids, own, *outs):
    pairs, blocks = keep.shape[:2]
    chip = lax.axis_index("sec") // 2
    own[...] = keep[chip] + got[chip].astype(F32)
    for flip, out in zip(range(len(outs), 0, -1), outs):
        m = chip ^ flip
        out[:blocks, :] = (keep[m] + got[m].astype(F32)).astype(BF16)
        out[blocks:, :] = ids[flip]


def send_body(away, own, order, ids, rec_packed, hyd_packed, *refs):
    terms, (runoff, ready, places) = refs[:-3], refs[-3:]
    places[0] = ids[0]
    for flip, term in zip(range(len(terms), 0, -1), terms):
        places[flip] = term[term.shape[0] - PACK_ROWS :, :]
    blocks = runoff.shape[0]
    tiles = ready.shape[0] // LANES
    total = own[...]
    for term in terms:
        total = total + term[:blocks, :].astype(F32)
    runoff[...] = total
    at = order[...]
    turned = lookup(total, at >> 7, at & (LANES - 1)).T
    for t in range(tiles):
        rows = pl.ds(t * LANES, LANES)
        col = away * tiles + t
        ready[rows, :] = (
            rec_packed[rows, :].astype(F32) + turned[:, col : col + 1] * hyd_packed[rows, :].astype(F32)
        ).astype(BF16)


def record_body(aways, runoff, records, hydro, order, kept, *ready):
    turned = runoff[...].T
    for t in range(runoff.shape[0]):
        rows = pl.ds(t * LANES, LANES)
        kept[rows, :] = (
            shift_time(records[rows, :].astype(F32)) + turned[:, t : t + 1] * hydro[rows, :].astype(F32)
        ).astype(BF16)
    for away, out in zip(aways, ready):
        hot = picked(order, away, out.shape[0] // LANES, kept.shape[0])
        out[...] = jnp.dot(hot, kept[...], preferred_element_type=F32).astype(BF16)


def hot_of(digits, tiles, basins, other):
    core = parity("sec")
    base = ((1 - core) if other else core) * basins
    slot = lax.broadcasted_iota(I32, (basins, LANES), 0) + base
    slot = slot.astype(F32)
    place = digits[:tiles] * 256.0 + digits[tiles : 2 * tiles]
    parts = [jnp.where(slot == place[t : t + 1, :], 1.0, 0.0).astype(BF16) for t in range(tiles)]
    return parts[0] if len(parts) == 1 else jnp.concatenate(parts, axis=1)


def summed(digits, blocks, basins, other):
    tiles = blocks[0].shape[0] // LANES
    total = None
    for digit, block in zip(digits, blocks):
        hot = hot_of(digit, tiles, basins, other)
        part = jnp.dot(hot, block[...], preferred_element_type=F32)
        total = part if total is None else total + part
    return total


def rest_body(
    near, order, kept, places, landed, moist, heat, out, moist_out, heat_out, theirs, mine, own, sems
):
    copies = fetch((kept, moist, heat), (out, moist_out, heat_out), sems)
    hot = picked(order, 0, own.shape[0] // LANES, kept.shape[0])
    own[...] = jnp.dot(hot, kept[...], preferred_element_type=F32).astype(BF16)
    digits = [places[away].astype(F32) for away in (0, near)]
    basins = mine.shape[0]
    theirs[...] = summed(digits, [own, landed], basins, True)
    mine[...] = summed(digits, [own, landed], basins, False)
    for copy in copies:
        copy.wait()


def early_body(aways, theirs_so_far, mine_so_far, places, *refs):
    blocks, (theirs, mine) = refs[:-2], refs[-2:]
    digits = [places[away].astype(F32) for away in aways]
    basins = mine.shape[0]
    theirs[...] = theirs_so_far[...] + summed(digits, blocks, basins, True)
    mine[...] = mine_so_far[...] + summed(digits, blocks, basins, False)


def late_body(aways, other, so_far, places, *refs):
    blocks, out = refs[:-1], refs[-1]
    digits = [places[away].astype(F32) for away in aways]
    out[...] = (so_far[...] + summed(digits, blocks, out.shape[0], other)).astype(out.dtype)


def final_body(mine, passed, out, held, sems):
    rows = mine.shape[0]
    parts = 2
    size = rows // parts
    copies = []
    for i in range(parts):
        at = pl.ds(i * size, size)
        held[at, :] = mine[at, :] + passed[at, :].astype(F32)
        copy = pltpu.make_async_copy(held.at[at, :], out.at[at, :], sems.at[i])
        copy.start()
        copies.append(copy)
    for copy in copies:
        copy.wait()


def per_device(
    moisture, heat, moist_cond, heat_cond, rain, surface_flux, cell_reach,
    records, unit_hydro, down_basin, basin_home, send_index, send_count,
):
    lons = lax.axis_size("lon")
    sections = lax.axis_size("sec")
    layers, lats, cols = moisture.shape
    reaches, steps = records.shape[1:]
    cap = send_index.shape[3]
    pairs = sections // 2
    basins = basin_home.shape[1] // sections
    blocks = reaches // LANES
    shape = jax.ShapeDtypeStruct
    dma = pltpu.SemaphoreType.DMA

    home = basin_home.reshape(-1, LANES)
    down = down_basin.reshape(-1, LANES)
    listed = send_index.reshape(sections, cap)
    moist_v, heat_v, sec_near, sec_far, lon_near, lon_far = call(
        edges_body,
        [
            shape(moisture.shape, F32),
            shape(heat.shape, F32),
            shape((2 * layers, cols), BF16),
            shape((2 * layers, cols), BF16),
            shape((lats, LANES), BF16),
            shape((lats, LANES), BF16),
        ],
        moisture, heat,
        ins=[HBM] * 2,
        scratch=[dma((2,))],
        moved=moisture.size * 8,
    )
    swap = lambda count: [(i, i ^ 1) for i in range(count)]
    between = lambda count: [(i, i + 1) for i in range(1, count - 1, 2)] + [
        (i + 1, i) for i in range(1, count - 1, 2)
    ]
    got_sec_far = lax.ppermute(sec_far, "sec", between(sections))
    got_sec_near = lax.ppermute(sec_near, "sec", swap(sections))
    got_lon_far = lax.ppermute(
        lon_far, "lon", [(i, (i - 1 + 2 * (i % 2)) % lons) for i in range(lons)]
    )
    got_lon_near = lax.ppermute(lon_near, "lon", swap(lons))

    land = [moist_cond, heat_cond, rain, surface_flux, cell_reach]
    tables = [send_count, home, down, listed]
    order, ids, *land = call(
        index_body,
        [shape((blocks, LANES), I32), shape((pairs, PACK_ROWS, LANES), BF16)]
        + [shape(x.shape, x.dtype) for x in land],
        *tables, *land,
        ins=[HBM] * 9,
        scratch=[pltpu.SMEM(send_count.shape, I32)]
        + [pltpu.VMEM(x.shape, I32) for x in tables[1:]]
        + [dma((9,))],
        moved=moisture.size * 8,
    )
    moist_new, heat_new, keep, give = call(
        land_body,
        [
            shape(moisture.shape, F32),
            shape(heat.shape, F32),
            shape((pairs, blocks, LANES), F32),
            shape((pairs, blocks, LANES), BF16),
        ],
        moist_v, heat_v, *land,
        got_sec_near, got_sec_far, got_lon_near, got_lon_far,
        moved=moisture.size * 24,
    )
    got = lax.ppermute(give, "sec", swap(sections))
    aways = []
    for k in range(1, pairs // 2 + 1):
        aways += [k] if 2 * k == pairs else [pairs - k, k]
    own_terms, *terms = call(
        terms_body,
        [shape((blocks, LANES), F32)] + [shape((blocks + PACK_ROWS, LANES), BF16)] * (pairs - 1),
        keep, got, ids,
        moved=reaches * 8,
    )
    forward = lambda block, away: lax.ppermute(
        block, "sec", [(i, i ^ (2 * away)) for i in range(sections)]
    )
    terms = [forward(term, flip) for flip, term in zip(range(pairs - 1, 0, -1), terms)]
    rec_packed, hyd_packed = call(
        lambda *refs: first_body(aways[0], *refs),
        [shape((cap, steps), BF16)] * 2,
        order, records[0], unit_hydro[0],
        mib=12,
        flops=4 * cap * reaches * steps,
        moved=reaches * steps * 4,
    )
    runoff, ready, places = call(
        lambda *refs: send_body(aways[0], *refs),
        [shape((blocks, LANES), F32), shape((cap, steps), BF16), shape(ids.shape, BF16)],
        own_terms, order, ids, rec_packed, hyd_packed, *terms,
        moved=cap * steps * 6,
    )
    arrived = {aways[0]: forward(ready, aways[0])}
    kept, *ready = call(
        lambda *refs: record_body(aways[1:], *refs),
        [shape((reaches, steps), BF16)] + [shape((cap, steps), BF16)] * (len(aways) - 1),
        runoff, records[0], unit_hydro[0], order,
        mib=16,
        flops=2 * cap * reaches * steps,
        moved=reaches * steps * 8,
    )
    for away, block in zip(aways[1:], ready):
        arrived[away] = forward(block, away)
    near, late = aways[0], aways[-1:]
    record_new, moist_out, heat_out, theirs, mine = call(
        lambda *refs: rest_body(near, *refs),
        [
            shape((reaches, steps), BF16),
            shape(moisture.shape, F32),
            shape(heat.shape, F32),
            shape((basins, steps), F32),
            shape((basins, steps), F32),
        ],
        order, kept, places, arrived[near], moist_new, heat_new,
        out_specs=[HBM] * 3 + [VMEM] * 2,
        scratch=[pltpu.VMEM((cap, steps), BF16), dma((3,))],
        mib=16,
        flops=2 * cap * reaches * steps,
        moved=reaches * steps * 4,
    )
    early = [a for a in aways[:-1] if a != near]
    theirs, mine = call(
        lambda *refs: early_body(early, *refs),
        [shape((basins, steps), F32), shape((basins, steps), F32)],
        theirs, mine, places, *[arrived[a] for a in early],
        mib=12,
        moved=basins * steps * 16,
    )
    (theirs,) = call(
        lambda *refs: late_body(late, True, *refs),
        [shape((basins, steps), BF16)],
        theirs, places, *[arrived[a] for a in late],
        moved=basins * steps * 8,
    )
    passed = lax.ppermute(theirs, "sec", swap(sections))
    (mine,) = call(
        lambda *refs: late_body(late, False, *refs),
        [shape((basins, steps), F32)],
        mine, places, *[arrived[a] for a in late],
        moved=basins * steps * 8,
    )
    (inflow,) = call(
        final_body,
        [shape((basins, steps), F32)],
        mine, passed,
        out_specs=[HBM],
        scratch=[pltpu.VMEM((basins, steps), F32), dma((2,))],
        moved=basins * steps * 10,
    )
    return (moist_out, heat_out, record_new[None], inflow[None])


def solution(mesh):
    placed = (
        P(None, "sec", "lon"),
        P(None, "sec", "lon"),
        P(None, "sec", "lon"),
        P(None, "sec", "lon"),
        P("sec", "lon"),
        P("sec", "lon"),
        P("sec", "lon"),
        P("lon", "sec", None),
        P("lon", "sec", None),
        P("lon", "sec"),
        P("lon", None),
        P("lon", "sec", None, None),
        P("lon", "sec", None),
    )
    return jax.shard_map(
        per_device,
        mesh=mesh,
        in_specs=placed,
        out_specs=(
            P(None, "sec", "lon"),
            P(None, "sec", "lon"),
            P("lon", "sec", None),
            P("lon", "sec", None),
        ),
        check_vma=False,
    )
```

```python
import jax
import jax.numpy as jnp
from jax import lax
from jax.experimental import pallas as pl
from jax.experimental.pallas import tpu as pltpu
from jax.sharding import PartitionSpec as P

LATERAL = 0.2
LANES = 128
PACK_ROWS = 16
F32 = jnp.float32
BF16 = jnp.bfloat16
I32 = jnp.int32
VMEM = pl.BlockSpec(memory_space=pltpu.VMEM)
HBM = pl.BlockSpec(memory_space=pltpu.HBM)


def call(body, outs, *args, ins=None, out_specs=None, scratch=(), mib=8, flops=0, moved=0):
    ins = list(ins) if ins else [VMEM] * len(args)
    args = [
        pltpu.with_memory_space_constraint(arg, pltpu.HBM) if spec is HBM else arg
        for arg, spec in zip(args, ins)
    ]
    return pl.pallas_call(
        body,
        out_shape=list(outs),
        in_specs=ins,
        out_specs=list(out_specs) if out_specs else [VMEM] * len(outs),
        scratch_shapes=list(scratch),
        compiler_params=pltpu.CompilerParams(vmem_limit_bytes=mib * 1024 * 1024),
        cost_estimate=pl.CostEstimate(flops=flops, bytes_accessed=moved, transcendentals=0),
    )(*args)


def fetch(sources, targets, sems):
    copies = [
        pltpu.make_async_copy(src, dst, sems.at[i])
        for i, (src, dst) in enumerate(zip(sources, targets))
    ]
    for copy in copies:
        copy.start()
    return copies


def parity(axis):
    return lax.rem(lax.axis_index(axis), 2)


def edges_body(*refs):
    count = 2
    targets = refs[count : 2 * count]
    moist, heat = targets[:2]
    sec_near, sec_far, lon_near, lon_far, sems = refs[2 * count :]
    copies = fetch(refs[:count], targets, sems)
    layers, rows, cols = moist.shape
    lane = lax.broadcasted_iota(I32, (rows, LANES), 1)
    west = jnp.zeros((rows, LANES), F32)
    east = jnp.zeros((rows, LANES), F32)
    sec_even = parity("sec") == 0
    for f, ref in enumerate((moist, heat)):
        copies[f].wait()
        north = ref[:, 0, :]
        south = ref[:, rows - 1, :]
        sec_near[f * layers : (f + 1) * layers, :] = jnp.where(sec_even, south, north).astype(BF16)
        sec_far[f * layers : (f + 1) * layers, :] = jnp.where(sec_even, north, south).astype(BF16)
        for layer in range(layers):
            k = f * layers + layer
            west = jnp.where(lane == k, ref[layer, :, 0:1], west)
            east = jnp.where(lane == k, ref[layer, :, cols - 1 : cols], east)
    lon_even = parity("lon") == 0
    lon_near[...] = jnp.where(lon_even, east, west).astype(BF16)
    lon_far[...] = jnp.where(lon_even, west, east).astype(BF16)
    for copy in copies[2:]:
        copy.wait()


def lookup(table, hi, lo):
    out = jnp.zeros(hi.shape, table.dtype)
    for row in range(table.shape[0]):
        line = jnp.broadcast_to(table[row : row + 1, :], hi.shape)
        got = jnp.take_along_axis(line, lo, axis=1)
        out = jnp.where(hi == row, got, out)
    return out


def index_body(*refs):
    count_in, home_in, down_in, listed_in = refs[:4]
    order, ids = refs[9:11]
    count, home, down, listed, sems = refs[16:]
    copies = fetch(refs[:9], (count, home, down, listed, *refs[11:16]), sems)
    pairs, width = listed.shape[0] // 2, listed.shape[1]
    tiles = width // LANES
    chip = lax.axis_index("sec") // 2
    chip_basins = home.shape[0] * LANES // pairs
    for copy in copies[:4]:
        copy.wait()
    slot = lookup(home[...], down[...] >> 7, down[...] & (LANES - 1))
    pos = lax.broadcasted_iota(I32, (1, width), 1)
    for m in range(pairs):
        c = count[0, 0, 2 * m]
        second = pltpu.roll(listed[2 * m + 1 : 2 * m + 2, :], lax.rem(c, width), 1)
        line = jnp.where(pos < c, listed[2 * m : 2 * m + 1, :], second)
        away = m ^ chip
        for t in range(tiles):
            order[pl.ds(away * tiles + t, 1), :] = line[:, t * LANES : (t + 1) * LANES]
    at = order[...]
    place = lookup(slot, at >> 7, at & (LANES - 1))
    pad = jnp.zeros((PACK_ROWS - 2 * tiles, LANES), F32)
    for away in range(pairs):
        m = away ^ chip
        mine = place[away * tiles : (away + 1) * tiles, :] - m * chip_basins
        ids[away] = jnp.concatenate(
            [(mine >> 8).astype(F32), (mine & 255).astype(F32), pad], axis=0
        ).astype(BF16)
    for copy in copies[4:]:
        copy.wait()


def shift_time(x):
    steps = x.shape[1]
    lane = lax.broadcasted_iota(I32, x.shape, 1)
    return jnp.where(lane == steps - 1, 0.0, pltpu.roll(x, steps - 1, 1))


def picked(order, away, tiles, reaches):
    turned = order[...].astype(F32).T
    lane = lax.broadcasted_iota(I32, (LANES, reaches), 1).astype(F32)
    parts = [
        jnp.where(lane == turned[:, t : t + 1], 1.0, 0.0).astype(BF16)
        for t in range(away * tiles, (away + 1) * tiles)
    ]
    return parts[0] if len(parts) == 1 else jnp.concatenate(parts, axis=0)


def first_body(away, shifted, order, rows, packed):
    hot = picked(order, away, packed.shape[0] // LANES, rows.shape[0])
    out = jnp.dot(hot, rows[...], preferred_element_type=F32)
    packed[...] = (shift_time(out) if shifted else out).astype(BF16)


def land_body(
    moist, heat, moist_k, heat_k, rain, flux, cell, sec_near, sec_far, lon_near, lon_far,
    moist_out, heat_out, keep, give,
):
    layers, rows, cols = moist.shape
    row = lax.broadcasted_iota(I32, (rows, cols), 0)
    col = lax.broadcasted_iota(I32, (rows, cols), 1)
    sec_even = parity("sec") == 0
    lon_even = parity("lon") == 0
    south_all = jnp.where(sec_even, sec_near[...].astype(F32), sec_far[...].astype(F32))
    north_all = jnp.where(sec_even, sec_far[...].astype(F32), sec_near[...].astype(F32))
    lon = lax.axis_index("lon")
    outer = (lon == 0) | (lon == lax.axis_size("lon") - 1)
    lon_beyond = jnp.where(outer, 0.0, lon_far[...].astype(F32))
    east_all = jnp.where(lon_even, lon_near[...].astype(F32), lon_beyond)
    west_all = jnp.where(lon_even, lon_beyond, lon_near[...].astype(F32))
    for f, (x_ref, k_ref, top, out) in enumerate(
        ((moist, moist_k, rain, moist_out), (heat, heat_k, flux, heat_out))
    ):
        ratio = jnp.zeros((rows, cols), F32)
        value = jnp.zeros((rows, cols), F32)
        below = jnp.zeros((rows, cols), F32)
        ratios, values = [], []
        for layer in range(layers):
            k = f * layers + layer
            x = x_ref[layer]
            up = jnp.where(row == 0, north_all[k : k + 1, :], pltpu.roll(x, 1, 0))
            dn = jnp.where(row == rows - 1, south_all[k : k + 1, :], pltpu.roll(x, rows - 1, 0))
            lf = jnp.where(col == 0, west_all[:, k : k + 1], pltpu.roll(x, 1, 1))
            rt = jnp.where(col == cols - 1, east_all[:, k : k + 1], pltpu.roll(x, cols - 1, 1))
            rhs = x + LATERAL * (up + dn + lf + rt - 4.0 * x)
            if layer == 0:
                rhs = rhs + top[...]
            if layer < layers - 1:
                above = 0.5 * (k_ref[layer] + k_ref[layer + 1])
            else:
                above = jnp.zeros((rows, cols), F32)
            inv = 1.0 / (1.0 + below + above + below * ratio)
            ratio = -above * inv
            value = (rhs + below * value) * inv
            ratios.append(ratio)
            values.append(value)
            below = above
        x = values[-1]
        out[layers - 1] = x
        for layer in range(layers - 2, -1, -1):
            x = values[layer] - ratios[layer] * x
            out[layer] = x
    s = moist_out[0] - 1.0
    soft = jnp.maximum(s, 0.0) + jnp.log1p(jnp.exp(-jnp.abs(s)))
    gate = 1.0 / (1.0 + jnp.exp(-heat_out[0]))
    runoff = soft * gate + 0.5 * moist_k[layers - 1] * moist_out[layers - 1]
    cells = cell[...]
    hi = cells >> 7
    lo = cells & (LANES - 1)
    pairs, blocks = keep.shape[:2]
    his = 2 * pairs * blocks
    hi_iota = lax.broadcasted_iota(I32, (his, cols), 0)
    lo_iota = lax.broadcasted_iota(I32, (LANES, cols), 0)
    acc = jnp.zeros((his, LANES), F32)
    for i in range(rows):
        a = jnp.where(hi_iota == hi[i : i + 1, :], runoff[i : i + 1, :], 0.0).astype(BF16)
        b = jnp.where(lo_iota == lo[i : i + 1, :], 1.0, 0.0).astype(BF16)
        acc = acc + lax.dot_general(a, b, (((1,), (1,)), ((), ())), preferred_element_type=F32)
    both = acc.reshape(pairs, 2, blocks, LANES)
    keep[...] = jnp.where(sec_even, both[:, 0], both[:, 1])
    give[...] = jnp.where(sec_even, both[:, 1], both[:, 0]).astype(BF16)


def terms_body(keep, got, ids, packed, own, *outs):
    pairs, blocks = keep.shape[:2]
    chip = lax.axis_index("sec") // 2
    own[...] = keep[chip] + got[chip].astype(F32)
    for flip, out in zip(range(len(outs), 0, -1), outs):
        m = chip ^ flip
        out[:blocks, :] = (keep[m] + got[m].astype(F32)).astype(BF16)
        out[blocks:, :] = ids[flip]


def send_body(away, own, order, ids, rec_packed, hyd_packed, *refs):
    terms, (runoff, ready, places) = refs[:-3], refs[-3:]
    places[0] = ids[0]
    for flip, term in zip(range(len(terms), 0, -1), terms):
        places[flip] = term[term.shape[0] - PACK_ROWS :, :]
    blocks = runoff.shape[0]
    tiles = ready.shape[0] // LANES
    total = own[...]
    for term in terms:
        total = total + term[:blocks, :].astype(F32)
    runoff[...] = total
    at = order[...]
    turned = lookup(total, at >> 7, at & (LANES - 1)).T
    for t in range(tiles):
        rows = pl.ds(t * LANES, LANES)
        col = away * tiles + t
        ready[rows, :] = (
            rec_packed[rows, :].astype(F32) + turned[:, col : col + 1] * hyd_packed[rows, :].astype(F32)
        ).astype(BF16)


def record_body(aways, runoff, records, hydro, order, kept, *ready):
    turned = runoff[...].T
    for t in range(runoff.shape[0]):
        rows = pl.ds(t * LANES, LANES)
        kept[rows, :] = (
            shift_time(records[rows, :].astype(F32)) + turned[:, t : t + 1] * hydro[rows, :].astype(F32)
        ).astype(BF16)
    for away, out in zip(aways, ready):
        hot = picked(order, away, out.shape[0] // LANES, kept.shape[0])
        out[...] = jnp.dot(hot, kept[...], preferred_element_type=F32).astype(BF16)


def hot_of(digits, tiles, basins, other):
    core = parity("sec")
    base = ((1 - core) if other else core) * basins
    slot = lax.broadcasted_iota(I32, (basins, LANES), 0) + base
    slot = slot.astype(F32)
    place = digits[:tiles] * 256.0 + digits[tiles : 2 * tiles]
    parts = [jnp.where(slot == place[t : t + 1, :], 1.0, 0.0).astype(BF16) for t in range(tiles)]
    return parts[0] if len(parts) == 1 else jnp.concatenate(parts, axis=1)


def summed(digits, blocks, basins, other):
    tiles = blocks[0].shape[0] // LANES
    total = None
    for digit, block in zip(digits, blocks):
        hot = hot_of(digit, tiles, basins, other)
        part = jnp.dot(hot, block[...], preferred_element_type=F32)
        total = part if total is None else total + part
    return total


def rest_body(
    near, order, kept, places, landed, moist, heat, out, moist_out, heat_out, theirs, mine, own, sems
):
    copies = fetch((kept, moist, heat), (out, moist_out, heat_out), sems)
    hot = picked(order, 0, own.shape[0] // LANES, kept.shape[0])
    own[...] = jnp.dot(hot, kept[...], preferred_element_type=F32).astype(BF16)
    digits = [places[away].astype(F32) for away in (0, near)]
    basins = mine.shape[0]
    theirs[...] = summed(digits, [own, landed], basins, True)
    mine[...] = summed(digits, [own, landed], basins, False)
    for copy in copies:
        copy.wait()


def early_body(aways, theirs_so_far, mine_so_far, places, *refs):
    blocks, (theirs, mine) = refs[:-2], refs[-2:]
    digits = [places[away].astype(F32) for away in aways]
    basins = mine.shape[0]
    theirs[...] = theirs_so_far[...] + summed(digits, blocks, basins, True)
    mine[...] = mine_so_far[...] + summed(digits, blocks, basins, False)


def late_body(aways, other, part, so_far, places, *refs):
    blocks, out = refs[:-1], refs[-1]
    cut = pl.ds(part * out.shape[1], out.shape[1])
    digits = [places[away].astype(F32) for away in aways]
    blocks = [block.at[:, cut] for block in blocks]
    out[...] = (so_far[:, cut] + summed(digits, blocks, out.shape[0], other)).astype(out.dtype)


def final_body(mine, *refs):
    passed, (out, held, sems) = refs[:-3], refs[-3:]
    size = mine.shape[1] // len(passed)
    copies = []
    for i, part in enumerate(passed):
        cut = pl.ds(i * size, size)
        held[:, cut] = mine[:, cut] + part[...].astype(F32)
        copy = pltpu.make_async_copy(held.at[:, cut], out.at[:, cut], sems.at[i])
        copy.start()
        copies.append(copy)
    for copy in copies:
        copy.wait()


def per_device(
    moisture, heat, moist_cond, heat_cond, rain, surface_flux, cell_reach,
    records, unit_hydro, down_basin, basin_home, send_index, send_count,
):
    lons = lax.axis_size("lon")
    sections = lax.axis_size("sec")
    layers, lats, cols = moisture.shape
    reaches, steps = records.shape[1:]
    cap = send_index.shape[3]
    pairs = sections // 2
    basins = basin_home.shape[1] // sections
    blocks = reaches // LANES
    shape = jax.ShapeDtypeStruct
    dma = pltpu.SemaphoreType.DMA

    home = basin_home.reshape(-1, LANES)
    down = down_basin.reshape(-1, LANES)
    listed = send_index.reshape(sections, cap)
    moist_v, heat_v, sec_near, sec_far, lon_near, lon_far = call(
        edges_body,
        [
            shape(moisture.shape, F32),
            shape(heat.shape, F32),
            shape((2 * layers, cols), BF16),
            shape((2 * layers, cols), BF16),
            shape((lats, LANES), BF16),
            shape((lats, LANES), BF16),
        ],
        moisture, heat,
        ins=[HBM] * 2,
        scratch=[dma((2,))],
        moved=moisture.size * 8,
    )
    swap = lambda count: [(i, i ^ 1) for i in range(count)]
    between = lambda count: [(i, i + 1) for i in range(1, count - 1, 2)] + [
        (i + 1, i) for i in range(1, count - 1, 2)
    ]
    got_sec_far = lax.ppermute(sec_far, "sec", between(sections))
    got_sec_near = lax.ppermute(sec_near, "sec", swap(sections))
    got_lon_far = lax.ppermute(
        lon_far, "lon", [(i, (i - 1 + 2 * (i % 2)) % lons) for i in range(lons)]
    )
    got_lon_near = lax.ppermute(lon_near, "lon", swap(lons))

    land = [moist_cond, heat_cond, rain, surface_flux, cell_reach]
    tables = [send_count, home, down, listed]
    order, ids, *land = call(
        index_body,
        [shape((blocks, LANES), I32), shape((pairs, PACK_ROWS, LANES), BF16)]
        + [shape(x.shape, x.dtype) for x in land],
        *tables, *land,
        ins=[HBM] * 9,
        scratch=[pltpu.SMEM(send_count.shape, I32)]
        + [pltpu.VMEM(x.shape, I32) for x in tables[1:]]
        + [dma((9,))],
        moved=moisture.size * 8,
    )
    moist_new, heat_new, keep, give = call(
        land_body,
        [
            shape(moisture.shape, F32),
            shape(heat.shape, F32),
            shape((pairs, blocks, LANES), F32),
            shape((pairs, blocks, LANES), BF16),
        ],
        moist_v, heat_v, *land,
        got_sec_near, got_sec_far, got_lon_near, got_lon_far,
        moved=moisture.size * 24,
    )
    got = lax.ppermute(give, "sec", swap(sections))
    aways = []
    for k in range(1, pairs // 2 + 1):
        aways += [k] if 2 * k == pairs else [pairs - k, k]
    pack_first = lambda rows, shifted: call(
        lambda *refs: first_body(aways[0], shifted, *refs),
        [shape((cap, steps), BF16)],
        order, rows,
        mib=12,
        flops=2 * cap * reaches * steps,
        moved=reaches * steps * 2,
    )[0]
    rec_packed = pack_first(records[0], True)
    own_terms, *terms = call(
        terms_body,
        [shape((blocks, LANES), F32)] + [shape((blocks + PACK_ROWS, LANES), BF16)] * (pairs - 1),
        keep, got, ids, rec_packed,
        moved=reaches * 8,
    )
    forward = lambda block, away: lax.ppermute(
        block, "sec", [(i, i ^ (2 * away)) for i in range(sections)]
    )
    terms = [forward(term, flip) for flip, term in zip(range(pairs - 1, 0, -1), terms)]
    hyd_packed = pack_first(unit_hydro[0], False)
    runoff, ready, places = call(
        lambda *refs: send_body(aways[0], *refs),
        [shape((blocks, LANES), F32), shape((cap, steps), BF16), shape(ids.shape, BF16)],
        own_terms, order, ids, rec_packed, hyd_packed, *terms,
        moved=cap * steps * 6,
    )
    arrived = {aways[0]: forward(ready, aways[0])}
    kept, *ready = call(
        lambda *refs: record_body(aways[1:], *refs),
        [shape((reaches, steps), BF16)] + [shape((cap, steps), BF16)] * (len(aways) - 1),
        runoff, records[0], unit_hydro[0], order,
        mib=16,
        flops=2 * cap * reaches * steps,
        moved=reaches * steps * 8,
    )
    for away, block in zip(aways[1:], ready):
        arrived[away] = forward(block, away)
    near, late = aways[0], aways[-1:]
    record_new, moist_out, heat_out, theirs, mine = call(
        lambda *refs: rest_body(near, *refs),
        [
            shape((reaches, steps), BF16),
            shape(moisture.shape, F32),
            shape(heat.shape, F32),
            shape((basins, steps), F32),
            shape((basins, steps), F32),
        ],
        order, kept, places, arrived[near], moist_new, heat_new,
        out_specs=[HBM] * 3 + [VMEM] * 2,
        scratch=[pltpu.VMEM((cap, steps), BF16), dma((3,))],
        mib=16,
        flops=2 * cap * reaches * steps,
        moved=reaches * steps * 4,
    )
    early = [a for a in aways[:-1] if a != near]
    theirs, mine = call(
        lambda *refs: early_body(early, *refs),
        [shape((basins, steps), F32), shape((basins, steps), F32)],
        theirs, mine, places, *[arrived[a] for a in early],
        mib=12,
        moved=basins * steps * 16,
    )
    parts = steps // LANES
    passed = []
    for part in range(parts):
        (sums,) = call(
            lambda *refs, part=part: late_body(late, True, part, *refs),
            [shape((basins, LANES), BF16)],
            theirs, places, *[arrived[a] for a in late],
            moved=basins * steps * 4,
        )
        passed.append(lax.ppermute(sums, "sec", swap(sections)))
    (mine,) = call(
        lambda *refs: late_body(late, False, 0, *refs),
        [shape((basins, steps), F32)],
        mine, places, *[arrived[a] for a in late],
        moved=basins * steps * 8,
    )
    (inflow,) = call(
        final_body,
        [shape((basins, steps), F32)],
        mine, *passed,
        out_specs=[HBM],
        scratch=[pltpu.VMEM((basins, steps), F32), dma((parts,))],
        moved=basins * steps * 10,
    )
    return (moist_out, heat_out, record_new[None], inflow[None])


def solution(mesh):
    placed = (
        P(None, "sec", "lon"),
        P(None, "sec", "lon"),
        P(None, "sec", "lon"),
        P(None, "sec", "lon"),
        P("sec", "lon"),
        P("sec", "lon"),
        P("sec", "lon"),
        P("lon", "sec", None),
        P("lon", "sec", None),
        P("lon", "sec"),
        P("lon", None),
        P("lon", "sec", None, None),
        P("lon", "sec", None),
    )
    return jax.shard_map(
        per_device,
        mesh=mesh,
        in_specs=placed,
        out_specs=(
            P(None, "sec", "lon"),
            P(None, "sec", "lon"),
            P("lon", "sec", None),
            P("lon", "sec", None),
        ),
        check_vma=False,
    )
```

```python
import jax
import jax.numpy as jnp
from jax import lax
from jax.experimental import pallas as pl
from jax.experimental.pallas import tpu as pltpu
from jax.sharding import PartitionSpec as P

LATERAL = 0.2
LANES = 128
PACK_ROWS = 16
F32 = jnp.float32
BF16 = jnp.bfloat16
I32 = jnp.int32
VMEM = pl.BlockSpec(memory_space=pltpu.VMEM)
HBM = pl.BlockSpec(memory_space=pltpu.HBM)


def call(body, outs, *args, ins=None, out_specs=None, scratch=(), mib=8, flops=0, moved=0):
    ins = list(ins) if ins else [VMEM] * len(args)
    args = [
        pltpu.with_memory_space_constraint(arg, pltpu.HBM) if spec is HBM else arg
        for arg, spec in zip(args, ins)
    ]
    return pl.pallas_call(
        body,
        out_shape=list(outs),
        in_specs=ins,
        out_specs=list(out_specs) if out_specs else [VMEM] * len(outs),
        scratch_shapes=list(scratch),
        compiler_params=pltpu.CompilerParams(vmem_limit_bytes=mib * 1024 * 1024),
        cost_estimate=pl.CostEstimate(flops=flops, bytes_accessed=moved, transcendentals=0),
    )(*args)


def fetch(sources, targets, sems):
    copies = [
        pltpu.make_async_copy(src, dst, sems.at[i])
        for i, (src, dst) in enumerate(zip(sources, targets))
    ]
    for copy in copies:
        copy.start()
    return copies


def parity(axis):
    return lax.rem(lax.axis_index(axis), 2)


def edges_body(*refs):
    count = 2
    targets = refs[count : 2 * count]
    moist, heat = targets[:2]
    sec_near, sec_far, lon_near, lon_far, sems = refs[2 * count :]
    copies = fetch(refs[:count], targets, sems)
    layers, rows, cols = moist.shape
    lane = lax.broadcasted_iota(I32, (rows, LANES), 1)
    west = jnp.zeros((rows, LANES), F32)
    east = jnp.zeros((rows, LANES), F32)
    sec_even = parity("sec") == 0
    for f, ref in enumerate((moist, heat)):
        copies[f].wait()
        north = ref[:, 0, :]
        south = ref[:, rows - 1, :]
        sec_near[f * layers : (f + 1) * layers, :] = jnp.where(sec_even, south, north).astype(BF16)
        sec_far[f * layers : (f + 1) * layers, :] = jnp.where(sec_even, north, south).astype(BF16)
        for layer in range(layers):
            k = f * layers + layer
            west = jnp.where(lane == k, ref[layer, :, 0:1], west)
            east = jnp.where(lane == k, ref[layer, :, cols - 1 : cols], east)
    lon_even = parity("lon") == 0
    lon_near[...] = jnp.where(lon_even, east, west).astype(BF16)
    lon_far[...] = jnp.where(lon_even, west, east).astype(BF16)
    for copy in copies[2:]:
        copy.wait()


def lookup(table, hi, lo):
    out = jnp.zeros(hi.shape, table.dtype)
    for row in range(table.shape[0]):
        line = jnp.broadcast_to(table[row : row + 1, :], hi.shape)
        got = jnp.take_along_axis(line, lo, axis=1)
        out = jnp.where(hi == row, got, out)
    return out


def index_body(*refs):
    count_in, home_in, down_in, listed_in = refs[:4]
    order, ids = refs[9:11]
    count, home, down, listed, sems = refs[16:]
    copies = fetch(refs[:9], (count, home, down, listed, *refs[11:16]), sems)
    pairs, width = listed.shape[0] // 2, listed.shape[1]
    tiles = width // LANES
    chip = lax.axis_index("sec") // 2
    chip_basins = home.shape[0] * LANES // pairs
    for copy in copies[:4]:
        copy.wait()
    slot = lookup(home[...], down[...] >> 7, down[...] & (LANES - 1))
    pos = lax.broadcasted_iota(I32, (1, width), 1)
    for m in range(pairs):
        c = count[0, 0, 2 * m]
        second = pltpu.roll(listed[2 * m + 1 : 2 * m + 2, :], lax.rem(c, width), 1)
        line = jnp.where(pos < c, listed[2 * m : 2 * m + 1, :], second)
        away = m ^ chip
        for t in range(tiles):
            order[pl.ds(away * tiles + t, 1), :] = line[:, t * LANES : (t + 1) * LANES]
    at = order[...]
    place = lookup(slot, at >> 7, at & (LANES - 1))
    pad = jnp.zeros((PACK_ROWS - 2 * tiles, LANES), F32)
    for away in range(pairs):
        m = away ^ chip
        mine = place[away * tiles : (away + 1) * tiles, :] - m * chip_basins
        ids[away] = jnp.concatenate(
            [(mine >> 8).astype(F32), (mine & 255).astype(F32), pad], axis=0
        ).astype(BF16)
    for copy in copies[4:]:
        copy.wait()


def shift_time(x):
    steps = x.shape[1]
    lane = lax.broadcasted_iota(I32, x.shape, 1)
    return jnp.where(lane == steps - 1, 0.0, pltpu.roll(x, steps - 1, 1))


def picked(order, away, tiles, reaches):
    turned = order[...].astype(F32).T
    lane = lax.broadcasted_iota(I32, (LANES, reaches), 1).astype(F32)
    parts = [
        jnp.where(lane == turned[:, t : t + 1], 1.0, 0.0).astype(BF16)
        for t in range(away * tiles, (away + 1) * tiles)
    ]
    return parts[0] if len(parts) == 1 else jnp.concatenate(parts, axis=0)


def first_body(away, order, records, hydro, rec_packed, hyd_packed):
    hot = picked(order, away, rec_packed.shape[0] // LANES, records.shape[0])
    rec = jnp.dot(hot, records[...], preferred_element_type=F32)
    rec_packed[...] = shift_time(rec).astype(BF16)
    hyd_packed[...] = jnp.dot(hot, hydro[...], preferred_element_type=F32).astype(BF16)


def land_body(
    moist, heat, moist_k, heat_k, rain, flux, cell, sec_near, sec_far, lon_near, lon_far,
    moist_out, heat_out, keep, give,
):
    layers, rows, cols = moist.shape
    row = lax.broadcasted_iota(I32, (rows, cols), 0)
    col = lax.broadcasted_iota(I32, (rows, cols), 1)
    sec_even = parity("sec") == 0
    lon_even = parity("lon") == 0
    outer = lambda axis: (lax.axis_index(axis) == 0) | (
        lax.axis_index(axis) == lax.axis_size(axis) - 1
    )
    sec_beyond = jnp.where(outer("sec"), 0.0, sec_far[...].astype(F32))
    lon_beyond = jnp.where(outer("lon"), 0.0, lon_far[...].astype(F32))
    south_all = jnp.where(sec_even, sec_near[...].astype(F32), sec_beyond)
    north_all = jnp.where(sec_even, sec_beyond, sec_near[...].astype(F32))
    east_all = jnp.where(lon_even, lon_near[...].astype(F32), lon_beyond)
    west_all = jnp.where(lon_even, lon_beyond, lon_near[...].astype(F32))
    for f, (x_ref, k_ref, top, out) in enumerate(
        ((moist, moist_k, rain, moist_out), (heat, heat_k, flux, heat_out))
    ):
        ratio = jnp.zeros((rows, cols), F32)
        value = jnp.zeros((rows, cols), F32)
        below = jnp.zeros((rows, cols), F32)
        ratios, values = [], []
        for layer in range(layers):
            k = f * layers + layer
            x = x_ref[layer]
            up = jnp.where(row == 0, north_all[k : k + 1, :], pltpu.roll(x, 1, 0))
            dn = jnp.where(row == rows - 1, south_all[k : k + 1, :], pltpu.roll(x, rows - 1, 0))
            lf = jnp.where(col == 0, west_all[:, k : k + 1], pltpu.roll(x, 1, 1))
            rt = jnp.where(col == cols - 1, east_all[:, k : k + 1], pltpu.roll(x, cols - 1, 1))
            rhs = x + LATERAL * (up + dn + lf + rt - 4.0 * x)
            if layer == 0:
                rhs = rhs + top[...]
            if layer < layers - 1:
                above = 0.5 * (k_ref[layer] + k_ref[layer + 1])
            else:
                above = jnp.zeros((rows, cols), F32)
            inv = 1.0 / (1.0 + below + above + below * ratio)
            ratio = -above * inv
            value = (rhs + below * value) * inv
            ratios.append(ratio)
            values.append(value)
            below = above
        x = values[-1]
        out[layers - 1] = x
        for layer in range(layers - 2, -1, -1):
            x = values[layer] - ratios[layer] * x
            out[layer] = x
    s = moist_out[0] - 1.0
    soft = jnp.maximum(s, 0.0) + jnp.log1p(jnp.exp(-jnp.abs(s)))
    gate = 1.0 / (1.0 + jnp.exp(-heat_out[0]))
    runoff = soft * gate + 0.5 * moist_k[layers - 1] * moist_out[layers - 1]
    cells = cell[...]
    hi = cells >> 7
    lo = cells & (LANES - 1)
    pairs, blocks = keep.shape[:2]
    his = 2 * pairs * blocks
    hi_iota = lax.broadcasted_iota(I32, (his, cols), 0)
    lo_iota = lax.broadcasted_iota(I32, (LANES, cols), 0)
    acc = jnp.zeros((his, LANES), F32)
    for i in range(rows):
        a = jnp.where(hi_iota == hi[i : i + 1, :], runoff[i : i + 1, :], 0.0).astype(BF16)
        b = jnp.where(lo_iota == lo[i : i + 1, :], 1.0, 0.0).astype(BF16)
        acc = acc + lax.dot_general(a, b, (((1,), (1,)), ((), ())), preferred_element_type=F32)
    both = acc.reshape(pairs, 2, blocks, LANES)
    keep[...] = jnp.where(sec_even, both[:, 0], both[:, 1])
    give[...] = jnp.where(sec_even, both[:, 1], both[:, 0]).astype(BF16)


def terms_body(keep, got, ids, own, *outs):
    pairs, blocks = keep.shape[:2]
    chip = lax.axis_index("sec") // 2
    own[...] = keep[chip] + got[chip].astype(F32)
    for flip, out in zip(range(len(outs), 0, -1), outs):
        m = chip ^ flip
        out[:blocks, :] = (keep[m] + got[m].astype(F32)).astype(BF16)
        out[blocks:, :] = ids[flip]


def send_body(away, own, order, ids, rec_packed, hyd_packed, *refs):
    terms, (runoff, ready, places) = refs[:-3], refs[-3:]
    places[0] = ids[0]
    for flip, term in zip(range(len(terms), 0, -1), terms):
        places[flip] = term[term.shape[0] - PACK_ROWS :, :]
    blocks = runoff.shape[0]
    tiles = ready.shape[0] // LANES
    total = own[...]
    for term in terms:
        total = total + term[:blocks, :].astype(F32)
    runoff[...] = total
    at = order[...]
    turned = lookup(total, at >> 7, at & (LANES - 1)).T
    for t in range(tiles):
        rows = pl.ds(t * LANES, LANES)
        col = away * tiles + t
        ready[rows, :] = (
            rec_packed[rows, :].astype(F32) + turned[:, col : col + 1] * hyd_packed[rows, :].astype(F32)
        ).astype(BF16)


def record_body(aways, runoff, records, hydro, order, kept, *ready):
    turned = runoff[...].T
    for t in range(runoff.shape[0]):
        rows = pl.ds(t * LANES, LANES)
        kept[rows, :] = (
            shift_time(records[rows, :].astype(F32)) + turned[:, t : t + 1] * hydro[rows, :].astype(F32)
        ).astype(BF16)
    for away, out in zip(aways, ready):
        hot = picked(order, away, out.shape[0] // LANES, kept.shape[0])
        out[...] = jnp.dot(hot, kept[...], preferred_element_type=F32).astype(BF16)


def hot_of(digits, tiles, basins, other):
    core = parity("sec")
    base = ((1 - core) if other else core) * basins
    slot = lax.broadcasted_iota(I32, (basins, LANES), 0) + base
    slot = slot.astype(F32)
    place = digits[:tiles] * 256.0 + digits[tiles : 2 * tiles]
    parts = [jnp.where(slot == place[t : t + 1, :], 1.0, 0.0).astype(BF16) for t in range(tiles)]
    return parts[0] if len(parts) == 1 else jnp.concatenate(parts, axis=1)


def summed(digits, blocks, basins, other):
    tiles = blocks[0].shape[0] // LANES
    total = None
    for digit, block in zip(digits, blocks):
        hot = hot_of(digit, tiles, basins, other)
        part = jnp.dot(hot, block[...], preferred_element_type=F32)
        total = part if total is None else total + part
    return total


def rest_body(
    near, order, kept, places, landed, moist, heat, out, moist_out, heat_out, theirs, mine, own, sems
):
    copies = fetch((kept, moist, heat), (out, moist_out, heat_out), sems)
    hot = picked(order, 0, own.shape[0] // LANES, kept.shape[0])
    own[...] = jnp.dot(hot, kept[...], preferred_element_type=F32).astype(BF16)
    digits = [places[away].astype(F32) for away in (0, near)]
    basins = mine.shape[0]
    theirs[...] = summed(digits, [own, landed], basins, True)
    mine[...] = summed(digits, [own, landed], basins, False)
    for copy in copies:
        copy.wait()


def early_body(aways, theirs_so_far, mine_so_far, places, *refs):
    blocks, (theirs, mine) = refs[:-2], refs[-2:]
    digits = [places[away].astype(F32) for away in aways]
    basins = mine.shape[0]
    theirs[...] = theirs_so_far[...] + summed(digits, blocks, basins, True)
    mine[...] = mine_so_far[...] + summed(digits, blocks, basins, False)


def late_body(aways, other, so_far, places, *refs):
    blocks, out = refs[:-1], refs[-1]
    digits = [places[away].astype(F32) for away in aways]
    out[...] = (so_far[...] + summed(digits, blocks, out.shape[0], other)).astype(out.dtype)


def final_body(mine, passed, out, held, sems):
    rows = mine.shape[0]
    parts = 2
    size = rows // parts
    copies = []
    for i in range(parts):
        at = pl.ds(i * size, size)
        held[at, :] = mine[at, :] + passed[at, :].astype(F32)
        copy = pltpu.make_async_copy(held.at[at, :], out.at[at, :], sems.at[i])
        copy.start()
        copies.append(copy)
    for copy in copies:
        copy.wait()


def per_device(
    moisture, heat, moist_cond, heat_cond, rain, surface_flux, cell_reach,
    records, unit_hydro, down_basin, basin_home, send_index, send_count,
):
    lons = lax.axis_size("lon")
    sections = lax.axis_size("sec")
    layers, lats, cols = moisture.shape
    reaches, steps = records.shape[1:]
    cap = send_index.shape[3]
    pairs = sections // 2
    basins = basin_home.shape[1] // sections
    blocks = reaches // LANES
    shape = jax.ShapeDtypeStruct
    dma = pltpu.SemaphoreType.DMA

    home = basin_home.reshape(-1, LANES)
    down = down_basin.reshape(-1, LANES)
    listed = send_index.reshape(sections, cap)
    moist_v, heat_v, sec_near, sec_far, lon_near, lon_far = call(
        edges_body,
        [
            shape(moisture.shape, F32),
            shape(heat.shape, F32),
            shape((2 * layers, cols), BF16),
            shape((2 * layers, cols), BF16),
            shape((lats, LANES), BF16),
            shape((lats, LANES), BF16),
        ],
        moisture, heat,
        ins=[HBM] * 2,
        scratch=[dma((2,))],
        moved=moisture.size * 8,
    )
    swap = lambda count: [(i, i ^ 1) for i in range(count)]
    between = lambda count: [(i, (i - 1 + 2 * (i % 2)) % count) for i in range(count)]
    got_sec_far = lax.ppermute(sec_far, "sec", between(sections))
    got_sec_near = lax.ppermute(sec_near, "sec", swap(sections))
    got_lon_far = lax.ppermute(lon_far, "lon", between(lons))
    got_lon_near = lax.ppermute(lon_near, "lon", swap(lons))

    land = [moist_cond, heat_cond, rain, surface_flux, cell_reach]
    tables = [send_count, home, down, listed]
    order, ids, *land = call(
        index_body,
        [shape((blocks, LANES), I32), shape((pairs, PACK_ROWS, LANES), BF16)]
        + [shape(x.shape, x.dtype) for x in land],
        *tables, *land,
        ins=[HBM] * 9,
        scratch=[pltpu.SMEM(send_count.shape, I32)]
        + [pltpu.VMEM(x.shape, I32) for x in tables[1:]]
        + [dma((9,))],
        moved=moisture.size * 8,
    )
    moist_new, heat_new, keep, give = call(
        land_body,
        [
            shape(moisture.shape, F32),
            shape(heat.shape, F32),
            shape((pairs, blocks, LANES), F32),
            shape((pairs, blocks, LANES), BF16),
        ],
        moist_v, heat_v, *land,
        got_sec_near, got_sec_far, got_lon_near, got_lon_far,
        moved=moisture.size * 24,
    )
    got = lax.ppermute(give, "sec", swap(sections))
    aways = []
    for k in range(1, pairs // 2 + 1):
        aways += [k] if 2 * k == pairs else [pairs - k, k]
    own_terms, *terms = call(
        terms_body,
        [shape((blocks, LANES), F32)] + [shape((blocks + PACK_ROWS, LANES), BF16)] * (pairs - 1),
        keep, got, ids,
        moved=reaches * 8,
    )
    forward = lambda block, away: lax.ppermute(
        block, "sec", [(i, i ^ (2 * away)) for i in range(sections)]
    )
    terms = [forward(term, flip) for flip, term in zip(range(pairs - 1, 0, -1), terms)]
    rec_packed, hyd_packed = call(
        lambda *refs: first_body(aways[0], *refs),
        [shape((cap, steps), BF16)] * 2,
        order, records[0], unit_hydro[0],
        mib=12,
        flops=4 * cap * reaches * steps,
        moved=reaches * steps * 4,
    )
    runoff, ready, places = call(
        lambda *refs: send_body(aways[0], *refs),
        [shape((blocks, LANES), F32), shape((cap, steps), BF16), shape(ids.shape, BF16)],
        own_terms, order, ids, rec_packed, hyd_packed, *terms,
        moved=cap * steps * 6,
    )
    arrived = {aways[0]: forward(ready, aways[0])}
    kept, *ready = call(
        lambda *refs: record_body(aways[1:], *refs),
        [shape((reaches, steps), BF16)] + [shape((cap, steps), BF16)] * (len(aways) - 1),
        runoff, records[0], unit_hydro[0], order,
        mib=16,
        flops=2 * cap * reaches * steps,
        moved=reaches * steps * 8,
    )
    for away, block in zip(aways[1:], ready):
        arrived[away] = forward(block, away)
    near, late = aways[0], aways[-1:]
    record_new, moist_out, heat_out, theirs, mine = call(
        lambda *refs: rest_body(near, *refs),
        [
            shape((reaches, steps), BF16),
            shape(moisture.shape, F32),
            shape(heat.shape, F32),
            shape((basins, steps), F32),
            shape((basins, steps), F32),
        ],
        order, kept, places, arrived[near], moist_new, heat_new,
        out_specs=[HBM] * 3 + [VMEM] * 2,
        scratch=[pltpu.VMEM((cap, steps), BF16), dma((3,))],
        mib=16,
        flops=2 * cap * reaches * steps,
        moved=reaches * steps * 4,
    )
    early = [a for a in aways[:-1] if a != near]
    theirs, mine = call(
        lambda *refs: early_body(early, *refs),
        [shape((basins, steps), F32), shape((basins, steps), F32)],
        theirs, mine, places, *[arrived[a] for a in early],
        mib=12,
        moved=basins * steps * 16,
    )
    (theirs,) = call(
        lambda *refs: late_body(late, True, *refs),
        [shape((basins, steps), BF16)],
        theirs, places, *[arrived[a] for a in late],
        moved=basins * steps * 8,
    )
    passed = lax.ppermute(theirs, "sec", swap(sections))
    (mine,) = call(
        lambda *refs: late_body(late, False, *refs),
        [shape((basins, steps), F32)],
        mine, places, *[arrived[a] for a in late],
        moved=basins * steps * 8,
    )
    (inflow,) = call(
        final_body,
        [shape((basins, steps), F32)],
        mine, passed,
        out_specs=[HBM],
        scratch=[pltpu.VMEM((basins, steps), F32), dma((2,))],
        moved=basins * steps * 10,
    )
    return (moist_out, heat_out, record_new[None], inflow[None])


def solution(mesh):
    placed = (
        P(None, "sec", "lon"),
        P(None, "sec", "lon"),
        P(None, "sec", "lon"),
        P(None, "sec", "lon"),
        P("sec", "lon"),
        P("sec", "lon"),
        P("sec", "lon"),
        P("lon", "sec", None),
        P("lon", "sec", None),
        P("lon", "sec"),
        P("lon", None),
        P("lon", "sec", None, None),
        P("lon", "sec", None),
    )
    return jax.shard_map(
        per_device,
        mesh=mesh,
        in_specs=placed,
        out_specs=(
            P(None, "sec", "lon"),
            P(None, "sec", "lon"),
            P("lon", "sec", None),
            P("lon", "sec", None),
        ),
        check_vma=False,
    )
```

```python
import jax
import jax.numpy as jnp
from jax import lax
from jax.experimental import pallas as pl
from jax.experimental.pallas import tpu as pltpu
from jax.sharding import PartitionSpec as P

LATERAL = 0.2
LANES = 128
PACK_ROWS = 16
F32 = jnp.float32
BF16 = jnp.bfloat16
I32 = jnp.int32
VMEM = pl.BlockSpec(memory_space=pltpu.VMEM)
HBM = pl.BlockSpec(memory_space=pltpu.HBM)


def call(body, outs, *args, ins=None, out_specs=None, scratch=(), mib=8, flops=0, moved=0):
    ins = list(ins) if ins else [VMEM] * len(args)
    args = [
        pltpu.with_memory_space_constraint(arg, pltpu.HBM) if spec is HBM else arg
        for arg, spec in zip(args, ins)
    ]
    return pl.pallas_call(
        body,
        out_shape=list(outs),
        in_specs=ins,
        out_specs=list(out_specs) if out_specs else [VMEM] * len(outs),
        scratch_shapes=list(scratch),
        compiler_params=pltpu.CompilerParams(vmem_limit_bytes=mib * 1024 * 1024),
        cost_estimate=pl.CostEstimate(flops=flops, bytes_accessed=moved, transcendentals=0),
    )(*args)


def fetch(sources, targets, sems):
    copies = [
        pltpu.make_async_copy(src, dst, sems.at[i])
        for i, (src, dst) in enumerate(zip(sources, targets))
    ]
    for copy in copies:
        copy.start()
    return copies


def parity(axis):
    return lax.rem(lax.axis_index(axis), 2)


def edges_body(*refs):
    count = 2
    targets = refs[count : 2 * count]
    moist, heat = targets[:2]
    sec_near, sec_far, lon_near, lon_far, sems = refs[2 * count :]
    copies = fetch(refs[:count], targets, sems)
    layers, rows, cols = moist.shape
    lane = lax.broadcasted_iota(I32, (rows, LANES), 1)
    west = jnp.zeros((rows, LANES), F32)
    east = jnp.zeros((rows, LANES), F32)
    sec_even = parity("sec") == 0
    for f, ref in enumerate((moist, heat)):
        copies[f].wait()
        north = ref[:, 0, :]
        south = ref[:, rows - 1, :]
        sec_near[f * layers : (f + 1) * layers, :] = jnp.where(sec_even, south, north).astype(BF16)
        sec_far[f * layers : (f + 1) * layers, :] = jnp.where(sec_even, north, south).astype(BF16)
        for layer in range(layers):
            k = f * layers + layer
            west = jnp.where(lane == k, ref[layer, :, 0:1], west)
            east = jnp.where(lane == k, ref[layer, :, cols - 1 : cols], east)
    lon_even = parity("lon") == 0
    lon_near[...] = jnp.where(lon_even, east, west).astype(BF16)
    lon_far[...] = jnp.where(lon_even, west, east).astype(BF16)
    for copy in copies[2:]:
        copy.wait()


def lookup(table, hi, lo):
    out = jnp.zeros(hi.shape, table.dtype)
    for row in range(table.shape[0]):
        line = jnp.broadcast_to(table[row : row + 1, :], hi.shape)
        got = jnp.take_along_axis(line, lo, axis=1)
        out = jnp.where(hi == row, got, out)
    return out


def index_body(*refs):
    count_in, home_in, down_in, listed_in = refs[:4]
    order, ids = refs[9:11]
    count, home, down, listed, sems = refs[16:]
    copies = fetch(refs[:9], (count, home, down, listed, *refs[11:16]), sems)
    pairs, width = listed.shape[0] // 2, listed.shape[1]
    tiles = width // LANES
    chip = lax.axis_index("sec") // 2
    chip_basins = home.shape[0] * LANES // pairs
    for copy in copies[:4]:
        copy.wait()
    slot = lookup(home[...], down[...] >> 7, down[...] & (LANES - 1))
    pos = lax.broadcasted_iota(I32, (1, width), 1)
    for m in range(pairs):
        c = count[0, 0, 2 * m]
        second = pltpu.roll(listed[2 * m + 1 : 2 * m + 2, :], lax.rem(c, width), 1)
        line = jnp.where(pos < c, listed[2 * m : 2 * m + 1, :], second)
        away = m ^ chip
        for t in range(tiles):
            order[pl.ds(away * tiles + t, 1), :] = line[:, t * LANES : (t + 1) * LANES]
    at = order[...]
    place = lookup(slot, at >> 7, at & (LANES - 1))
    pad = jnp.zeros((PACK_ROWS - 2 * tiles, LANES), F32)
    for away in range(pairs):
        m = away ^ chip
        mine = place[away * tiles : (away + 1) * tiles, :] - m * chip_basins
        ids[away] = jnp.concatenate(
            [(mine >> 8).astype(F32), (mine & 255).astype(F32), pad], axis=0
        ).astype(BF16)
    for copy in copies[4:]:
        copy.wait()


def shift_time(x):
    steps = x.shape[1]
    lane = lax.broadcasted_iota(I32, x.shape, 1)
    return jnp.where(lane == steps - 1, 0.0, pltpu.roll(x, steps - 1, 1))


def picked(order, away, tiles, reaches):
    turned = order[...].astype(F32).T
    lane = lax.broadcasted_iota(I32, (LANES, reaches), 1).astype(F32)
    parts = [
        jnp.where(lane == turned[:, t : t + 1], 1.0, 0.0).astype(BF16)
        for t in range(away * tiles, (away + 1) * tiles)
    ]
    return parts[0] if len(parts) == 1 else jnp.concatenate(parts, axis=0)


def first_body(away, shifted, order, rows, packed):
    hot = picked(order, away, packed.shape[0] // LANES, rows.shape[0])
    out = jnp.dot(hot, rows[...], preferred_element_type=F32)
    packed[...] = (shift_time(out) if shifted else out).astype(BF16)


def land_body(
    moist, heat, moist_k, heat_k, rain, flux, cell, sec_near, sec_far, lon_near, lon_far,
    moist_out, heat_out, keep, give,
):
    layers, rows, cols = moist.shape
    row = lax.broadcasted_iota(I32, (rows, cols), 0)
    col = lax.broadcasted_iota(I32, (rows, cols), 1)
    sec_even = parity("sec") == 0
    lon_even = parity("lon") == 0
    outer = lambda axis: (lax.axis_index(axis) == 0) | (
        lax.axis_index(axis) == lax.axis_size(axis) - 1
    )
    sec_beyond = jnp.where(outer("sec"), 0.0, sec_far[...].astype(F32))
    lon_beyond = jnp.where(outer("lon"), 0.0, lon_far[...].astype(F32))
    south_all = jnp.where(sec_even, sec_near[...].astype(F32), sec_beyond)
    north_all = jnp.where(sec_even, sec_beyond, sec_near[...].astype(F32))
    east_all = jnp.where(lon_even, lon_near[...].astype(F32), lon_beyond)
    west_all = jnp.where(lon_even, lon_beyond, lon_near[...].astype(F32))
    for f, (x_ref, k_ref, top, out) in enumerate(
        ((moist, moist_k, rain, moist_out), (heat, heat_k, flux, heat_out))
    ):
        ratio = jnp.zeros((rows, cols), F32)
        value = jnp.zeros((rows, cols), F32)
        below = jnp.zeros((rows, cols), F32)
        ratios, values = [], []
        for layer in range(layers):
            k = f * layers + layer
            x = x_ref[layer]
            up = jnp.where(row == 0, north_all[k : k + 1, :], pltpu.roll(x, 1, 0))
            dn = jnp.where(row == rows - 1, south_all[k : k + 1, :], pltpu.roll(x, rows - 1, 0))
            lf = jnp.where(col == 0, west_all[:, k : k + 1], pltpu.roll(x, 1, 1))
            rt = jnp.where(col == cols - 1, east_all[:, k : k + 1], pltpu.roll(x, cols - 1, 1))
            rhs = x + LATERAL * (up + dn + lf + rt - 4.0 * x)
            if layer == 0:
                rhs = rhs + top[...]
            if layer < layers - 1:
                above = 0.5 * (k_ref[layer] + k_ref[layer + 1])
            else:
                above = jnp.zeros((rows, cols), F32)
            inv = 1.0 / (1.0 + below + above + below * ratio)
            ratio = -above * inv
            value = (rhs + below * value) * inv
            ratios.append(ratio)
            values.append(value)
            below = above
        x = values[-1]
        out[layers - 1] = x
        for layer in range(layers - 2, -1, -1):
            x = values[layer] - ratios[layer] * x
            out[layer] = x
    s = moist_out[0] - 1.0
    soft = jnp.maximum(s, 0.0) + jnp.log1p(jnp.exp(-jnp.abs(s)))
    gate = 1.0 / (1.0 + jnp.exp(-heat_out[0]))
    runoff = soft * gate + 0.5 * moist_k[layers - 1] * moist_out[layers - 1]
    cells = cell[...]
    hi = cells >> 7
    lo = cells & (LANES - 1)
    pairs, blocks = keep.shape[:2]
    his = 2 * pairs * blocks
    hi_iota = lax.broadcasted_iota(I32, (his, cols), 0)
    lo_iota = lax.broadcasted_iota(I32, (LANES, cols), 0)
    acc = jnp.zeros((his, LANES), F32)
    for i in range(rows):
        a = jnp.where(hi_iota == hi[i : i + 1, :], runoff[i : i + 1, :], 0.0).astype(BF16)
        b = jnp.where(lo_iota == lo[i : i + 1, :], 1.0, 0.0).astype(BF16)
        acc = acc + lax.dot_general(a, b, (((1,), (1,)), ((), ())), preferred_element_type=F32)
    both = acc.reshape(pairs, 2, blocks, LANES)
    keep[...] = jnp.where(sec_even, both[:, 0], both[:, 1])
    give[...] = jnp.where(sec_even, both[:, 1], both[:, 0]).astype(BF16)


def terms_body(keep, got, ids, packed, own, *outs):
    pairs, blocks = keep.shape[:2]
    chip = lax.axis_index("sec") // 2
    own[...] = keep[chip] + got[chip].astype(F32)
    for flip, out in zip(range(len(outs), 0, -1), outs):
        m = chip ^ flip
        out[:blocks, :] = (keep[m] + got[m].astype(F32)).astype(BF16)
        out[blocks:, :] = ids[flip]


def send_body(away, own, order, ids, rec_packed, hyd_packed, *refs):
    terms, (runoff, ready, places) = refs[:-3], refs[-3:]
    places[0] = ids[0]
    for flip, term in zip(range(len(terms), 0, -1), terms):
        places[flip] = term[term.shape[0] - PACK_ROWS :, :]
    blocks = runoff.shape[0]
    tiles = ready.shape[0] // LANES
    total = own[...]
    for term in terms:
        total = total + term[:blocks, :].astype(F32)
    runoff[...] = total
    at = order[...]
    turned = lookup(total, at >> 7, at & (LANES - 1)).T
    for t in range(tiles):
        rows = pl.ds(t * LANES, LANES)
        col = away * tiles + t
        ready[rows, :] = (
            rec_packed[rows, :].astype(F32) + turned[:, col : col + 1] * hyd_packed[rows, :].astype(F32)
        ).astype(BF16)


def record_body(aways, runoff, records, hydro, order, kept, *ready):
    turned = runoff[...].T
    for t in range(runoff.shape[0]):
        rows = pl.ds(t * LANES, LANES)
        kept[rows, :] = (
            shift_time(records[rows, :].astype(F32)) + turned[:, t : t + 1] * hydro[rows, :].astype(F32)
        ).astype(BF16)
    for away, out in zip(aways, ready):
        hot = picked(order, away, out.shape[0] // LANES, kept.shape[0])
        out[...] = jnp.dot(hot, kept[...], preferred_element_type=F32).astype(BF16)


def hot_of(digits, tiles, basins, other):
    core = parity("sec")
    base = ((1 - core) if other else core) * basins
    slot = lax.broadcasted_iota(I32, (basins, LANES), 0) + base
    slot = slot.astype(F32)
    place = digits[:tiles] * 256.0 + digits[tiles : 2 * tiles]
    parts = [jnp.where(slot == place[t : t + 1, :], 1.0, 0.0).astype(BF16) for t in range(tiles)]
    return parts[0] if len(parts) == 1 else jnp.concatenate(parts, axis=1)


def summed(digits, blocks, basins, other):
    tiles = blocks[0].shape[0] // LANES
    total = None
    for digit, block in zip(digits, blocks):
        hot = hot_of(digit, tiles, basins, other)
        part = jnp.dot(hot, block[...], preferred_element_type=F32)
        total = part if total is None else total + part
    return total


def rest_body(
    near, order, kept, places, landed, moist, heat, out, moist_out, heat_out, theirs, mine, own, sems
):
    copies = fetch((kept, moist, heat), (out, moist_out, heat_out), sems)
    hot = picked(order, 0, own.shape[0] // LANES, kept.shape[0])
    own[...] = jnp.dot(hot, kept[...], preferred_element_type=F32).astype(BF16)
    digits = [places[away].astype(F32) for away in (0, near)]
    basins = mine.shape[0]
    theirs[...] = summed(digits, [own, landed], basins, True)
    mine[...] = summed(digits, [own, landed], basins, False)
    for copy in copies:
        copy.wait()


def early_body(aways, theirs_so_far, mine_so_far, places, *refs):
    blocks, (theirs, mine) = refs[:-2], refs[-2:]
    digits = [places[away].astype(F32) for away in aways]
    basins = mine.shape[0]
    theirs[...] = theirs_so_far[...] + summed(digits, blocks, basins, True)
    mine[...] = mine_so_far[...] + summed(digits, blocks, basins, False)


def late_body(aways, other, so_far, places, *refs):
    blocks, out = refs[:-1], refs[-1]
    digits = [places[away].astype(F32) for away in aways]
    out[...] = (so_far[...] + summed(digits, blocks, out.shape[0], other)).astype(out.dtype)


def final_body(mine, passed, out, held, sems):
    rows = mine.shape[0]
    parts = 2
    size = rows // parts
    copies = []
    for i in range(parts):
        at = pl.ds(i * size, size)
        held[at, :] = mine[at, :] + passed[at, :].astype(F32)
        copy = pltpu.make_async_copy(held.at[at, :], out.at[at, :], sems.at[i])
        copy.start()
        copies.append(copy)
    for copy in copies:
        copy.wait()


def per_device(
    moisture, heat, moist_cond, heat_cond, rain, surface_flux, cell_reach,
    records, unit_hydro, down_basin, basin_home, send_index, send_count,
):
    lons = lax.axis_size("lon")
    sections = lax.axis_size("sec")
    layers, lats, cols = moisture.shape
    reaches, steps = records.shape[1:]
    cap = send_index.shape[3]
    pairs = sections // 2
    basins = basin_home.shape[1] // sections
    blocks = reaches // LANES
    shape = jax.ShapeDtypeStruct
    dma = pltpu.SemaphoreType.DMA

    home = basin_home.reshape(-1, LANES)
    down = down_basin.reshape(-1, LANES)
    listed = send_index.reshape(sections, cap)
    moist_v, heat_v, sec_near, sec_far, lon_near, lon_far = call(
        edges_body,
        [
            shape(moisture.shape, F32),
            shape(heat.shape, F32),
            shape((2 * layers, cols), BF16),
            shape((2 * layers, cols), BF16),
            shape((lats, LANES), BF16),
            shape((lats, LANES), BF16),
        ],
        moisture, heat,
        ins=[HBM] * 2,
        scratch=[dma((2,))],
        moved=moisture.size * 8,
    )
    swap = lambda count: [(i, i ^ 1) for i in range(count)]
    between = lambda count: [(i, (i - 1 + 2 * (i % 2)) % count) for i in range(count)]
    got_sec_far = lax.ppermute(sec_far, "sec", between(sections))
    got_sec_near = lax.ppermute(sec_near, "sec", swap(sections))
    got_lon_far = lax.ppermute(lon_far, "lon", between(lons))
    got_lon_near = lax.ppermute(lon_near, "lon", swap(lons))

    land = [moist_cond, heat_cond, rain, surface_flux, cell_reach]
    tables = [send_count, home, down, listed]
    order, ids, *land = call(
        index_body,
        [shape((blocks, LANES), I32), shape((pairs, PACK_ROWS, LANES), BF16)]
        + [shape(x.shape, x.dtype) for x in land],
        *tables, *land,
        ins=[HBM] * 9,
        scratch=[pltpu.SMEM(send_count.shape, I32)]
        + [pltpu.VMEM(x.shape, I32) for x in tables[1:]]
        + [dma((9,))],
        moved=moisture.size * 8,
    )
    moist_new, heat_new, keep, give = call(
        land_body,
        [
            shape(moisture.shape, F32),
            shape(heat.shape, F32),
            shape((pairs, blocks, LANES), F32),
            shape((pairs, blocks, LANES), BF16),
        ],
        moist_v, heat_v, *land,
        got_sec_near, got_sec_far, got_lon_near, got_lon_far,
        moved=moisture.size * 24,
    )
    got = lax.ppermute(give, "sec", swap(sections))
    aways = []
    for k in range(1, pairs // 2 + 1):
        aways += [k] if 2 * k == pairs else [pairs - k, k]
    pack_first = lambda rows, shifted: call(
        lambda *refs: first_body(aways[0], shifted, *refs),
        [shape((cap, steps), BF16)],
        order, rows,
        mib=12,
        flops=2 * cap * reaches * steps,
        moved=reaches * steps * 2,
    )[0]
    rec_packed = pack_first(records[0], True)
    own_terms, *terms = call(
        terms_body,
        [shape((blocks, LANES), F32)] + [shape((blocks + PACK_ROWS, LANES), BF16)] * (pairs - 1),
        keep, got, ids, rec_packed,
        moved=reaches * 8,
    )
    forward = lambda block, away: lax.ppermute(
        block, "sec", [(i, i ^ (2 * away)) for i in range(sections)]
    )
    terms = [forward(term, flip) for flip, term in zip(range(pairs - 1, 0, -1), terms)]
    hyd_packed = pack_first(unit_hydro[0], False)
    runoff, ready, places = call(
        lambda *refs: send_body(aways[0], *refs),
        [shape((blocks, LANES), F32), shape((cap, steps), BF16), shape(ids.shape, BF16)],
        own_terms, order, ids, rec_packed, hyd_packed, *terms,
        moved=cap * steps * 6,
    )
    arrived = {aways[0]: forward(ready, aways[0])}
    kept, *ready = call(
        lambda *refs: record_body(aways[1:], *refs),
        [shape((reaches, steps), BF16)] + [shape((cap, steps), BF16)] * (len(aways) - 1),
        runoff, records[0], unit_hydro[0], order,
        mib=16,
        flops=2 * cap * reaches * steps,
        moved=reaches * steps * 8,
    )
    for away, block in zip(aways[1:], ready):
        arrived[away] = forward(block, away)
    near, late = aways[0], aways[-1:]
    record_new, moist_out, heat_out, theirs, mine = call(
        lambda *refs: rest_body(near, *refs),
        [
            shape((reaches, steps), BF16),
            shape(moisture.shape, F32),
            shape(heat.shape, F32),
            shape((basins, steps), F32),
            shape((basins, steps), F32),
        ],
        order, kept, places, arrived[near], moist_new, heat_new,
        out_specs=[HBM] * 3 + [VMEM] * 2,
        scratch=[pltpu.VMEM((cap, steps), BF16), dma((3,))],
        mib=16,
        flops=2 * cap * reaches * steps,
        moved=reaches * steps * 4,
    )
    early = [a for a in aways[:-1] if a != near]
    theirs, mine = call(
        lambda *refs: early_body(early, *refs),
        [shape((basins, steps), F32), shape((basins, steps), F32)],
        theirs, mine, places, *[arrived[a] for a in early],
        mib=12,
        moved=basins * steps * 16,
    )
    (theirs,) = call(
        lambda *refs: late_body(late, True, *refs),
        [shape((basins, steps), BF16)],
        theirs, places, *[arrived[a] for a in late],
        moved=basins * steps * 8,
    )
    passed = lax.ppermute(theirs, "sec", swap(sections))
    (mine,) = call(
        lambda *refs: late_body(late, False, *refs),
        [shape((basins, steps), F32)],
        mine, places, *[arrived[a] for a in late],
        moved=basins * steps * 8,
    )
    (inflow,) = call(
        final_body,
        [shape((basins, steps), F32)],
        mine, passed,
        out_specs=[HBM],
        scratch=[pltpu.VMEM((basins, steps), F32), dma((2,))],
        moved=basins * steps * 10,
    )
    return (moist_out, heat_out, record_new[None], inflow[None])


def solution(mesh):
    placed = (
        P(None, "sec", "lon"),
        P(None, "sec", "lon"),
        P(None, "sec", "lon"),
        P(None, "sec", "lon"),
        P("sec", "lon"),
        P("sec", "lon"),
        P("sec", "lon"),
        P("lon", "sec", None),
        P("lon", "sec", None),
        P("lon", "sec"),
        P("lon", None),
        P("lon", "sec", None, None),
        P("lon", "sec", None),
    )
    return jax.shard_map(
        per_device,
        mesh=mesh,
        in_specs=placed,
        out_specs=(
            P(None, "sec", "lon"),
            P(None, "sec", "lon"),
            P("lon", "sec", None),
            P("lon", "sec", None),
        ),
        check_vma=False,
    )
```

```python
import jax
import jax.numpy as jnp
from jax import lax
from jax.experimental import pallas as pl
from jax.experimental.pallas import tpu as pltpu
from jax.sharding import PartitionSpec as P

LATERAL = 0.2
LANES = 128
PACK_ROWS = 16
F32 = jnp.float32
BF16 = jnp.bfloat16
I32 = jnp.int32
VMEM = pl.BlockSpec(memory_space=pltpu.VMEM)
HBM = pl.BlockSpec(memory_space=pltpu.HBM)


def call(body, outs, *args, ins=None, out_specs=None, scratch=(), mib=8, flops=0, moved=0):
    ins = list(ins) if ins else [VMEM] * len(args)
    args = [
        pltpu.with_memory_space_constraint(arg, pltpu.HBM) if spec is HBM else arg
        for arg, spec in zip(args, ins)
    ]
    return pl.pallas_call(
        body,
        out_shape=list(outs),
        in_specs=ins,
        out_specs=list(out_specs) if out_specs else [VMEM] * len(outs),
        scratch_shapes=list(scratch),
        compiler_params=pltpu.CompilerParams(vmem_limit_bytes=mib * 1024 * 1024),
        cost_estimate=pl.CostEstimate(flops=flops, bytes_accessed=moved, transcendentals=0),
    )(*args)


def fetch(sources, targets, sems):
    copies = [
        pltpu.make_async_copy(src, dst, sems.at[i])
        for i, (src, dst) in enumerate(zip(sources, targets))
    ]
    for copy in copies:
        copy.start()
    return copies


def parity(axis):
    return lax.rem(lax.axis_index(axis), 2)


def edges_body(*refs):
    count = 2
    targets = refs[count : 2 * count]
    moist, heat = targets[:2]
    sec_near, sec_far, lon_near, lon_far, sems = refs[2 * count :]
    copies = fetch(refs[:count], targets, sems)
    layers, rows, cols = moist.shape
    lane = lax.broadcasted_iota(I32, (rows, LANES), 1)
    west = jnp.zeros((rows, LANES), F32)
    east = jnp.zeros((rows, LANES), F32)
    sec_even = parity("sec") == 0
    for f, ref in enumerate((moist, heat)):
        copies[f].wait()
        north = ref[:, 0, :]
        south = ref[:, rows - 1, :]
        sec_near[f * layers : (f + 1) * layers, :] = jnp.where(sec_even, south, north).astype(BF16)
        sec_far[f * layers : (f + 1) * layers, :] = jnp.where(sec_even, north, south).astype(BF16)
        for layer in range(layers):
            k = f * layers + layer
            west = jnp.where(lane == k, ref[layer, :, 0:1], west)
            east = jnp.where(lane == k, ref[layer, :, cols - 1 : cols], east)
    lon_even = parity("lon") == 0
    lon_near[...] = jnp.where(lon_even, east, west).astype(BF16)
    lon_far[...] = jnp.where(lon_even, west, east).astype(BF16)
    for copy in copies[2:]:
        copy.wait()


def lookup(table, hi, lo):
    out = jnp.zeros(hi.shape, table.dtype)
    for row in range(table.shape[0]):
        line = jnp.broadcast_to(table[row : row + 1, :], hi.shape)
        got = jnp.take_along_axis(line, lo, axis=1)
        out = jnp.where(hi == row, got, out)
    return out


def index_body(*refs):
    count_in, home_in, down_in, listed_in = refs[:4]
    order, ids = refs[9:11]
    count, home, down, listed, sems = refs[16:]
    copies = fetch(refs[:9], (count, home, down, listed, *refs[11:16]), sems)
    pairs, width = listed.shape[0] // 2, listed.shape[1]
    tiles = width // LANES
    chip = lax.axis_index("sec") // 2
    chip_basins = home.shape[0] * LANES // pairs
    for copy in copies[:4]:
        copy.wait()
    slot = lookup(home[...], down[...] >> 7, down[...] & (LANES - 1))
    pos = lax.broadcasted_iota(I32, (1, width), 1)
    for m in range(pairs):
        c = count[0, 0, 2 * m]
        second = pltpu.roll(listed[2 * m + 1 : 2 * m + 2, :], lax.rem(c, width), 1)
        line = jnp.where(pos < c, listed[2 * m : 2 * m + 1, :], second)
        away = m ^ chip
        for t in range(tiles):
            order[pl.ds(away * tiles + t, 1), :] = line[:, t * LANES : (t + 1) * LANES]
    at = order[...]
    place = lookup(slot, at >> 7, at & (LANES - 1))
    pad = jnp.zeros((PACK_ROWS - 2 * tiles, LANES), F32)
    for away in range(pairs):
        m = away ^ chip
        mine = place[away * tiles : (away + 1) * tiles, :] - m * chip_basins
        ids[away] = jnp.concatenate(
            [(mine >> 8).astype(F32), (mine & 255).astype(F32), pad], axis=0
        ).astype(BF16)
    for copy in copies[4:]:
        copy.wait()


def shift_time(x):
    steps = x.shape[1]
    lane = lax.broadcasted_iota(I32, x.shape, 1)
    return jnp.where(lane == steps - 1, 0.0, pltpu.roll(x, steps - 1, 1))


def picked(order, away, tiles, reaches):
    turned = order[...].astype(F32).T
    lane = lax.broadcasted_iota(I32, (LANES, reaches), 1).astype(F32)
    parts = [
        jnp.where(lane == turned[:, t : t + 1], 1.0, 0.0).astype(BF16)
        for t in range(away * tiles, (away + 1) * tiles)
    ]
    return parts[0] if len(parts) == 1 else jnp.concatenate(parts, axis=0)


def first_body(away, order, records, hydro, rec_packed, hyd_packed):
    hot = picked(order, away, rec_packed.shape[0] // LANES, records.shape[0])
    rec = jnp.dot(hot, records[...], preferred_element_type=F32)
    rec_packed[...] = shift_time(rec).astype(BF16)
    hyd_packed[...] = jnp.dot(hot, hydro[...], preferred_element_type=F32).astype(BF16)


def land_body(
    moist, heat, moist_k, heat_k, rain, flux, cell, sec_near, sec_far, lon_near, lon_far,
    moist_out, heat_out, keep, give,
):
    layers, rows, cols = moist.shape
    row = lax.broadcasted_iota(I32, (rows, cols), 0)
    col = lax.broadcasted_iota(I32, (rows, cols), 1)
    sec_even = parity("sec") == 0
    lon_even = parity("lon") == 0
    outer = lambda axis: (lax.axis_index(axis) == 0) | (
        lax.axis_index(axis) == lax.axis_size(axis) - 1
    )
    sec_beyond = jnp.where(outer("sec"), 0.0, sec_far[...].astype(F32))
    lon_beyond = jnp.where(outer("lon"), 0.0, lon_far[...].astype(F32))
    south_all = jnp.where(sec_even, sec_near[...].astype(F32), sec_beyond)
    north_all = jnp.where(sec_even, sec_beyond, sec_near[...].astype(F32))
    east_all = jnp.where(lon_even, lon_near[...].astype(F32), lon_beyond)
    west_all = jnp.where(lon_even, lon_beyond, lon_near[...].astype(F32))
    for f, (x_ref, k_ref, top, out) in enumerate(
        ((moist, moist_k, rain, moist_out), (heat, heat_k, flux, heat_out))
    ):
        ratio = jnp.zeros((rows, cols), F32)
        value = jnp.zeros((rows, cols), F32)
        below = jnp.zeros((rows, cols), F32)
        ratios, values = [], []
        for layer in range(layers):
            k = f * layers + layer
            x = x_ref[layer]
            up = jnp.where(row == 0, north_all[k : k + 1, :], pltpu.roll(x, 1, 0))
            dn = jnp.where(row == rows - 1, south_all[k : k + 1, :], pltpu.roll(x, rows - 1, 0))
            lf = jnp.where(col == 0, west_all[:, k : k + 1], pltpu.roll(x, 1, 1))
            rt = jnp.where(col == cols - 1, east_all[:, k : k + 1], pltpu.roll(x, cols - 1, 1))
            rhs = x + LATERAL * (up + dn + lf + rt - 4.0 * x)
            if layer == 0:
                rhs = rhs + top[...]
            if layer < layers - 1:
                above = 0.5 * (k_ref[layer] + k_ref[layer + 1])
            else:
                above = jnp.zeros((rows, cols), F32)
            inv = 1.0 / (1.0 + below + above + below * ratio)
            ratio = -above * inv
            value = (rhs + below * value) * inv
            ratios.append(ratio)
            values.append(value)
            below = above
        x = values[-1]
        out[layers - 1] = x
        for layer in range(layers - 2, -1, -1):
            x = values[layer] - ratios[layer] * x
            out[layer] = x
    s = moist_out[0] - 1.0
    soft = jnp.maximum(s, 0.0) + jnp.log1p(jnp.exp(-jnp.abs(s)))
    gate = 1.0 / (1.0 + jnp.exp(-heat_out[0]))
    runoff = soft * gate + 0.5 * moist_k[layers - 1] * moist_out[layers - 1]
    cells = cell[...]
    hi = cells >> 7
    lo = cells & (LANES - 1)
    pairs, blocks = keep.shape[:2]
    his = 2 * pairs * blocks
    hi_iota = lax.broadcasted_iota(I32, (his, cols), 0)
    lo_iota = lax.broadcasted_iota(I32, (LANES, cols), 0)
    acc = jnp.zeros((his, LANES), F32)
    for i in range(rows):
        a = jnp.where(hi_iota == hi[i : i + 1, :], runoff[i : i + 1, :], 0.0).astype(BF16)
        b = jnp.where(lo_iota == lo[i : i + 1, :], 1.0, 0.0).astype(BF16)
        acc = acc + lax.dot_general(a, b, (((1,), (1,)), ((), ())), preferred_element_type=F32)
    both = acc.reshape(pairs, 2, blocks, LANES)
    keep[...] = jnp.where(sec_even, both[:, 0], both[:, 1])
    give[...] = jnp.where(sec_even, both[:, 1], both[:, 0]).astype(BF16)


def terms_body(keep, got, ids, own, *outs):
    pairs, blocks = keep.shape[:2]
    chip = lax.axis_index("sec") // 2
    own[...] = keep[chip] + got[chip].astype(F32)
    for flip, out in enumerate(outs, 1):
        m = chip ^ flip
        out[:blocks, :] = (keep[m] + got[m].astype(F32)).astype(BF16)
        out[blocks:, :] = ids[flip]


def send_body(away, own, order, ids, rec_packed, hyd_packed, *refs):
    terms, (runoff, ready, places) = refs[:-3], refs[-3:]
    places[0] = ids[0]
    for flip, term in enumerate(terms, 1):
        places[flip] = term[term.shape[0] - PACK_ROWS :, :]
    blocks = runoff.shape[0]
    tiles = ready.shape[0] // LANES
    total = own[...]
    for term in terms:
        total = total + term[:blocks, :].astype(F32)
    runoff[...] = total
    at = order[...]
    turned = lookup(total, at >> 7, at & (LANES - 1)).T
    for t in range(tiles):
        rows = pl.ds(t * LANES, LANES)
        col = away * tiles + t
        ready[rows, :] = (
            rec_packed[rows, :].astype(F32) + turned[:, col : col + 1] * hyd_packed[rows, :].astype(F32)
        ).astype(BF16)


def record_body(aways, runoff, records, hydro, order, kept, *ready):
    turned = runoff[...].T
    for t in range(runoff.shape[0]):
        rows = pl.ds(t * LANES, LANES)
        kept[rows, :] = (
            shift_time(records[rows, :].astype(F32)) + turned[:, t : t + 1] * hydro[rows, :].astype(F32)
        ).astype(BF16)
    for away, out in zip(aways, ready):
        hot = picked(order, away, out.shape[0] // LANES, kept.shape[0])
        out[...] = jnp.dot(hot, kept[...], preferred_element_type=F32).astype(BF16)


def hot_of(digits, tiles, basins, other):
    core = parity("sec")
    base = ((1 - core) if other else core) * basins
    slot = lax.broadcasted_iota(I32, (basins, LANES), 0) + base
    slot = slot.astype(F32)
    place = digits[:tiles] * 256.0 + digits[tiles : 2 * tiles]
    parts = [jnp.where(slot == place[t : t + 1, :], 1.0, 0.0).astype(BF16) for t in range(tiles)]
    return parts[0] if len(parts) == 1 else jnp.concatenate(parts, axis=1)


def summed(digits, blocks, basins, other):
    tiles = blocks[0].shape[0] // LANES
    total = None
    for digit, block in zip(digits, blocks):
        hot = hot_of(digit, tiles, basins, other)
        part = jnp.dot(hot, block[...], preferred_element_type=F32)
        total = part if total is None else total + part
    return total


def rest_body(
    near, order, kept, places, landed, moist, heat, out, moist_out, heat_out, theirs, mine, own, sems
):
    copies = fetch((kept, moist, heat), (out, moist_out, heat_out), sems)
    hot = picked(order, 0, own.shape[0] // LANES, kept.shape[0])
    own[...] = jnp.dot(hot, kept[...], preferred_element_type=F32).astype(BF16)
    digits = [places[away].astype(F32) for away in (0, near)]
    basins = mine.shape[0]
    theirs[...] = summed(digits, [own, landed], basins, True)
    mine[...] = summed(digits, [own, landed], basins, False)
    for copy in copies:
        copy.wait()


def early_body(aways, theirs_so_far, mine_so_far, places, *refs):
    blocks, (theirs, mine) = refs[:-2], refs[-2:]
    digits = [places[away].astype(F32) for away in aways]
    basins = mine.shape[0]
    theirs[...] = theirs_so_far[...] + summed(digits, blocks, basins, True)
    mine[...] = mine_so_far[...] + summed(digits, blocks, basins, False)


def late_body(aways, other, so_far, places, *refs):
    blocks, out = refs[:-1], refs[-1]
    digits = [places[away].astype(F32) for away in aways]
    out[...] = (so_far[...] + summed(digits, blocks, out.shape[0], other)).astype(out.dtype)


def final_body(mine, passed, out, held, sems):
    rows = mine.shape[0]
    parts = 2
    size = rows // parts
    copies = []
    for i in range(parts):
        at = pl.ds(i * size, size)
        held[at, :] = mine[at, :] + passed[at, :].astype(F32)
        copy = pltpu.make_async_copy(held.at[at, :], out.at[at, :], sems.at[i])
        copy.start()
        copies.append(copy)
    for copy in copies:
        copy.wait()


def per_device(
    moisture, heat, moist_cond, heat_cond, rain, surface_flux, cell_reach,
    records, unit_hydro, down_basin, basin_home, send_index, send_count,
):
    lons = lax.axis_size("lon")
    sections = lax.axis_size("sec")
    layers, lats, cols = moisture.shape
    reaches, steps = records.shape[1:]
    cap = send_index.shape[3]
    pairs = sections // 2
    basins = basin_home.shape[1] // sections
    blocks = reaches // LANES
    shape = jax.ShapeDtypeStruct
    dma = pltpu.SemaphoreType.DMA

    home = basin_home.reshape(-1, LANES)
    down = down_basin.reshape(-1, LANES)
    listed = send_index.reshape(sections, cap)
    moist_v, heat_v, sec_near, sec_far, lon_near, lon_far = call(
        edges_body,
        [
            shape(moisture.shape, F32),
            shape(heat.shape, F32),
            shape((2 * layers, cols), BF16),
            shape((2 * layers, cols), BF16),
            shape((lats, LANES), BF16),
            shape((lats, LANES), BF16),
        ],
        moisture, heat,
        ins=[HBM] * 2,
        scratch=[dma((2,))],
        moved=moisture.size * 8,
    )
    swap = lambda count: [(i, i ^ 1) for i in range(count)]
    between = lambda count: [(i, (i - 1 + 2 * (i % 2)) % count) for i in range(count)]
    got_sec_far = lax.ppermute(sec_far, "sec", between(sections))
    got_sec_near = lax.ppermute(sec_near, "sec", swap(sections))
    got_lon_far = lax.ppermute(lon_far, "lon", between(lons))
    got_lon_near = lax.ppermute(lon_near, "lon", swap(lons))

    land = [moist_cond, heat_cond, rain, surface_flux, cell_reach]
    tables = [send_count, home, down, listed]
    order, ids, *land = call(
        index_body,
        [shape((blocks, LANES), I32), shape((pairs, PACK_ROWS, LANES), BF16)]
        + [shape(x.shape, x.dtype) for x in land],
        *tables, *land,
        ins=[HBM] * 9,
        scratch=[pltpu.SMEM(send_count.shape, I32)]
        + [pltpu.VMEM(x.shape, I32) for x in tables[1:]]
        + [dma((9,))],
        moved=moisture.size * 8,
    )
    moist_new, heat_new, keep, give = call(
        land_body,
        [
            shape(moisture.shape, F32),
            shape(heat.shape, F32),
            shape((pairs, blocks, LANES), F32),
            shape((pairs, blocks, LANES), BF16),
        ],
        moist_v, heat_v, *land,
        got_sec_near, got_sec_far, got_lon_near, got_lon_far,
        moved=moisture.size * 24,
    )
    got = lax.ppermute(give, "sec", swap(sections))
    aways = []
    for k in range(1, pairs // 2 + 1):
        aways += [k] if 2 * k == pairs else [pairs - k, k]
    own_terms, *terms = call(
        terms_body,
        [shape((blocks, LANES), F32)] + [shape((blocks + PACK_ROWS, LANES), BF16)] * (pairs - 1),
        keep, got, ids,
        moved=reaches * 8,
    )
    forward = lambda block, away: lax.ppermute(
        block, "sec", [(i, i ^ (2 * away)) for i in range(sections)]
    )
    terms = [forward(term, flip) for flip, term in enumerate(terms, 1)]
    rec_packed, hyd_packed = call(
        lambda *refs: first_body(aways[0], *refs),
        [shape((cap, steps), BF16)] * 2,
        order, records[0], unit_hydro[0],
        mib=12,
        flops=4 * cap * reaches * steps,
        moved=reaches * steps * 4,
    )
    runoff, ready, places = call(
        lambda *refs: send_body(aways[0], *refs),
        [shape((blocks, LANES), F32), shape((cap, steps), BF16), shape(ids.shape, BF16)],
        own_terms, order, ids, rec_packed, hyd_packed, *terms,
        moved=cap * steps * 6,
    )
    arrived = {aways[0]: forward(ready, aways[0])}
    kept, *ready = call(
        lambda *refs: record_body(aways[1:], *refs),
        [shape((reaches, steps), BF16)] + [shape((cap, steps), BF16)] * (len(aways) - 1),
        runoff, records[0], unit_hydro[0], order,
        mib=16,
        flops=2 * cap * reaches * steps,
        moved=reaches * steps * 8,
    )
    for away, block in zip(aways[1:], ready):
        arrived[away] = forward(block, away)
    near, late = aways[0], aways[-1:]
    record_new, moist_out, heat_out, theirs, mine = call(
        lambda *refs: rest_body(near, *refs),
        [
            shape((reaches, steps), BF16),
            shape(moisture.shape, F32),
            shape(heat.shape, F32),
            shape((basins, steps), F32),
            shape((basins, steps), F32),
        ],
        order, kept, places, arrived[near], moist_new, heat_new,
        out_specs=[HBM] * 3 + [VMEM] * 2,
        scratch=[pltpu.VMEM((cap, steps), BF16), dma((3,))],
        mib=16,
        flops=2 * cap * reaches * steps,
        moved=reaches * steps * 4,
    )
    early = [a for a in aways[:-1] if a != near]
    theirs, mine = call(
        lambda *refs: early_body(early, *refs),
        [shape((basins, steps), F32), shape((basins, steps), F32)],
        theirs, mine, places, *[arrived[a] for a in early],
        mib=12,
        moved=basins * steps * 16,
    )
    (theirs,) = call(
        lambda *refs: late_body(late, True, *refs),
        [shape((basins, steps), BF16)],
        theirs, places, *[arrived[a] for a in late],
        moved=basins * steps * 8,
    )
    passed = lax.ppermute(theirs, "sec", swap(sections))
    (mine,) = call(
        lambda *refs: late_body(late, False, *refs),
        [shape((basins, steps), F32)],
        mine, places, *[arrived[a] for a in late],
        moved=basins * steps * 8,
    )
    (inflow,) = call(
        final_body,
        [shape((basins, steps), F32)],
        mine, passed,
        out_specs=[HBM],
        scratch=[pltpu.VMEM((basins, steps), F32), dma((2,))],
        moved=basins * steps * 10,
    )
    return (moist_out, heat_out, record_new[None], inflow[None])


def solution(mesh):
    placed = (
        P(None, "sec", "lon"),
        P(None, "sec", "lon"),
        P(None, "sec", "lon"),
        P(None, "sec", "lon"),
        P("sec", "lon"),
        P("sec", "lon"),
        P("sec", "lon"),
        P("lon", "sec", None),
        P("lon", "sec", None),
        P("lon", "sec"),
        P("lon", None),
        P("lon", "sec", None, None),
        P("lon", "sec", None),
    )
    return jax.shard_map(
        per_device,
        mesh=mesh,
        in_specs=placed,
        out_specs=(
            P(None, "sec", "lon"),
            P(None, "sec", "lon"),
            P("lon", "sec", None),
            P("lon", "sec", None),
        ),
        check_vma=False,
    )
```

```python
import jax
import jax.numpy as jnp
from jax import lax
from jax.experimental import pallas as pl
from jax.experimental.pallas import tpu as pltpu
from jax.sharding import PartitionSpec as P

LATERAL = 0.2
LANES = 128
PACK_ROWS = 16
F32 = jnp.float32
BF16 = jnp.bfloat16
I32 = jnp.int32
VMEM = pl.BlockSpec(memory_space=pltpu.VMEM)
HBM = pl.BlockSpec(memory_space=pltpu.HBM)


def call(body, outs, *args, ins=None, out_specs=None, scratch=(), mib=8, flops=0, moved=0):
    ins = list(ins) if ins else [VMEM] * len(args)
    args = [
        pltpu.with_memory_space_constraint(arg, pltpu.HBM) if spec is HBM else arg
        for arg, spec in zip(args, ins)
    ]
    return pl.pallas_call(
        body,
        out_shape=list(outs),
        in_specs=ins,
        out_specs=list(out_specs) if out_specs else [VMEM] * len(outs),
        scratch_shapes=list(scratch),
        compiler_params=pltpu.CompilerParams(vmem_limit_bytes=mib * 1024 * 1024),
        cost_estimate=pl.CostEstimate(flops=flops, bytes_accessed=moved, transcendentals=0),
    )(*args)


def fetch(sources, targets, sems):
    copies = [
        pltpu.make_async_copy(src, dst, sems.at[i])
        for i, (src, dst) in enumerate(zip(sources, targets))
    ]
    for copy in copies:
        copy.start()
    return copies


def parity(axis):
    return lax.rem(lax.axis_index(axis), 2)


def edges_body(*refs):
    count = 2
    targets = refs[count : 2 * count]
    moist, heat = targets[:2]
    sec_near, sec_far, lon_near, lon_far, sems = refs[2 * count :]
    copies = fetch(refs[:count], targets, sems)
    layers, rows, cols = moist.shape
    lane = lax.broadcasted_iota(I32, (rows, LANES), 1)
    west = jnp.zeros((rows, LANES), F32)
    east = jnp.zeros((rows, LANES), F32)
    sec_even = parity("sec") == 0
    for f, ref in enumerate((moist, heat)):
        copies[f].wait()
        north = ref[:, 0, :]
        south = ref[:, rows - 1, :]
        sec_near[f * layers : (f + 1) * layers, :] = jnp.where(sec_even, south, north).astype(BF16)
        sec_far[f * layers : (f + 1) * layers, :] = jnp.where(sec_even, north, south).astype(BF16)
        for layer in range(layers):
            k = f * layers + layer
            west = jnp.where(lane == k, ref[layer, :, 0:1], west)
            east = jnp.where(lane == k, ref[layer, :, cols - 1 : cols], east)
    lon_even = parity("lon") == 0
    lon_near[...] = jnp.where(lon_even, east, west).astype(BF16)
    lon_far[...] = jnp.where(lon_even, west, east).astype(BF16)
    for copy in copies[2:]:
        copy.wait()


def lookup(table, hi, lo):
    out = jnp.zeros(hi.shape, table.dtype)
    for row in range(table.shape[0]):
        line = jnp.broadcast_to(table[row : row + 1, :], hi.shape)
        got = jnp.take_along_axis(line, lo, axis=1)
        out = jnp.where(hi == row, got, out)
    return out


def index_body(*refs):
    count_in, home_in, down_in, listed_in = refs[:4]
    order, ids = refs[9:11]
    count, home, down, listed, sems = refs[16:]
    copies = fetch(refs[:9], (count, home, down, listed, *refs[11:16]), sems)
    pairs, width = listed.shape[0] // 2, listed.shape[1]
    tiles = width // LANES
    chip = lax.axis_index("sec") // 2
    chip_basins = home.shape[0] * LANES // pairs
    for copy in copies[:4]:
        copy.wait()
    slot = lookup(home[...], down[...] >> 7, down[...] & (LANES - 1))
    pos = lax.broadcasted_iota(I32, (1, width), 1)
    for m in range(pairs):
        c = count[0, 0, 2 * m]
        second = pltpu.roll(listed[2 * m + 1 : 2 * m + 2, :], lax.rem(c, width), 1)
        line = jnp.where(pos < c, listed[2 * m : 2 * m + 1, :], second)
        away = m ^ chip
        for t in range(tiles):
            order[pl.ds(away * tiles + t, 1), :] = line[:, t * LANES : (t + 1) * LANES]
    at = order[...]
    place = lookup(slot, at >> 7, at & (LANES - 1))
    pad = jnp.zeros((PACK_ROWS - 2 * tiles, LANES), F32)
    for away in range(pairs):
        m = away ^ chip
        mine = place[away * tiles : (away + 1) * tiles, :] - m * chip_basins
        ids[away] = jnp.concatenate(
            [(mine >> 8).astype(F32), (mine & 255).astype(F32), pad], axis=0
        ).astype(BF16)
    for copy in copies[4:]:
        copy.wait()


def shift_time(x):
    steps = x.shape[1]
    lane = lax.broadcasted_iota(I32, x.shape, 1)
    return jnp.where(lane == steps - 1, 0.0, pltpu.roll(x, steps - 1, 1))


def picked(order, away, tiles, reaches):
    turned = order[...].astype(F32).T
    lane = lax.broadcasted_iota(I32, (LANES, reaches), 1).astype(F32)
    parts = [
        jnp.where(lane == turned[:, t : t + 1], 1.0, 0.0).astype(BF16)
        for t in range(away * tiles, (away + 1) * tiles)
    ]
    return parts[0] if len(parts) == 1 else jnp.concatenate(parts, axis=0)


def first_body(away, order, records, hydro, rec_packed, hyd_packed):
    hot = picked(order, away, rec_packed.shape[0] // LANES, records.shape[0])
    rec = jnp.dot(hot, records[...], preferred_element_type=F32)
    rec_packed[...] = shift_time(rec).astype(BF16)
    hyd_packed[...] = jnp.dot(hot, hydro[...], preferred_element_type=F32).astype(BF16)


def land_body(
    moist, heat, moist_k, heat_k, rain, flux, cell, sec_near, sec_far, lon_near, lon_far,
    moist_out, heat_out, keep, give,
):
    layers, rows, cols = moist.shape
    row = lax.broadcasted_iota(I32, (rows, cols), 0)
    col = lax.broadcasted_iota(I32, (rows, cols), 1)
    sec_even = parity("sec") == 0
    lon_even = parity("lon") == 0
    outer = lambda axis: (lax.axis_index(axis) == 0) | (
        lax.axis_index(axis) == lax.axis_size(axis) - 1
    )
    sec_beyond = jnp.where(outer("sec"), 0.0, sec_far[...].astype(F32))
    lon_beyond = jnp.where(outer("lon"), 0.0, lon_far[...].astype(F32))
    south_all = jnp.where(sec_even, sec_near[...].astype(F32), sec_beyond)
    north_all = jnp.where(sec_even, sec_beyond, sec_near[...].astype(F32))
    east_all = jnp.where(lon_even, lon_near[...].astype(F32), lon_beyond)
    west_all = jnp.where(lon_even, lon_beyond, lon_near[...].astype(F32))
    for f, (x_ref, k_ref, top, out) in enumerate(
        ((moist, moist_k, rain, moist_out), (heat, heat_k, flux, heat_out))
    ):
        ratio = jnp.zeros((rows, cols), F32)
        value = jnp.zeros((rows, cols), F32)
        below = jnp.zeros((rows, cols), F32)
        ratios, values = [], []
        for layer in range(layers):
            k = f * layers + layer
            x = x_ref[layer]
            up = jnp.where(row == 0, north_all[k : k + 1, :], pltpu.roll(x, 1, 0))
            dn = jnp.where(row == rows - 1, south_all[k : k + 1, :], pltpu.roll(x, rows - 1, 0))
            lf = jnp.where(col == 0, west_all[:, k : k + 1], pltpu.roll(x, 1, 1))
            rt = jnp.where(col == cols - 1, east_all[:, k : k + 1], pltpu.roll(x, cols - 1, 1))
            rhs = x + LATERAL * (up + dn + lf + rt - 4.0 * x)
            if layer == 0:
                rhs = rhs + top[...]
            if layer < layers - 1:
                above = 0.5 * (k_ref[layer] + k_ref[layer + 1])
            else:
                above = jnp.zeros((rows, cols), F32)
            inv = 1.0 / (1.0 + below + above + below * ratio)
            ratio = -above * inv
            value = (rhs + below * value) * inv
            ratios.append(ratio)
            values.append(value)
            below = above
        x = values[-1]
        out[layers - 1] = x
        for layer in range(layers - 2, -1, -1):
            x = values[layer] - ratios[layer] * x
            out[layer] = x
    s = moist_out[0] - 1.0
    soft = jnp.maximum(s, 0.0) + jnp.log1p(jnp.exp(-jnp.abs(s)))
    gate = 1.0 / (1.0 + jnp.exp(-heat_out[0]))
    runoff = soft * gate + 0.5 * moist_k[layers - 1] * moist_out[layers - 1]
    cells = cell[...]
    hi = cells >> 7
    lo = cells & (LANES - 1)
    pairs, blocks = keep.shape[:2]
    his = 2 * pairs * blocks
    hi_iota = lax.broadcasted_iota(I32, (his, cols), 0)
    lo_iota = lax.broadcasted_iota(I32, (LANES, cols), 0)
    acc = jnp.zeros((his, LANES), F32)
    for i in range(rows):
        a = jnp.where(hi_iota == hi[i : i + 1, :], runoff[i : i + 1, :], 0.0).astype(BF16)
        b = jnp.where(lo_iota == lo[i : i + 1, :], 1.0, 0.0).astype(BF16)
        acc = acc + lax.dot_general(a, b, (((1,), (1,)), ((), ())), preferred_element_type=F32)
    both = acc.reshape(pairs, 2, blocks, LANES)
    keep[...] = jnp.where(sec_even, both[:, 0], both[:, 1])
    give[...] = jnp.where(sec_even, both[:, 1], both[:, 0]).astype(BF16)


def turn(count):
    return [1, *range(count, 1, -1)]


def terms_body(keep, got, ids, own, *outs):
    pairs, blocks = keep.shape[:2]
    chip = lax.axis_index("sec") // 2
    own[...] = keep[chip] + got[chip].astype(F32)
    for flip, out in zip(turn(len(outs)), outs):
        m = chip ^ flip
        out[:blocks, :] = (keep[m] + got[m].astype(F32)).astype(BF16)
        out[blocks:, :] = ids[flip]


def send_body(away, own, order, ids, rec_packed, hyd_packed, *refs):
    terms, (runoff, ready, places) = refs[:-3], refs[-3:]
    places[0] = ids[0]
    for flip, term in zip(turn(len(terms)), terms):
        places[flip] = term[term.shape[0] - PACK_ROWS :, :]
    blocks = runoff.shape[0]
    tiles = ready.shape[0] // LANES
    total = own[...]
    for term in terms:
        total = total + term[:blocks, :].astype(F32)
    runoff[...] = total
    at = order[...]
    turned = lookup(total, at >> 7, at & (LANES - 1)).T
    for t in range(tiles):
        rows = pl.ds(t * LANES, LANES)
        col = away * tiles + t
        ready[rows, :] = (
            rec_packed[rows, :].astype(F32) + turned[:, col : col + 1] * hyd_packed[rows, :].astype(F32)
        ).astype(BF16)


def record_body(aways, runoff, records, hydro, order, kept, *ready):
    turned = runoff[...].T
    for t in range(runoff.shape[0]):
        rows = pl.ds(t * LANES, LANES)
        kept[rows, :] = (
            shift_time(records[rows, :].astype(F32)) + turned[:, t : t + 1] * hydro[rows, :].astype(F32)
        ).astype(BF16)
    for away, out in zip(aways, ready):
        hot = picked(order, away, out.shape[0] // LANES, kept.shape[0])
        out[...] = jnp.dot(hot, kept[...], preferred_element_type=F32).astype(BF16)


def hot_of(digits, tiles, basins, other):
    core = parity("sec")
    base = ((1 - core) if other else core) * basins
    slot = lax.broadcasted_iota(I32, (basins, LANES), 0) + base
    slot = slot.astype(F32)
    place = digits[:tiles] * 256.0 + digits[tiles : 2 * tiles]
    parts = [jnp.where(slot == place[t : t + 1, :], 1.0, 0.0).astype(BF16) for t in range(tiles)]
    return parts[0] if len(parts) == 1 else jnp.concatenate(parts, axis=1)


def summed(digits, blocks, basins, other):
    tiles = blocks[0].shape[0] // LANES
    total = None
    for digit, block in zip(digits, blocks):
        hot = hot_of(digit, tiles, basins, other)
        part = jnp.dot(hot, block[...], preferred_element_type=F32)
        total = part if total is None else total + part
    return total


def rest_body(
    near, order, kept, places, landed, moist, heat, out, moist_out, heat_out, theirs, mine, own, sems
):
    copies = fetch((kept, moist, heat), (out, moist_out, heat_out), sems)
    hot = picked(order, 0, own.shape[0] // LANES, kept.shape[0])
    own[...] = jnp.dot(hot, kept[...], preferred_element_type=F32).astype(BF16)
    digits = [places[away].astype(F32) for away in (0, near)]
    basins = mine.shape[0]
    theirs[...] = summed(digits, [own, landed], basins, True)
    mine[...] = summed(digits, [own, landed], basins, False)
    for copy in copies:
        copy.wait()


def early_body(aways, theirs_so_far, mine_so_far, places, *refs):
    blocks, (theirs, mine) = refs[:-2], refs[-2:]
    digits = [places[away].astype(F32) for away in aways]
    basins = mine.shape[0]
    theirs[...] = theirs_so_far[...] + summed(digits, blocks, basins, True)
    mine[...] = mine_so_far[...] + summed(digits, blocks, basins, False)


def late_body(aways, other, so_far, places, *refs):
    blocks, out = refs[:-1], refs[-1]
    digits = [places[away].astype(F32) for away in aways]
    out[...] = (so_far[...] + summed(digits, blocks, out.shape[0], other)).astype(out.dtype)


def final_body(mine, passed, out, held, sems):
    rows = mine.shape[0]
    parts = 2
    size = rows // parts
    copies = []
    for i in range(parts):
        at = pl.ds(i * size, size)
        held[at, :] = mine[at, :] + passed[at, :].astype(F32)
        copy = pltpu.make_async_copy(held.at[at, :], out.at[at, :], sems.at[i])
        copy.start()
        copies.append(copy)
    for copy in copies:
        copy.wait()


def per_device(
    moisture, heat, moist_cond, heat_cond, rain, surface_flux, cell_reach,
    records, unit_hydro, down_basin, basin_home, send_index, send_count,
):
    lons = lax.axis_size("lon")
    sections = lax.axis_size("sec")
    layers, lats, cols = moisture.shape
    reaches, steps = records.shape[1:]
    cap = send_index.shape[3]
    pairs = sections // 2
    basins = basin_home.shape[1] // sections
    blocks = reaches // LANES
    shape = jax.ShapeDtypeStruct
    dma = pltpu.SemaphoreType.DMA

    home = basin_home.reshape(-1, LANES)
    down = down_basin.reshape(-1, LANES)
    listed = send_index.reshape(sections, cap)
    moist_v, heat_v, sec_near, sec_far, lon_near, lon_far = call(
        edges_body,
        [
            shape(moisture.shape, F32),
            shape(heat.shape, F32),
            shape((2 * layers, cols), BF16),
            shape((2 * layers, cols), BF16),
            shape((lats, LANES), BF16),
            shape((lats, LANES), BF16),
        ],
        moisture, heat,
        ins=[HBM] * 2,
        scratch=[dma((2,))],
        moved=moisture.size * 8,
    )
    swap = lambda count: [(i, i ^ 1) for i in range(count)]
    between = lambda count: [(i, (i - 1 + 2 * (i % 2)) % count) for i in range(count)]
    got_sec_far = lax.ppermute(sec_far, "sec", between(sections))
    got_sec_near = lax.ppermute(sec_near, "sec", swap(sections))
    got_lon_far = lax.ppermute(lon_far, "lon", between(lons))
    got_lon_near = lax.ppermute(lon_near, "lon", swap(lons))

    land = [moist_cond, heat_cond, rain, surface_flux, cell_reach]
    tables = [send_count, home, down, listed]
    order, ids, *land = call(
        index_body,
        [shape((blocks, LANES), I32), shape((pairs, PACK_ROWS, LANES), BF16)]
        + [shape(x.shape, x.dtype) for x in land],
        *tables, *land,
        ins=[HBM] * 9,
        scratch=[pltpu.SMEM(send_count.shape, I32)]
        + [pltpu.VMEM(x.shape, I32) for x in tables[1:]]
        + [dma((9,))],
        moved=moisture.size * 8,
    )
    moist_new, heat_new, keep, give = call(
        land_body,
        [
            shape(moisture.shape, F32),
            shape(heat.shape, F32),
            shape((pairs, blocks, LANES), F32),
            shape((pairs, blocks, LANES), BF16),
        ],
        moist_v, heat_v, *land,
        got_sec_near, got_sec_far, got_lon_near, got_lon_far,
        moved=moisture.size * 24,
    )
    got = lax.ppermute(give, "sec", swap(sections))
    aways = []
    for k in range(1, pairs // 2 + 1):
        aways += [k] if 2 * k == pairs else [pairs - k, k]
    own_terms, *terms = call(
        terms_body,
        [shape((blocks, LANES), F32)] + [shape((blocks + PACK_ROWS, LANES), BF16)] * (pairs - 1),
        keep, got, ids,
        moved=reaches * 8,
    )
    forward = lambda block, away: lax.ppermute(
        block, "sec", [(i, i ^ (2 * away)) for i in range(sections)]
    )
    terms = [forward(term, flip) for flip, term in zip(turn(len(terms)), terms)]
    rec_packed, hyd_packed = call(
        lambda *refs: first_body(aways[0], *refs),
        [shape((cap, steps), BF16)] * 2,
        order, records[0], unit_hydro[0],
        mib=12,
        flops=4 * cap * reaches * steps,
        moved=reaches * steps * 4,
    )
    runoff, ready, places = call(
        lambda *refs: send_body(aways[0], *refs),
        [shape((blocks, LANES), F32), shape((cap, steps), BF16), shape(ids.shape, BF16)],
        own_terms, order, ids, rec_packed, hyd_packed, *terms,
        moved=cap * steps * 6,
    )
    arrived = {aways[0]: forward(ready, aways[0])}
    kept, *ready = call(
        lambda *refs: record_body(aways[1:], *refs),
        [shape((reaches, steps), BF16)] + [shape((cap, steps), BF16)] * (len(aways) - 1),
        runoff, records[0], unit_hydro[0], order,
        mib=16,
        flops=2 * cap * reaches * steps,
        moved=reaches * steps * 8,
    )
    for away, block in zip(aways[1:], ready):
        arrived[away] = forward(block, away)
    near, late = aways[0], aways[-1:]
    record_new, moist_out, heat_out, theirs, mine = call(
        lambda *refs: rest_body(near, *refs),
        [
            shape((reaches, steps), BF16),
            shape(moisture.shape, F32),
            shape(heat.shape, F32),
            shape((basins, steps), F32),
            shape((basins, steps), F32),
        ],
        order, kept, places, arrived[near], moist_new, heat_new,
        out_specs=[HBM] * 3 + [VMEM] * 2,
        scratch=[pltpu.VMEM((cap, steps), BF16), dma((3,))],
        mib=16,
        flops=2 * cap * reaches * steps,
        moved=reaches * steps * 4,
    )
    early = [a for a in aways[:-1] if a != near]
    theirs, mine = call(
        lambda *refs: early_body(early, *refs),
        [shape((basins, steps), F32), shape((basins, steps), F32)],
        theirs, mine, places, *[arrived[a] for a in early],
        mib=12,
        moved=basins * steps * 16,
    )
    (theirs,) = call(
        lambda *refs: late_body(late, True, *refs),
        [shape((basins, steps), BF16)],
        theirs, places, *[arrived[a] for a in late],
        moved=basins * steps * 8,
    )
    passed = lax.ppermute(theirs, "sec", swap(sections))
    (mine,) = call(
        lambda *refs: late_body(late, False, *refs),
        [shape((basins, steps), F32)],
        mine, places, *[arrived[a] for a in late],
        moved=basins * steps * 8,
    )
    (inflow,) = call(
        final_body,
        [shape((basins, steps), F32)],
        mine, passed,
        out_specs=[HBM],
        scratch=[pltpu.VMEM((basins, steps), F32), dma((2,))],
        moved=basins * steps * 10,
    )
    return (moist_out, heat_out, record_new[None], inflow[None])


def solution(mesh):
    placed = (
        P(None, "sec", "lon"),
        P(None, "sec", "lon"),
        P(None, "sec", "lon"),
        P(None, "sec", "lon"),
        P("sec", "lon"),
        P("sec", "lon"),
        P("sec", "lon"),
        P("lon", "sec", None),
        P("lon", "sec", None),
        P("lon", "sec"),
        P("lon", None),
        P("lon", "sec", None, None),
        P("lon", "sec", None),
    )
    return jax.shard_map(
        per_device,
        mesh=mesh,
        in_specs=placed,
        out_specs=(
            P(None, "sec", "lon"),
            P(None, "sec", "lon"),
            P("lon", "sec", None),
            P("lon", "sec", None),
        ),
        check_vma=False,
    )
```
